32 devices in a mesh: region: 16 (over z, y, x), rays: 2 (over core).
Axes of the slice: x: 2, y: 2, z: 4, core: 2. Of those that a mesh axis runs over, the one named last changes fastest.
Arguments:
- ray_codes: bfloat16 [2, 1024, 128], P(None, 'rays'), may hold values from -6 to 6
- target: bfloat16 [1024, 384], P('rays'), may hold values from -0.19921875 to 1
- direction: int32 [1024], P('rays'), may hold values from 0 to 1
- entries: int32 [16, 1024], P('region', 'rays'), may hold values from 0 to 4
- exits: int32 [16, 1024], P('region', 'rays'), may hold values from 4 to 8
- depth_bins: int32 [16, 8, 1024], P('region', None, 'rays'), may hold values from 0 to 63, as said below
- in_layer: float32 [3, 16, 128, 256], P(None, 'region', 'rays'), as said below
- mid_layer: float32 [3, 16, 256, 256], P(None, 'region', 'rays'), as said below
- feat_layer: float32 [3, 16, 256, 384], P(None, 'region', 'rays'), as said below
- vectors: float32 [3, 16, 1152], P(None, 'region', 'rays'), as said below
Outputs:
- new_in_layer: float32 [3, 16, 128, 256], P(None, 'region', 'rays')
- new_mid_layer: float32 [3, 16, 256, 256], P(None, 'region', 'rays')
- new_feat_layer: float32 [3, 16, 256, 384], P(None, 'region', 'rays')
- new_vectors: float32 [3, 16, 1152], P(None, 'region', 'rays')
- depth_grad: float32 [16, 1024], P('region', 'rays')
The draws below stay inside these ranges and needn't reach their ends.
Inputs may be any that keep to these rules, and one draw needn't show every extreme that they name: `direction`: 0: the ray meets the regions in increasing index order; 1: in decreasing order. A ray's samples inside a region are the slots j with entries <= j < exits. `depth_bins`: slot j lies in bins j * (8) to (j + 1) * 8 - 1. `in_layer`: the second moments (index 2 of the first dimension) are positive. `mid_layer`: the second moments (index 2 of the first dimension) are positive. `feat_layer`: the second moments (index 2 of the first dimension) are positive. `vectors`: the second moments (index 2 of the first dimension) are positive.
All inputs are finite; a program needn't handle non-finite values.
Results may differ from the reference program's by a relative error of at most 0.0025.
The reference program's roundings to bfloat16 on the way (of `encoded`, `hidden_one`, `hidden_two`, `feature_grad`, `density_grad`, `colour_grad`, `second_grad` and `first_grad`) count: a program that leaves them out, or rounds other values in their place, can miss the bound.
Values may be sent and summed in bfloat16 or wider, within the bound.
No kernel may reach another device: no remote copies, remote signals or barrier semaphores. Data moves between devices by JAX's collectives and lax.ppermute only.
A program may use at most 64 MiB of HBM per device.

```python
import math
import jax
import jax.numpy as jnp
from jax import lax

IN = 128
HID = 256
FEAT = 384
SAMPLES = 8
BINS = 64
RAYS = 1024
REGIONS = 16
VEC = 1152


def moments(key, full_shape, spread, state_scale):
    master_key = jax.random.fold_in(key, 101)
    first_key = jax.random.fold_in(key, 202)
    second_key = jax.random.fold_in(key, 303)
    master = jax.random.normal(master_key, full_shape, jnp.float32) * spread
    first_moment = jax.random.normal(first_key, full_shape, jnp.float32) * (0.3 * state_scale)
    second = jnp.exp(jax.random.uniform(second_key, full_shape, jnp.float32, math.log(0.3), 0.0)) * (state_scale * state_scale)
    return jnp.stack([master, first_moment, second])


def draw_in_layer(key, part):
    return moments(key, (REGIONS, IN, HID), IN ** (-0.5), 0.2)


def draw_mid_layer(key, part):
    return moments(key, (REGIONS, HID, HID), HID ** (-0.5), 0.15)


def draw_feat_layer(key, part):
    return moments(key, (REGIONS, HID, FEAT), 4.0 * HID ** (-0.5), 0.15)


def draw_vectors(key, part):
    spread = jnp.concatenate([jnp.full((2 * HID,), 0.5, jnp.float32), jnp.full((HID,), HID ** (-0.5), jnp.float32), jnp.full((FEAT,), 1.0, jnp.float32)])
    state_scale = jnp.concatenate([jnp.full((HID,), 0.15, jnp.float32), jnp.full((HID,), 0.2, jnp.float32), jnp.full((HID,), 1.0, jnp.float32), jnp.full((FEAT,), 0.15, jnp.float32)])
    return moments(key, (REGIONS, VEC), spread[None, :], state_scale[None, :])


def draw_depth_bins(key, part):
    stride = BINS // SAMPLES
    jitter = jax.random.randint(key, (REGIONS, SAMPLES, RAYS), 0, stride, jnp.int32)
    base = lax.broadcasted_iota(jnp.int32, (REGIONS, SAMPLES, RAYS), 1) * stride
    return (base + jitter).astype(jnp.int32)


def set_ends(values, key, smallest, high):
    extent = values.shape
    spot = [jax.random.randint(jax.random.fold_in(key, axis), (), 0, extent[axis]) for axis in range(len(extent))]
    values = values.at[tuple(spot)].set(smallest)
    longest = extent.index(max(extent))
    spot[longest] = (spot[longest] + 1) % extent[longest]
    return values.at[tuple(spot)].set(high)


def block_scale(key, dims, cuts, smallest, high):
    factor_of, own = 1.0, jax.random.fold_in(key, 6)
    for dim, parts in cuts:
        steps = jnp.exp(jax.random.uniform(jax.random.fold_in(own, dim), (parts,), jnp.float32, smallest / len(cuts), high / len(cuts)))
        factor_of = factor_of * jnp.repeat(steps, dims[dim] // parts).reshape([-1 if axis == dim else 1 for axis in range(len(dims))])
    return factor_of


def gaussian(stream_key, dims, width, limit, cuts=(), held_as=jnp.bfloat16):
    values = width * jax.random.normal(stream_key, dims, jnp.float32)
    if cuts:
        values = values * block_scale(stream_key, dims, cuts, -0.22, 0.18)
    return jnp.clip(values, -limit, limit).astype(held_as)


def setup_inputs(seed: int = 0) -> dict:
    keys = jax.random.split(jax.random.key(seed), 11)
    return {
        "ray_codes": gaussian(keys[0], (2, RAYS, IN), 1.0, 6.0, ((1, 2),)),
        "target": jnp.clip(-0.19921875 + 1.1992188 * jax.random.uniform(keys[1], (RAYS, FEAT), jnp.float32) ** block_scale(keys[1], (RAYS, FEAT), ((0, 2),), -0.2, 0.2), -0.19921875, 1.0).astype(jnp.bfloat16),
        "direction": set_ends(jax.random.randint(keys[2], (RAYS,), 0, 2), jax.random.fold_in(keys[2], 1), 0, 1).astype(jnp.int32),
        "entries": set_ends(jax.random.randint(keys[3], (REGIONS, RAYS), 0, SAMPLES // 2 + 1), jax.random.fold_in(keys[3], 1), 0, (SAMPLES // 2 + 1) - 1).astype(jnp.int32),
        "exits": set_ends(jax.random.randint(keys[4], (REGIONS, RAYS), SAMPLES // 2, SAMPLES + 1), jax.random.fold_in(keys[4], 1), SAMPLES // 2, SAMPLES).astype(jnp.int32),
        "depth_bins": draw_depth_bins(jax.random.fold_in(keys[10], 71), 0),
        "in_layer": draw_in_layer(jax.random.fold_in(keys[10], 71), 0),
        "mid_layer": draw_mid_layer(jax.random.fold_in(keys[10], 71), 0),
        "feat_layer": draw_feat_layer(jax.random.fold_in(keys[10], 71), 0),
        "vectors": draw_vectors(jax.random.fold_in(keys[10], 71), 0),
    }


depth_scale = 4.0
beta_one = 0.9
beta_two = 0.999
learn_rate = 0.001
epsilon = 1e-08
first_fix = 1.0 - 0.9 ** 10
second_fix = 1.0 - 0.999 ** 10

def forward(ray_codes, depth_bins, entry_row, exit_row, weights, unit_length):
    in_weight, mid_weight, feat_weight, vec_weight = weights
    hidden_width = in_weight.shape[1]
    bias_one = vec_weight[:hidden_width].astype(jnp.float32)
    bias_two = vec_weight[hidden_width:2 * hidden_width].astype(jnp.float32)
    density_weight = vec_weight[2 * hidden_width:3 * hidden_width]
    bias_feat = vec_weight[3 * hidden_width:].astype(jnp.float32)
    samples, ray_count = depth_bins.shape
    bin_float = depth_bins.astype(jnp.float32)
    following = jnp.concatenate([bin_float[1:], jnp.full((1, ray_count), float(BINS), jnp.float32)], 0)
    spacing = (following - bin_float) * unit_length
    position = (bin_float + 0.5) / BINS
    sample_slot = lax.broadcasted_iota(jnp.int32, (samples, ray_count), 0)
    inside = ((sample_slot >= entry_row[None, :]) & (sample_slot < exit_row[None, :])).astype(jnp.float32)
    codes_float = ray_codes.astype(jnp.float32)
    encoded = (codes_float[0][None] + position[:, :, None] * codes_float[1][None]).astype(jnp.bfloat16)
    encoded = encoded.reshape(samples * ray_count, codes_float.shape[2])
    hidden_one = jnp.maximum(jnp.dot(encoded, in_weight, preferred_element_type=jnp.float32) + bias_one, 0.0).astype(jnp.bfloat16)
    hidden_two = jnp.maximum(jnp.dot(hidden_one, mid_weight, preferred_element_type=jnp.float32) + bias_two, 0.0).astype(jnp.bfloat16)
    density_raw = jnp.dot(hidden_two, density_weight, preferred_element_type=jnp.float32).reshape(samples, ray_count)
    colour = jax.nn.sigmoid(jnp.dot(hidden_two, feat_weight, preferred_element_type=jnp.float32) + bias_feat)
    colour = colour.reshape(samples, ray_count, feat_weight.shape[1])
    optical = jax.nn.softplus(density_raw) * spacing * inside
    optical_before = jnp.cumsum(optical, 0) - optical
    local_weight = jnp.exp(-optical_before) * -jnp.expm1(-optical)
    return (encoded, hidden_one, hidden_two, density_raw, colour, optical, optical_before, local_weight, spacing, inside)

def backward(found, weights, entry_trans, after_sum, feature_grad):
    encoded, hidden_one, hidden_two, density_raw, colour, optical, optical_before, local_weight, spacing, inside = found
    in_weight, mid_weight, feat_weight, vec_weight = weights
    hidden_width = in_weight.shape[1]
    density_weight = vec_weight[2 * hidden_width:3 * hidden_width]
    grad_float = feature_grad.astype(jnp.float32)
    sample_grad = lax.optimization_barrier(jnp.sum(colour * grad_float[None], -1))
    weighted = local_weight * sample_grad
    later_local = jnp.cumsum(weighted[::-1], 0)[::-1] - weighted
    optical_grad = entry_trans[None] * (jnp.exp(-(optical_before + optical)) * sample_grad - later_local) - after_sum[None]
    density_grad = (optical_grad * spacing * inside * jax.nn.sigmoid(density_raw)).astype(jnp.bfloat16).reshape(-1)
    colour_grad = ((entry_trans[None] * local_weight)[:, :, None] * grad_float[None] * colour * (1.0 - colour)).astype(jnp.bfloat16)
    colour_grad = colour_grad.reshape(-1, colour.shape[2])
    hidden_grad = jnp.dot(colour_grad, feat_weight.T, preferred_element_type=jnp.float32)
    hidden_grad = hidden_grad + density_grad.astype(jnp.float32)[:, None] * density_weight.astype(jnp.float32)[None, :]
    second_grad = (hidden_grad * (hidden_two > 0)).astype(jnp.bfloat16)
    first_grad = (jnp.dot(second_grad, mid_weight.T, preferred_element_type=jnp.float32) * (hidden_one > 0)).astype(jnp.bfloat16)
    in_grad = jnp.dot(encoded.T, first_grad, preferred_element_type=jnp.float32)
    mid_grad = jnp.dot(hidden_one.T, second_grad, preferred_element_type=jnp.float32)
    feat_grad = jnp.dot(hidden_two.T, colour_grad, preferred_element_type=jnp.float32)
    density_sum = jnp.dot(density_grad, hidden_two, preferred_element_type=jnp.float32)
    vec_grad = jnp.concatenate([lax.optimization_barrier(jnp.sum(first_grad, 0, dtype=jnp.float32)), lax.optimization_barrier(jnp.sum(second_grad, 0, dtype=jnp.float32)), density_sum, lax.optimization_barrier(jnp.sum(colour_grad, 0, dtype=jnp.float32))])
    return (in_grad, mid_grad, feat_grad, vec_grad)

def adam_update(stacked, gradient):
    first_moment = beta_one * stacked[1] + (1.0 - beta_one) * gradient
    second = beta_two * stacked[2] + (1.0 - beta_two) * gradient * gradient
    update_step = first_moment / first_fix / (jnp.sqrt(second / second_fix) + epsilon)
    return jnp.stack([stacked[0] - learn_rate * update_step, first_moment, second])

def exclusive_lower(values):
    running = jnp.cumsum(values, 0)
    return jnp.concatenate([jnp.zeros_like(values[:1]), running[:-1]], 0)

def exclusive_upper(values):
    running = jnp.cumsum(values[::-1], 0)[::-1]
    return jnp.concatenate([running[1:], jnp.zeros_like(values[:1])], 0)

def reference(ray_codes, target, direction, entries, exits, depth_bins, in_layer, mid_layer, feat_layer, vectors):
    unit_length = depth_scale / (REGIONS * BINS)
    weight_sets = (in_layer[0].astype(jnp.bfloat16), mid_layer[0].astype(jnp.bfloat16), feat_layer[0].astype(jnp.bfloat16), vectors[0].astype(jnp.bfloat16))

    def first_pass(region_inputs):
        found = forward(ray_codes, region_inputs[0], region_inputs[1], region_inputs[2], region_inputs[3:], unit_length)
        colour, optical, local_weight = (found[4], found[5], found[7])
        return (lax.optimization_barrier(jnp.sum(optical, 0)), lax.optimization_barrier(jnp.sum(local_weight[:, :, None] * colour, 0)))
    depth, local_partial = lax.map(first_pass, (depth_bins, entries, exits) + weight_sets)
    onward = (direction == 0)[None, :]
    entry_trans = jnp.exp(-jnp.where(onward, exclusive_lower(depth), exclusive_upper(depth)))
    rendered = lax.optimization_barrier(jnp.sum(entry_trans[:, :, None] * local_partial, 0))
    feature_grad = (rendered - target.astype(jnp.float32)).astype(jnp.bfloat16)
    region_grad = entry_trans * lax.optimization_barrier(jnp.sum(feature_grad.astype(jnp.float32)[None] * local_partial, -1))
    after_sum = jnp.where(onward, exclusive_upper(region_grad), exclusive_lower(region_grad))

    def second_pass(region_inputs):
        weights = region_inputs[3:7]
        found = forward(ray_codes, region_inputs[0], region_inputs[1], region_inputs[2], weights, unit_length)
        return backward(found, weights, region_inputs[7], region_inputs[8], feature_grad)
    in_grad, mid_grad, feat_grad, vec_grad = lax.map(second_pass, (depth_bins, entries, exits) + weight_sets + (entry_trans, after_sum))
    return (adam_update(in_layer, in_grad), adam_update(mid_layer, mid_grad), adam_update(feat_layer, feat_grad), adam_update(vectors, vec_grad), -after_sum)
```

```python
import functools

import jax
import jax.numpy as jnp
from jax import lax
from jax.experimental import pallas as pl
from jax.experimental.pallas import tpu as pltpu
from jax.sharding import PartitionSpec as P

BINS = 64
LANES = 128

depth_scale = 4.0
beta_one = 0.9
beta_two = 0.999
learn_rate = 0.001
epsilon = 1e-08
first_fix = 1.0 - 0.9**10
second_fix = 1.0 - 0.999**10

f32 = jnp.float32
bf16 = jnp.bfloat16
LIMIT = 48 * 1024 * 1024


def whole():
    return pl.BlockSpec(memory_space=pltpu.VMEM)


def call(body, out_shape, n_in, scratch=(), limit=LIMIT, flops=1000000, moved=1000000):
    many = isinstance(out_shape, (tuple, list))
    return pl.pallas_call(
        body,
        out_shape=out_shape,
        in_specs=[whole()] * n_in,
        out_specs=tuple(whole() for _ in out_shape) if many else whole(),
        scratch_shapes=list(scratch),
        compiler_params=pltpu.CompilerParams(vmem_limit_bytes=limit),
        cost_estimate=pl.CostEstimate(flops=flops, bytes_accessed=moved, transcendentals=0),
    )


def blocks(width):
    return [slice(LANES * k, LANES * (k + 1)) for k in range(width // LANES)]


def wide_rows(count):
    return -(-count // LANES)


def row_block(row, rows):
    width = row.shape[1]
    padded = wide_rows(width) * LANES
    if padded != width:
        row = jnp.concatenate([row, jnp.zeros((1, padded - width), f32)], 1)
    place = lax.broadcasted_iota(jnp.int32, (rows, LANES), 0)
    out = jnp.zeros((rows, LANES), f32)
    for k, cut in enumerate(blocks(padded)):
        out = jnp.where(place == k, jnp.broadcast_to(row[:, cut], (rows, LANES)), out)
    return out


def block_row(block, count):
    return jnp.concatenate([block[k : k + 1] for k in range(count)], 1)


def split3(value):
    high = value.astype(bf16).astype(f32)
    rest = value - high
    mid = rest.astype(bf16).astype(f32)
    return (high, mid, rest - mid)


def lanes_of(shape):
    return lax.broadcasted_iota(jnp.int32, shape, 1)


def turned(rows, ray_count):
    fill = LANES - rows.shape[0]
    return jnp.concatenate([rows, jnp.zeros((fill, ray_count), f32)], 0).T


def fold(extra, own_rows, regions):
    fold_rows = min(own_rows, 16)
    groups = own_rows // fold_rows
    extra = extra.reshape(regions, own_rows, LANES)
    out = extra[:, :fold_rows]
    for g in range(1, groups):
        piece = extra[:, fold_rows * g : fold_rows * (g + 1)].reshape(regions * fold_rows, LANES)
        piece = pltpu.roll(piece, (LANES // groups) * g, 1)
        out = out + piece.reshape(regions, fold_rows, LANES)
    return out


def unfold(folded, own_rows, used):
    regions, fold_rows, _ = folded.shape
    groups = own_rows // fold_rows
    flat = folded.reshape(regions * fold_rows, LANES)
    keep = lanes_of(flat.shape) < used
    parts = []
    for g in range(groups):
        piece = flat if g == 0 else pltpu.roll(flat, LANES - (LANES // groups) * g, 1)
        parts.append(jnp.where(keep, piece, 0.0).reshape(regions, fold_rows, LANES))
    return jnp.concatenate(parts, 1) if groups > 1 else parts[0]


def pack_body(in_ref, mid_ref, feat_ref, vec_ref, out_ref):
    spot = 0
    for ref in (in_ref, mid_ref, feat_ref):
        rows, width = ref.shape[2:]
        for cut in blocks(width):
            out_ref[spot : spot + rows, :] = ref[0, 0, :, cut].astype(bf16)
            spot += rows
    out_ref[spot : spot + 16, :] = row_block(vec_ref[0], 16).astype(bf16)


def forward_body(
    pack_ref,
    codes_ref,
    bins_ref,
    entry_ref,
    exit_ref,
    send_ref,
    enc_ref,
    one_ref,
    two_ref,
    colour_ref,
    scalar_ref,
    mid_ref,
    head_ref,
    *,
    shapes,
    vec_share,
    regions,
):
    shards = pack_ref.shape[0]
    samples, ray_count = bins_ref.shape
    own_rows = ray_count // regions
    in_rows, hidden = shapes[0]
    mid_rows = shapes[1][0]
    feat_rows, feat = shapes[2]
    spot = 0
    mats = []
    for rows, width in shapes:
        pieces = []
        for cut in blocks(width):
            pieces.append(
                jnp.concatenate([pack_ref[s, spot : spot + rows, :] for s in range(shards)], 0)
            )
            spot += rows
        mats.append(jnp.concatenate(pieces, 1))
    in_weight, mid_weight, feat_weight = mats
    vec_total = vec_share * shards
    vec = jnp.zeros((1, vec_total), f32)
    for s in range(shards):
        block = pack_ref[s, spot : spot + 16, :].astype(f32)
        count = wide_rows(vec_share)
        row = block_row(block, count)
        fill = vec_total - count * LANES
        if fill:
            row = jnp.concatenate([row, jnp.zeros((1, fill), f32)], 1)
        if s:
            row = pltpu.roll(row, vec_share * s, 1)
        vec = vec + row
    bias_one = vec[:, :hidden]
    bias_two = vec[:, hidden : 2 * hidden]
    density_row = vec[:, 2 * hidden : 3 * hidden]
    bias_feat = vec[:, 3 * hidden :]
    density_cols = jnp.broadcast_to(density_row, (LANES, hidden)).T
    mid_ref[...] = mid_weight
    head_ref[...] = jnp.concatenate([feat_weight, density_cols.astype(bf16)], 1)

    bins = bins_ref[...].astype(f32)
    slot = lax.broadcasted_iota(jnp.int32, bins.shape, 0)
    following = jnp.where(slot == samples - 1, float(BINS), pltpu.roll(bins, samples - 1, 0))
    spacing = (following - bins) * (depth_scale / (regions * BINS))
    inside = ((slot >= entry_ref[...]) & (slot < exit_ref[...])).astype(f32)
    position = turned((bins + 0.5) / BINS, ray_count)
    code_zero = codes_ref[0].astype(f32)
    code_one = codes_ref[1].astype(f32)
    density = jnp.zeros((ray_count, LANES), f32)
    lane = lanes_of((hidden, LANES))
    for j in range(samples):
        rows = slice(ray_count * j, ray_count * (j + 1))
        encoded = (code_zero + position[:, j : j + 1] * code_one).astype(bf16)
        enc_ref[rows, :] = encoded
        one = jnp.dot(encoded, in_weight, preferred_element_type=f32) + bias_one
        one = jnp.maximum(one, 0.0).astype(bf16)
        one_ref[rows, :] = one
        two = jnp.dot(one, mid_weight, preferred_element_type=f32) + bias_two
        two = jnp.maximum(two, 0.0).astype(bf16)
        two_ref[rows, :] = two
        head = jnp.concatenate(
            [feat_weight, jnp.where(lane == j, density_cols, 0.0).astype(bf16)], 1
        )
        raw = jnp.dot(two, head, preferred_element_type=f32)
        density = density + raw[:, feat:]
        colour_ref[rows, :] = 0.5 * jnp.tanh(0.5 * (raw[:, :feat] + bias_feat)) + 0.5
    density = density.T[:samples]
    soft = jnp.maximum(density, 0.0) + jnp.log1p(jnp.exp(-jnp.abs(density)))
    optical = soft * spacing * inside
    before = [jnp.zeros((1, ray_count), f32)]
    for j in range(samples):
        before.append(before[-1] + optical[j : j + 1])
    depth = before.pop()
    optical_before = jnp.concatenate(before, 0)
    local_weight = jnp.exp(-optical_before) * (jnp.tanh(0.5 * optical) * (1.0 + jnp.exp(-optical)))
    sig = 0.5 * jnp.tanh(0.5 * density) + 0.5
    scalar_ref[0] = local_weight
    scalar_ref[1] = jnp.exp(-(optical_before + optical))
    scalar_ref[2] = spacing * inside * sig
    columns = turned(jnp.concatenate([*split3(depth), local_weight], 0), ray_count)
    total = jnp.zeros((ray_count, feat), f32)
    for j in range(samples):
        rows = slice(ray_count * j, ray_count * (j + 1))
        total = total + columns[:, 3 + j : 4 + j] * colour_ref[rows, :]
    extra = jnp.where(lanes_of(columns.shape) < 3, columns, 0.0)
    parts = [total[:, cut].reshape(regions, own_rows, LANES) for cut in blocks(feat)]
    parts.append(fold(extra, own_rows, regions))
    send_ref[...] = jnp.concatenate(parts, 1).astype(bf16)


def owner_body(got_ref, target_ref, direction_ref, out_ref):
    regions = got_ref.shape[0]
    own_rows, feat = target_ref.shape
    cuts = blocks(feat)
    got = got_ref[...].astype(f32)
    extra = unfold(got[:, own_rows * len(cuts) :], own_rows, 3)
    depth = [jnp.sum(extra[q], 1, keepdims=True) for q in range(regions)]
    onward = direction_ref[...] == 0

    def side(values):
        below, above = ([jnp.zeros_like(values[0])], [jnp.zeros_like(values[0])])
        for q in range(regions - 1):
            below.append(below[-1] + values[q])
            above.append(above[-1] + values[regions - 1 - q])
        return (below, above[::-1])

    below, above = side(depth)
    trans = [jnp.exp(-jnp.where(onward, below[q], above[q])) for q in range(regions)]

    def part(q, k):
        return got[q, own_rows * k : own_rows * (k + 1)]

    grads = []
    for k, cut in enumerate(cuts):
        rendered = trans[0] * part(0, k)
        for q in range(1, regions):
            rendered = rendered + trans[q] * part(q, k)
        grads.append((rendered - target_ref[:, cut].astype(f32)).astype(bf16).astype(f32))
    region_grad = []
    for q in range(regions):
        product = grads[0] * part(q, 0)
        for k in range(1, len(cuts)):
            product = product + grads[k] * part(q, k)
        region_grad.append(trans[q] * jnp.sum(product, 1, keepdims=True))
    below, above = side(region_grad)
    lane = lanes_of((own_rows, LANES))
    for q in range(regions):
        after = jnp.where(onward, above[q], below[q])
        extra = jnp.zeros((own_rows, LANES), f32)
        for i, piece in enumerate((*split3(trans[q]), *split3(after))):
            extra = jnp.where(lane == i, piece, extra)
        out_ref[q] = jnp.concatenate([*grads, fold(extra, own_rows, 1)[0]], 0).astype(bf16)


def over_rows(left, right):
    return lax.dot_general(left, right, (((0,), (0,)), ((), ())), preferred_element_type=f32)


def across(left, right):
    return lax.dot_general(left, right, (((1,), (1,)), ((), ())), preferred_element_type=f32)


def backward_body(
    got_ref,
    enc_ref,
    one_ref,
    two_ref,
    colour_ref,
    scalar_ref,
    mid_ref,
    head_ref,
    out_ref,
    depth_ref,
    head_grad_ref,
    second_ref,
    first_ref,
    *,
    shapes,
    vec_share,
    shards,
):
    regions = got_ref.shape[0]
    samples, ray_count = scalar_ref.shape[1:]
    own_rows = ray_count // regions
    hidden = mid_ref.shape[0]
    feat = colour_ref.shape[1]
    cuts = blocks(feat)
    got = got_ref[...].astype(f32)
    grad = jnp.concatenate(
        [
            got[:, own_rows * k : own_rows * (k + 1)].reshape(ray_count, LANES)
            for k in range(len(cuts))
        ],
        1,
    )
    extra = unfold(got[:, own_rows * len(cuts) :], own_rows, 6).reshape(ray_count, LANES).T
    trans = extra[0:1] + extra[1:2] + extra[2:3]
    after = extra[3:4] + extra[4:5] + extra[5:6]
    depth_ref[...] = -after
    lane = lanes_of((ray_count, LANES))
    sample_grad = jnp.zeros((ray_count, LANES), f32)
    for j in range(samples):
        rows = slice(ray_count * j, ray_count * (j + 1))
        product = jnp.sum(colour_ref[rows, :] * grad, 1, keepdims=True)
        sample_grad = jnp.where(lane == j, product, sample_grad)
    sample_grad = sample_grad.T[:samples]
    local_weight = scalar_ref[0]
    weighted = local_weight * sample_grad
    later = [jnp.zeros((1, ray_count), f32)]
    for j in range(samples - 1, 0, -1):
        later.append(later[-1] + weighted[j : j + 1])
    later = jnp.concatenate(later[::-1], 0)
    optical_grad = trans * (scalar_ref[1] * sample_grad - later) - after
    density_grad = optical_grad * scalar_ref[2]
    columns = turned(jnp.concatenate([trans * local_weight, density_grad], 0), ray_count)
    first_sum = jnp.zeros((1, hidden), f32)
    second_sum = jnp.zeros((1, hidden), f32)
    colour_sum = jnp.zeros((1, feat), f32)
    for j in range(samples):
        rows = slice(ray_count * j, ray_count * (j + 1))
        colour = colour_ref[rows, :]
        colour_grad = (columns[:, j : j + 1] * grad * colour * (1.0 - colour)).astype(bf16)
        density_part = jnp.where(lane == samples + j, columns, 0.0).astype(bf16)
        head_grad = jnp.concatenate([colour_grad, density_part], 1)
        head_grad_ref[rows, :] = head_grad
        hidden_grad = across(head_grad, head_ref[...])
        second = jnp.where(two_ref[rows, :].astype(f32) > 0, hidden_grad, 0.0).astype(bf16)
        second_ref[rows, :] = second
        below = across(second, mid_ref[...])
        first = jnp.where(one_ref[rows, :].astype(f32) > 0, below, 0.0).astype(bf16)
        first_ref[rows, :] = first
        colour_sum = colour_sum + jnp.sum(colour_grad.astype(f32), 0, keepdims=True)
        second_sum = second_sum + jnp.sum(second.astype(f32), 0, keepdims=True)
        first_sum = first_sum + jnp.sum(first.astype(f32), 0, keepdims=True)
    in_grad = over_rows(enc_ref[...], first_ref[...])
    mid_grad = over_rows(one_ref[...], second_ref[...])
    head_grad = over_rows(two_ref[...], head_grad_ref[...])
    density_sum = jnp.sum(head_grad[:, feat:].T, 0, keepdims=True)
    vec = jnp.concatenate([first_sum, second_sum, density_sum, colour_sum], 1)
    spot = 0
    for (rows, width), value in zip(shapes, (in_grad, mid_grad, head_grad)):
        for cut in blocks(width):
            for s in range(shards):
                out_ref[s, spot : spot + rows, :] = value[rows * s : rows * (s + 1), cut]
            spot += rows
    total = vec.shape[1]
    for s in range(shards):
        row = pltpu.roll(vec, total - vec_share * s, 1) if s else vec
        out_ref[s, spot : spot + 16, :] = row_block(row[:, : wide_rows(vec_share) * LANES], 16)


def adam_body(grad_ref, *refs):
    state_refs, out_refs = (refs[:4], refs[4:])

    def update(stacked, gradient):
        first_moment = beta_one * stacked[1] + (1.0 - beta_one) * gradient
        second = beta_two * stacked[2] + (1.0 - beta_two) * gradient * gradient
        step = first_moment / first_fix / (jnp.sqrt(second / second_fix) + epsilon)
        return (stacked[0] - learn_rate * step, first_moment, second)

    shards = grad_ref.shape[0]
    spot = 0
    for ref, out in zip(state_refs[:3], out_refs[:3]):
        rows, width = ref.shape[2:]
        for cut in blocks(width):
            gradient = grad_ref[0, spot : spot + rows, :]
            for s in range(1, shards):
                gradient = gradient + grad_ref[s, spot : spot + rows, :]
            spot += rows
            new = update([ref[i, 0, :, cut] for i in range(3)], gradient)
            for i in range(3):
                out[i, 0, :, cut] = new[i]
    ref, out = (state_refs[3], out_refs[3])
    share = ref.shape[2]
    block = grad_ref[0, spot : spot + 16, :]
    for s in range(1, shards):
        block = block + grad_ref[s, spot : spot + 16, :]
    gradient = block_row(block, wide_rows(share))[:, :share]
    new = update([ref[i] for i in range(3)], gradient)
    for i in range(3):
        out[i] = new[i]


def shaped(shape, dtype):
    return jax.ShapeDtypeStruct(shape, dtype)


def per_device(
    ray_codes,
    target,
    direction,
    entries,
    exits,
    depth_bins,
    in_layer,
    mid_layer,
    feat_layer,
    vectors,
):
    regions = lax.axis_size("region")
    shards = lax.axis_size("rays")
    region = lax.axis_index("region")
    samples, ray_count = depth_bins.shape[1:]
    own_rows = ray_count // regions
    layers = (in_layer, mid_layer, feat_layer)
    shapes = tuple(layer.shape[2:] for layer in layers)
    vec_share = vectors.shape[2]
    hidden = shapes[0][1]
    feat = shapes[2][1]
    code_width = ray_codes.shape[2]
    pack_rows = sum(rows * (width // LANES) for rows, width in shapes) + 16
    block_rows = own_rows * (feat // LANES) + min(own_rows, 16)
    total = samples * ray_count

    pack = call(pack_body, shaped((pack_rows, LANES), bf16), 4)(*layers, vectors)
    packs = lax.all_gather(pack, "rays", axis=0)
    send, encoded, one, two, colour, scalars, mid_weight, head_weight = call(
        functools.partial(forward_body, shapes=shapes, vec_share=vec_share, regions=regions),
        (
            shaped((regions, block_rows, LANES), bf16),
            shaped((total, code_width), bf16),
            shaped((total, hidden), bf16),
            shaped((total, hidden), bf16),
            shaped((total, feat), f32),
            shaped((3, samples, ray_count), f32),
            shaped((hidden, hidden), bf16),
            shaped((hidden, feat + LANES), bf16),
        ),
        5,
    )(packs, ray_codes, depth_bins[0], entries, exits)
    got = lax.all_to_all(send, "region", 0, 0)
    own_target = lax.dynamic_slice_in_dim(target, region * own_rows, own_rows, 0)
    own_direction = lax.dynamic_slice_in_dim(direction, region * own_rows, own_rows, 0)
    reply = call(owner_body, shaped((regions, block_rows, LANES), bf16), 3)(
        got, own_target, own_direction[:, None]
    )
    answer = lax.all_to_all(reply, "region", 0, 0)
    grads, depth_grad = call(
        functools.partial(
            backward_body, shapes=shapes, vec_share=vec_share, shards=shards
        ),
        (shaped((shards, pack_rows, LANES), f32), shaped((1, ray_count), f32)),
        8,
        scratch=(
            pltpu.VMEM((total, feat + LANES), bf16),
            pltpu.VMEM((total, hidden), bf16),
            pltpu.VMEM((total, hidden), bf16),
        ),
    )(answer, encoded, one, two, colour, scalars, mid_weight, head_weight)
    if shards == 2:
        mine = lax.axis_index("rays")
        other = lax.dynamic_index_in_dim(grads, 1 - mine, 0, keepdims=False)
        keep = lax.dynamic_index_in_dim(grads, mine, 0, keepdims=False)
        other = lax.ppermute(other, "rays", [(0, 1), (1, 0)])
        shares = jnp.stack([keep, other])
    else:
        shares = lax.all_to_all(grads, "rays", 0, 0)
    states = (*layers, vectors)
    new = call(adam_body, tuple(shaped(s.shape, f32) for s in states), 5)(shares, *states)
    return (*new, depth_grad)


def solution(mesh):
    placed = (
        P(None, "rays", None),
        P("rays", None),
        P("rays"),
        P("region", "rays"),
        P("region", "rays"),
        P("region", None, "rays"),
        P(None, "region", "rays", None),
        P(None, "region", "rays", None),
        P(None, "region", "rays", None),
        P(None, "region", "rays"),
    )
    return jax.shard_map(
        per_device,
        mesh=mesh,
        in_specs=placed,
        out_specs=(
            P(None, "region", "rays", None),
            P(None, "region", "rays", None),
            P(None, "region", "rays", None),
            P(None, "region", "rays"),
            P("region", "rays"),
        ),
        check_vma=False,
    )
```

```python
import functools

import jax
import jax.numpy as jnp
from jax import lax
from jax.experimental import pallas as pl
from jax.experimental.pallas import tpu as pltpu
from jax.sharding import PartitionSpec as P

BINS = 64
LANES = 128

depth_scale = 4.0
beta_one = 0.9
beta_two = 0.999
learn_rate = 0.001
epsilon = 1e-08
first_fix = 1.0 - 0.9**10
second_fix = 1.0 - 0.999**10

f32 = jnp.float32
bf16 = jnp.bfloat16


def in_vmem(value):
    return pltpu.with_memory_space_constraint(value, pltpu.VMEM)


def in_hbm(value):
    return pltpu.with_memory_space_constraint(value, pltpu.HBM)


def call(body, out_shape, inputs, limit, scratch=(), specs=None, flops=1000000, moved=1000000):
    many = isinstance(out_shape, (tuple, list))
    spec = pl.BlockSpec(memory_space=pltpu.VMEM)
    return pl.pallas_call(
        body,
        out_shape=out_shape,
        in_specs=specs or [spec] * len(inputs),
        out_specs=tuple(spec for _ in out_shape) if many else spec,
        scratch_shapes=list(scratch),
        compiler_params=pltpu.CompilerParams(vmem_limit_bytes=limit * 1024 * 1024),
        cost_estimate=pl.CostEstimate(flops=flops, bytes_accessed=moved, transcendentals=0),
    )(*inputs)


def blocks(width):
    return [slice(LANES * k, LANES * (k + 1)) for k in range(width // LANES)]


def wide_rows(count):
    return -(-count // LANES)


def row_block(row, rows):
    width = row.shape[1]
    padded = wide_rows(width) * LANES
    if padded != width:
        row = jnp.concatenate([row, jnp.zeros((1, padded - width), f32)], 1)
    place = lax.broadcasted_iota(jnp.int32, (rows, LANES), 0)
    out = jnp.zeros((rows, LANES), f32)
    for k, cut in enumerate(blocks(padded)):
        out = jnp.where(place == k, jnp.broadcast_to(row[:, cut], (rows, LANES)), out)
    return out


def block_row(block, count):
    return jnp.concatenate([block[k : k + 1] for k in range(count)], 1)


def split3(value):
    high = value.astype(bf16).astype(f32)
    rest = value - high
    mid = rest.astype(bf16).astype(f32)
    return (high, mid, rest - mid)


def lanes_of(shape):
    return lax.broadcasted_iota(jnp.int32, shape, 1)


def turned(rows, ray_count):
    fill = LANES - rows.shape[0]
    return jnp.concatenate([rows, jnp.zeros((fill, ray_count), f32)], 0).T


def fold(extra, own_rows, regions):
    fold_rows = 8
    groups = own_rows // fold_rows
    extra = extra.reshape(regions, own_rows, LANES)
    out = extra[:, :fold_rows]
    for g in range(1, groups):
        piece = extra[:, fold_rows * g : fold_rows * (g + 1)].reshape(regions * fold_rows, LANES)
        piece = pltpu.roll(piece, (LANES // groups) * g, 1)
        out = out + piece.reshape(regions, fold_rows, LANES)
    return out


def unfold(folded, own_rows, used):
    regions, fold_rows, _ = folded.shape
    groups = own_rows // fold_rows
    flat = folded.reshape(regions * fold_rows, LANES)
    keep = lanes_of(flat.shape) < used
    parts = []
    for g in range(groups):
        piece = flat if g == 0 else pltpu.roll(flat, LANES - (LANES // groups) * g, 1)
        parts.append(jnp.where(keep, piece, 0.0).reshape(regions, fold_rows, LANES))
    return jnp.concatenate(parts, 1) if groups > 1 else parts[0]


def prepare_body(*refs, unit_length, own_rows):
    ins, refs = (refs[:10], refs[10:])
    pack_ref, enc_ref, geometry_ref, *refs = refs
    target_ref = refs.pop(0) if own_rows else None
    held, sems = (refs[:-1], refs[-1])
    copies = []

    def fetch(source, place):
        copies.append(pltpu.make_async_copy(source, place, sems.at[len(copies)]))
        copies[-1].start()

    for ref, hold in zip(ins[:4], held[:4]):
        fetch(ref.at[0], hold)
    for ref, hold in zip(ins[4:9], held[4:9]):
        fetch(ref, hold)
    if own_rows:
        first = pl.multiple_of(lax.axis_index("region") * own_rows, 16)
        fetch(ins[9].at[pl.ds(first, own_rows)], target_ref)
    spot = 0
    for copy, hold in zip(copies[:3], held[:3]):
        copy.wait()
        rows, width = hold.shape[1:]
        for cut in blocks(width):
            pack_ref[spot : spot + rows, :] = hold[0, :, cut].astype(bf16)
            spot += rows
    for copy in copies[3:]:
        copy.wait()
    pack_ref[spot : spot + 16, :] = row_block(held[3][...], 16).astype(bf16)
    codes, bins, entry, exit_, direction = held[4:9]
    bins = bins[0].astype(f32)
    samples, ray_count = bins.shape
    slot = lax.broadcasted_iota(jnp.int32, bins.shape, 0)
    following = jnp.where(slot == samples - 1, float(BINS), pltpu.roll(bins, samples - 1, 0))
    inside = ((slot >= entry[...]) & (slot < exit_[...])).astype(f32)
    geometry_ref[:samples] = (following - bins) * unit_length * inside
    geometry_ref[samples : samples + 1] = direction[...].astype(f32)
    position = turned((bins + 0.5) / BINS, ray_count)
    code_zero = codes[0].astype(f32)
    code_one = codes[1].astype(f32)
    for j in range(samples):
        encoded = code_zero + position[:, j : j + 1] * code_one
        enc_ref[ray_count * j : ray_count * (j + 1), :] = encoded.astype(bf16)


def assemble(packs, shapes, vec_share):
    shards = len(packs)
    spot = 0
    mats = []
    for rows, width in shapes:
        pieces = []
        for cut in blocks(width):
            pieces.append(jnp.concatenate([p[spot : spot + rows, :] for p in packs], 0))
            spot += rows
        mats.append(jnp.concatenate(pieces, 1))
    vec_total = vec_share * shards
    vec = jnp.zeros((1, vec_total), f32)
    for s, p in enumerate(packs):
        block = p[spot : spot + 16, :].astype(f32)
        count = wide_rows(vec_share)
        row = block_row(block, count)
        fill = vec_total - count * LANES
        if fill:
            row = jnp.concatenate([row, jnp.zeros((1, fill), f32)], 1)
        if s:
            row = pltpu.roll(row, vec_share * s, 1)
        vec = vec + row
    return (*mats, vec)


def forward_body(*refs, shapes, vec_share, regions, pair):
    both = None
    if pair:
        own_ref, other_ref, *refs, both = refs
        mine = lax.axis_index("rays")
        both[mine] = own_ref[...]
        both[1 - mine] = other_ref[...]
        packs = [both.at[0], both.at[1]]
    else:
        packs_ref, *refs = refs
        packs = [packs_ref.at[s] for s in range(packs_ref.shape[0])]
    enc_ref, geometry_ref, send_ref, one_ref, two_ref, colour_ref, scalar_ref, *refs = refs
    mid_ref, head_ref = refs
    samples, ray_count = scalar_ref.shape[1:]
    own_rows = ray_count // regions
    hidden = mid_ref.shape[0]
    feat = colour_ref.shape[1]
    in_weight, mid_weight, feat_weight, vec = assemble(packs, shapes, vec_share)
    bias_one = vec[:, :hidden]
    bias_two = vec[:, hidden : 2 * hidden]
    density_row = vec[:, 2 * hidden : 3 * hidden]
    bias_feat = vec[:, 3 * hidden :]
    density_cols = jnp.broadcast_to(density_row, (LANES, hidden)).T
    mid_ref[...] = mid_weight
    head_ref[...] = jnp.concatenate([feat_weight, density_cols.astype(bf16)], 1)
    geometry = geometry_ref[:samples]
    density = jnp.zeros((ray_count, LANES), f32)
    lane = lanes_of((ray_count, LANES))
    for j in range(samples):
        rows = slice(ray_count * j, ray_count * (j + 1))
        one = jnp.dot(enc_ref[rows, :], in_weight, preferred_element_type=f32) + bias_one
        one = jnp.maximum(one, 0.0).astype(bf16)
        one_ref[rows, :] = one
        two = jnp.dot(one, mid_weight, preferred_element_type=f32) + bias_two
        two = jnp.maximum(two, 0.0).astype(bf16)
        two_ref[rows, :] = two
        raw = jnp.dot(two, head_ref[...], preferred_element_type=f32)
        density = jnp.where(lane == j, raw[:, feat:], density)
        colour_ref[rows, :] = 0.5 * jnp.tanh(0.5 * (raw[:, :feat] + bias_feat)) + 0.5
    density = density.T[:samples]
    soft = jnp.maximum(density, 0.0) + jnp.log1p(jnp.exp(-jnp.abs(density)))
    optical = soft * geometry
    before = [jnp.zeros((1, ray_count), f32)]
    for j in range(samples):
        before.append(before[-1] + optical[j : j + 1])
    depth = before.pop()
    optical_before = jnp.concatenate(before, 0)
    local_weight = jnp.exp(-optical_before) * (jnp.tanh(0.5 * optical) * (1.0 + jnp.exp(-optical)))
    sig = 0.5 * jnp.tanh(0.5 * density) + 0.5
    scalar_ref[0] = local_weight
    scalar_ref[1] = jnp.exp(-(optical_before + optical))
    scalar_ref[2] = geometry * sig
    direction = geometry_ref[samples : samples + 1]
    columns = turned(
        jnp.concatenate([*split3(depth), direction, local_weight], 0), ray_count
    )
    total = jnp.zeros((ray_count, feat), f32)
    for j in range(samples):
        rows = slice(ray_count * j, ray_count * (j + 1))
        total = total + columns[:, 4 + j : 5 + j] * colour_ref[rows, :]
    extra = jnp.where(lane < 4, columns, 0.0)
    parts = [total[:, cut].reshape(regions, own_rows, LANES) for cut in blocks(feat)]
    parts.append(fold(extra, own_rows, regions))
    send_ref[...] = jnp.concatenate(parts, 1).astype(bf16)


def owner_body(got_ref, target_ref, out_ref):
    regions = got_ref.shape[0]
    own_rows, feat = target_ref.shape
    cuts = blocks(feat)
    got = got_ref[...].astype(f32)
    extra = unfold(got[:, own_rows * len(cuts) :], own_rows, 4)
    lane = lanes_of((own_rows, LANES))
    depth = [
        jnp.sum(jnp.where(lane < 3, extra[q], 0.0), 1, keepdims=True) for q in range(regions)
    ]
    onward = extra[0][:, 3:4] < 0.5

    def side(values):
        below, above = ([jnp.zeros_like(values[0])], [jnp.zeros_like(values[0])])
        for q in range(regions - 1):
            below.append(below[-1] + values[q])
            above.append(above[-1] + values[regions - 1 - q])
        return (below, above[::-1])

    below, above = side(depth)
    trans = [jnp.exp(-jnp.where(onward, below[q], above[q])) for q in range(regions)]

    def part(q, k):
        return got[q, own_rows * k : own_rows * (k + 1)]

    grads = []
    for k, cut in enumerate(cuts):
        rendered = trans[0] * part(0, k)
        for q in range(1, regions):
            rendered = rendered + trans[q] * part(q, k)
        grads.append((rendered - target_ref[:, cut].astype(f32)).astype(bf16).astype(f32))
    region_grad = []
    for q in range(regions):
        product = grads[0] * part(q, 0)
        for k in range(1, len(cuts)):
            product = product + grads[k] * part(q, k)
        region_grad.append(trans[q] * jnp.sum(product, 1, keepdims=True))
    below, above = side(region_grad)
    for q in range(regions):
        after = jnp.where(onward, above[q], below[q])
        extra = jnp.zeros((own_rows, LANES), f32)
        for i, piece in enumerate((*split3(trans[q]), *split3(after))):
            extra = jnp.where(lane == i, piece, extra)
        out_ref[q] = jnp.concatenate([*grads, fold(extra, own_rows, 1)[0]], 0).astype(bf16)


def over_rows(left, right):
    return lax.dot_general(left, right, (((0,), (0,)), ((), ())), preferred_element_type=f32)


def across(left, right):
    return lax.dot_general(left, right, (((1,), (1,)), ((), ())), preferred_element_type=f32)


def backward_body(
    got_ref,
    enc_ref,
    one_ref,
    two_ref,
    colour_ref,
    scalar_ref,
    mid_ref,
    head_ref,
    depth_ref,
    *refs,
    shapes,
    vec_share,
    shards,
):
    *outs, head_grad_ref, second_ref, first_ref, shares = refs
    regions = got_ref.shape[0]
    samples, ray_count = scalar_ref.shape[1:]
    own_rows = ray_count // regions
    hidden = mid_ref.shape[0]
    feat = colour_ref.shape[1]
    cuts = blocks(feat)
    got = got_ref[...].astype(f32)
    grad = jnp.concatenate(
        [
            got[:, own_rows * k : own_rows * (k + 1)].reshape(ray_count, LANES)
            for k in range(len(cuts))
        ],
        1,
    )
    extra = unfold(got[:, own_rows * len(cuts) :], own_rows, 6).reshape(ray_count, LANES).T
    trans = extra[0:1] + extra[1:2] + extra[2:3]
    after = extra[3:4] + extra[4:5] + extra[5:6]
    depth_ref[...] = -after
    lane = lanes_of((ray_count, LANES))
    sample_grad = jnp.zeros((ray_count, LANES), f32)
    for j in range(samples):
        rows = slice(ray_count * j, ray_count * (j + 1))
        product = jnp.sum(colour_ref[rows, :] * grad, 1, keepdims=True)
        sample_grad = jnp.where(lane == j, product, sample_grad)
    sample_grad = sample_grad.T[:samples]
    local_weight = scalar_ref[0]
    weighted = local_weight * sample_grad
    later = [jnp.zeros((1, ray_count), f32)]
    for j in range(samples - 1, 0, -1):
        later.append(later[-1] + weighted[j : j + 1])
    later = jnp.concatenate(later[::-1], 0)
    optical_grad = trans * (scalar_ref[1] * sample_grad - later) - after
    density_grad = optical_grad * scalar_ref[2]
    columns = turned(jnp.concatenate([trans * local_weight, density_grad], 0), ray_count)
    first_sum = jnp.zeros((1, hidden), f32)
    second_sum = jnp.zeros((1, hidden), f32)
    colour_sum = jnp.zeros((1, feat), f32)
    for j in range(samples):
        rows = slice(ray_count * j, ray_count * (j + 1))
        colour = colour_ref[rows, :]
        colour_grad = (columns[:, j : j + 1] * grad * colour * (1.0 - colour)).astype(bf16)
        density_part = jnp.where(lane == samples + j, columns, 0.0).astype(bf16)
        head_grad_ref[rows, :] = jnp.concatenate([colour_grad, density_part], 1)
        colour_sum = colour_sum + jnp.sum(colour_grad.astype(f32), 0, keepdims=True)
    hidden_grad = across(head_grad_ref[...], head_ref[...])
    second = jnp.where(two_ref[...].astype(f32) > 0, hidden_grad, 0.0).astype(bf16)
    second_ref[...] = second
    second_sum = jnp.sum(second.astype(f32), 0, keepdims=True)
    below = across(second_ref[...], mid_ref[...])
    first = jnp.where(one_ref[...].astype(f32) > 0, below, 0.0).astype(bf16)
    first_ref[...] = first
    first_sum = jnp.sum(first.astype(f32), 0, keepdims=True)
    in_grad = over_rows(enc_ref[...], first_ref[...])
    mid_grad = over_rows(one_ref[...], second_ref[...])
    head_grad = over_rows(two_ref[...], head_grad_ref[...])
    density_sum = jnp.sum(head_grad[:, feat:].T, 0, keepdims=True)
    vec = jnp.concatenate([first_sum, second_sum, density_sum, colour_sum], 1)
    values = [in_grad, mid_grad, head_grad[:, :feat]]
    shares = refs[-1]
    mine = lax.axis_index("rays")
    total = vec.shape[1]
    for s in range(shards):
        place = lax.rem(s + shards - mine, shards) if shards == 2 else s
        spot = 0
        for (rows, width), value in zip(shapes, values):
            for cut in blocks(width):
                shares[place, spot : spot + rows, :] = value[rows * s : rows * (s + 1), cut]
                spot += rows
        row = pltpu.roll(vec, total - vec_share * s, 1) if s else vec
        shares[place, spot : spot + 16, :] = row_block(row[:, : wide_rows(vec_share) * LANES], 16)
    if shards == 2:
        outs[0][...] = shares[0]
        outs[1][...] = shares[1]
    else:
        outs[0][...] = shares[...]


def adam_body(*refs, shards):
    grad_refs = refs[:shards]
    state_refs, out_refs = (refs[shards : shards + 4], refs[shards + 4 :])

    def update(stacked, gradient):
        first_moment = beta_one * stacked[1] + (1.0 - beta_one) * gradient
        second = beta_two * stacked[2] + (1.0 - beta_two) * gradient * gradient
        step = first_moment / first_fix / (jnp.sqrt(second / second_fix) + epsilon)
        return (stacked[0] - learn_rate * step, first_moment, second)

    def gathered(spot, rows):
        total = grad_refs[0][spot : spot + rows, :]
        for ref in grad_refs[1:]:
            total = total + ref[spot : spot + rows, :]
        return total

    spot = 0
    for ref, out in zip(state_refs[:3], out_refs[:3]):
        rows, width = ref.shape[2:]
        for cut in blocks(width):
            new = update([ref[i, 0, :, cut] for i in range(3)], gathered(spot, rows))
            spot += rows
            for i in range(3):
                out[i, 0, :, cut] = new[i]
    ref, out = (state_refs[3], out_refs[3])
    share = ref.shape[2]
    gradient = block_row(gathered(spot, 16), wide_rows(share))[:, :share]
    new = update([ref[i] for i in range(3)], gradient)
    for i in range(3):
        out[i] = new[i]


def shaped(shape, dtype):
    return jax.ShapeDtypeStruct(shape, dtype)


def per_device(
    ray_codes,
    target,
    direction,
    entries,
    exits,
    depth_bins,
    in_layer,
    mid_layer,
    feat_layer,
    vectors,
):
    regions = lax.axis_size("region")
    shards = lax.axis_size("rays")
    samples, ray_count = depth_bins.shape[1:]
    own_rows = ray_count // regions
    layers = (in_layer, mid_layer, feat_layer)
    states = (*layers, vectors)
    shapes = tuple(layer.shape[2:] for layer in layers)
    vec_share = vectors.shape[2]
    hidden = shapes[0][1]
    feat = shapes[2][1]
    code_width = ray_codes.shape[2]
    pack_rows = sum(rows * (width // LANES) for rows, width in shapes) + 16
    block_rows = own_rows * (feat // LANES) + 8
    total = samples * ray_count
    sizes = dict(shapes=shapes, vec_share=vec_share)
    pair = shards == 2
    flops = 2 * total * (code_width * hidden + hidden * hidden + hidden * (feat + LANES))

    arguments = (*states, ray_codes, depth_bins, entries, exits, direction[None], target)
    aligned = own_rows % 16 == 0
    pack, encoded, geometry, *own_target = call(
        functools.partial(
            prepare_body,
            unit_length=depth_scale / (regions * BINS),
            own_rows=own_rows if aligned else 0,
        ),
        (
            pltpu.VMEM((pack_rows, LANES), bf16),
            pltpu.VMEM((total, code_width), bf16),
            pltpu.VMEM((samples + 8, ray_count), f32),
        )
        + ((pltpu.VMEM((own_rows, feat), bf16),) if aligned else ()),
        [in_hbm(a) for a in arguments],
        16,
        scratch=[pltpu.VMEM(a.shape[1:], f32) for a in states]
        + [pltpu.VMEM(a.shape, a.dtype) for a in arguments[4:9]]
        + [pltpu.SemaphoreType.DMA((10,))],
        specs=[pl.BlockSpec(memory_space=pltpu.HBM)] * 10,
    )
    if aligned:
        own_target = own_target[0]
    else:
        first = lax.axis_index("region") * own_rows
        own_target = lax.dynamic_slice_in_dim(target, first, own_rows, 0)
    if pair:
        packs = (pack, lax.ppermute(pack, "rays", [(0, 1), (1, 0)]))
    else:
        packs = (lax.all_gather(pack, "rays", axis=0),)
    send, *kept = call(
        functools.partial(forward_body, regions=regions, pair=pair, **sizes),
        (
            shaped((regions, block_rows, LANES), bf16),
            pltpu.VMEM((total, hidden), bf16),
            pltpu.VMEM((total, hidden), bf16),
            pltpu.VMEM((total, feat), f32),
            pltpu.VMEM((3, samples, ray_count), f32),
            pltpu.VMEM((hidden, hidden), bf16),
            pltpu.VMEM((hidden, feat + LANES), bf16),
        ),
        [in_vmem(v) for v in (*packs, encoded, geometry)],
        16,
        scratch=[pltpu.VMEM((2, pack_rows, LANES), bf16)] if pair else (),
        flops=flops,
        moved=total * (feat + hidden) * 4,
    )
    got = lax.all_to_all(send, "region", 0, 0)
    reply = call(
        owner_body, shaped((regions, block_rows, LANES), bf16), (got, own_target), 8
    )
    answer = lax.all_to_all(reply, "region", 0, 0)
    share = shaped((pack_rows, LANES), f32)
    shares = shaped((shards, pack_rows, LANES), f32)
    depth_grad, *grads = call(
        functools.partial(backward_body, shards=shards, **sizes),
        (shaped((1, ray_count), f32),) + ((share, share) if pair else (shares,)),
        (answer, *[in_vmem(v) for v in (encoded, *kept)]),
        24,
        scratch=[
            pltpu.VMEM((total, feat + LANES), bf16),
            pltpu.VMEM((total, hidden), bf16),
            pltpu.VMEM((total, hidden), bf16),
            pltpu.VMEM((shards, pack_rows, LANES), f32),
        ],
        flops=2 * flops,
        moved=total * (feat + hidden) * 4,
    )
    if pair:
        parts = (grads[0], lax.ppermute(grads[1], "rays", [(0, 1), (1, 0)]))
    else:
        exchanged = lax.all_to_all(grads[0], "rays", 0, 0)
        parts = tuple(exchanged[s] for s in range(shards))
    new = call(
        functools.partial(adam_body, shards=shards),
        tuple(shaped(s.shape, f32) for s in states),
        (*parts, *states),
        16,
    )
    return (*new, depth_grad)


def solution(mesh):
    placed = (
        P(None, "rays", None),
        P("rays", None),
        P("rays"),
        P("region", "rays"),
        P("region", "rays"),
        P("region", None, "rays"),
        P(None, "region", "rays", None),
        P(None, "region", "rays", None),
        P(None, "region", "rays", None),
        P(None, "region", "rays"),
    )
    return jax.shard_map(
        per_device,
        mesh=mesh,
        in_specs=placed,
        out_specs=(
            P(None, "region", "rays", None),
            P(None, "region", "rays", None),
            P(None, "region", "rays", None),
            P(None, "region", "rays"),
            P("region", "rays"),
        ),
        check_vma=False,
    )
```

```python
import functools

import jax
import jax.numpy as jnp
from jax import lax
from jax.experimental import pallas as pl
from jax.experimental.pallas import tpu as pltpu
from jax.sharding import PartitionSpec as P

BINS = 64
LANES = 128
QUAD = 4

depth_scale = 4.0
beta_one = 0.9
beta_two = 0.999
learn_rate = 0.001
epsilon = 1e-08
first_fix = 1.0 - 0.9**10
second_fix = 1.0 - 0.999**10

f32 = jnp.float32
bf16 = jnp.bfloat16


def in_vmem(value):
    return pltpu.with_memory_space_constraint(value, pltpu.VMEM)


def in_hbm(value):
    return pltpu.with_memory_space_constraint(value, pltpu.HBM)


def call(body, out_shape, inputs, limit, scratch=(), specs=None, flops=1000000, moved=1000000):
    many = isinstance(out_shape, (tuple, list))
    spec = pl.BlockSpec(memory_space=pltpu.VMEM)
    return pl.pallas_call(
        body,
        out_shape=out_shape,
        in_specs=specs or [spec] * len(inputs),
        out_specs=tuple(spec for _ in out_shape) if many else spec,
        scratch_shapes=list(scratch),
        compiler_params=pltpu.CompilerParams(vmem_limit_bytes=limit * 1024 * 1024),
        cost_estimate=pl.CostEstimate(flops=flops, bytes_accessed=moved, transcendentals=0),
    )(*inputs)


def blocks(width):
    return [slice(LANES * k, LANES * (k + 1)) for k in range(width // LANES)]


def wide_rows(count):
    return -(-count // LANES)


def row_block(row, rows):
    width = row.shape[1]
    padded = wide_rows(width) * LANES
    if padded != width:
        row = jnp.concatenate([row, jnp.zeros((1, padded - width), f32)], 1)
    place = lax.broadcasted_iota(jnp.int32, (rows, LANES), 0)
    out = jnp.zeros((rows, LANES), f32)
    for k, cut in enumerate(blocks(padded)):
        out = jnp.where(place == k, jnp.broadcast_to(row[:, cut], (rows, LANES)), out)
    return out


def block_row(block, count):
    return jnp.concatenate([block[k : k + 1] for k in range(count)], 1)


def split3(value):
    high = value.astype(bf16).astype(f32)
    rest = value - high
    mid = rest.astype(bf16).astype(f32)
    return (high, mid, rest - mid)


def lanes_of(shape):
    return lax.broadcasted_iota(jnp.int32, shape, 1)


def turned(rows, ray_count):
    fill = LANES - rows.shape[0]
    return jnp.concatenate([rows, jnp.zeros((fill, ray_count), f32)], 0).T


def fold(extra):
    rays = extra.shape[0]
    groups = rays // 8
    out = extra[:8]
    for g in range(1, groups):
        out = out + pltpu.roll(extra[8 * g : 8 * (g + 1)], (LANES // groups) * g, 1)
    return out


def unfold(folded, rays, used):
    groups = rays // 8
    keep = lanes_of(folded.shape) < used
    parts = []
    for g in range(groups):
        piece = pltpu.roll(folded, LANES - (LANES // groups) * g, 1) if g else folded
        parts.append(jnp.where(keep, piece, 0.0))
    return jnp.concatenate(parts, 0)


def prepare_body(*refs, unit_length, slots):
    ins, refs = (refs[:10], refs[10:])
    pack_ref, enc_ref, geometry_ref, target_ref, *held, flat_geometry, flat_position, sems = refs
    group_rows = target_ref.shape[0]
    spot_in_quad = lax.rem(lax.axis_index("region"), slots)
    copies = []

    def fetch(source, place):
        copies.append(pltpu.make_async_copy(source, place, sems.at[len(copies)]))
        copies[-1].start()

    def group(k):
        return pl.ds(pl.multiple_of((spot_in_quad ^ k) * group_rows, group_rows), group_rows)

    for ref, hold in zip(ins[:4], held[:4]):
        fetch(ref.at[0], hold)
    for ref, hold in zip(ins[4:9], held[4:9]):
        fetch(ref, hold)
    fetch(ins[9].at[group(0)], target_ref)
    spot = 0
    for copy, hold in zip(copies[:3], held[:3]):
        copy.wait()
        rows, width = hold.shape[1:]
        for cut in blocks(width):
            pack_ref[spot : spot + rows, :] = hold[0, :, cut].astype(bf16)
            spot += rows
    for copy in copies[3:]:
        copy.wait()
    pack_ref[spot : spot + 16, :] = row_block(held[3][...], 16).astype(bf16)
    codes, bins, entry, exit_, direction = held[4:9]
    bins = bins[0].astype(f32)
    samples, ray_count = bins.shape
    slot = lax.broadcasted_iota(jnp.int32, bins.shape, 0)
    following = jnp.where(slot == samples - 1, float(BINS), pltpu.roll(bins, samples - 1, 0))
    inside = ((slot >= entry[...]) & (slot < exit_[...])).astype(f32)
    flat_geometry[:samples] = (following - bins) * unit_length * inside
    flat_geometry[samples : samples + 1] = direction[...].astype(f32)
    flat_position[...] = turned((bins + 0.5) / BINS, ray_count)
    for k in range(slots):
        geometry_ref[k] = flat_geometry[:, group(k)]
        code_zero = codes[0, group(k)].astype(f32)
        code_one = codes[1, group(k)].astype(f32)
        position = flat_position[group(k), :]
        for j in range(samples):
            encoded = code_zero + position[:, j : j + 1] * code_one
            enc_ref[k, group_rows * j : group_rows * (j + 1), :] = encoded.astype(bf16)


def assemble(packs, shapes, vec_share):
    shards = len(packs)
    spot = 0
    mats = []
    for rows, width in shapes:
        pieces = []
        for cut in blocks(width):
            pieces.append(jnp.concatenate([p[spot : spot + rows, :] for p in packs], 0))
            spot += rows
        mats.append(jnp.concatenate(pieces, 1))
    vec_total = vec_share * shards
    vec = jnp.zeros((1, vec_total), f32)
    for s, p in enumerate(packs):
        block = p[spot : spot + 16, :].astype(f32)
        count = wide_rows(vec_share)
        row = block_row(block, count)
        fill = vec_total - count * LANES
        if fill:
            row = jnp.concatenate([row, jnp.zeros((1, fill), f32)], 1)
        if s:
            row = pltpu.roll(row, vec_share * s, 1)
        vec = vec + row
    return (*mats, vec)


def forward_slots(slots, weights, enc_ref, geometry_ref, message_refs, kept):
    in_weight, mid_ref, head_ref, vec = weights
    one_ref, two_ref, colour_ref, scalar_ref = kept
    samples, ray_count = scalar_ref.shape[2:]
    hidden = mid_ref.shape[0]
    feat = colour_ref.shape[2]
    bias_one = vec[:, :hidden]
    bias_two = vec[:, hidden : 2 * hidden]
    bias_feat = vec[:, 3 * hidden :]
    lane = lanes_of((ray_count, LANES))
    for i, k in enumerate(slots):
        one = jnp.dot(enc_ref[k], in_weight, preferred_element_type=f32) + bias_one
        one = jnp.maximum(one, 0.0).astype(bf16)
        one_ref[i] = one
        two = jnp.dot(one, mid_ref[...], preferred_element_type=f32) + bias_two
        two = jnp.maximum(two, 0.0).astype(bf16)
        two_ref[i] = two
        raw = jnp.dot(two, head_ref[...], preferred_element_type=f32)
        colour_ref[i] = 0.5 * jnp.tanh(0.5 * (raw[:, :feat] + bias_feat)) + 0.5
        density = jnp.zeros((ray_count, LANES), f32)
        for j in range(samples):
            rows = slice(ray_count * j, ray_count * (j + 1))
            density = jnp.where(lane == j, raw[rows, feat:], density)
        density = density.T[:samples]
        geometry = geometry_ref[k, :samples]
        soft = jnp.maximum(density, 0.0) + jnp.log1p(jnp.exp(-jnp.abs(density)))
        optical = soft * geometry
        before = [jnp.zeros((1, ray_count), f32)]
        for j in range(samples):
            before.append(before[-1] + optical[j : j + 1])
        depth = before.pop()
        optical_before = jnp.concatenate(before, 0)
        opacity = jnp.tanh(0.5 * optical) * (1.0 + jnp.exp(-optical))
        local_weight = jnp.exp(-optical_before) * opacity
        sig = 0.5 * jnp.tanh(0.5 * density) + 0.5
        scalar_ref[i, 0] = local_weight
        scalar_ref[i, 1] = jnp.exp(-(optical_before + optical))
        scalar_ref[i, 2] = geometry * sig
        direction = geometry_ref[k, samples : samples + 1]
        columns = turned(
            jnp.concatenate([*split3(depth), direction, local_weight], 0), ray_count
        )
        total = jnp.zeros((ray_count, feat), f32)
        for j in range(samples):
            rows = slice(ray_count * j, ray_count * (j + 1))
            total = total + columns[:, 4 + j : 5 + j] * colour_ref[i, rows, :]
        extra = jnp.where(lane < 4, columns, 0.0)
        message_refs[i][...] = as_message([total[:, cut] for cut in blocks(feat)], extra)


def as_message(parts, extra):
    return jnp.concatenate([*parts, fold(extra)], 0).astype(bf16)


def from_message(value, rays, used):
    value = value.astype(f32)
    count = value.shape[0] // rays
    parts = [value[rays * k : rays * (k + 1)] for k in range(count)]
    return (parts, unfold(value[rays * count :], rays, used))


def forward_first_body(*refs, shapes, vec_share, pair, slots):
    both = None
    if pair:
        own_ref, other_ref, *refs, both = refs
        mine = lax.axis_index("rays")
        both[mine] = own_ref[...]
        both[1 - mine] = other_ref[...]
        packs = [both.at[0], both.at[1]]
    else:
        packs_ref, *refs = refs
        packs = [packs_ref.at[s] for s in range(packs_ref.shape[0])]
    enc_ref, geometry_ref, in_ref, mid_ref, head_ref, vec_ref, *refs = refs
    hidden = mid_ref.shape[0]
    in_weight, mid_weight, feat_weight, vec = assemble(packs, shapes, vec_share)
    density_row = vec[:, 2 * hidden : 3 * hidden]
    density_cols = jnp.broadcast_to(density_row, (LANES, hidden)).T
    in_ref[...] = in_weight
    mid_ref[...] = mid_weight
    head_ref[...] = jnp.concatenate([feat_weight, density_cols.astype(bf16)], 1)
    vec_ref[...] = vec
    weights = (in_weight, mid_ref, head_ref, vec)
    forward_slots(slots, weights, enc_ref, geometry_ref, refs[4:], refs[:4])


def forward_own_body(in_ref, mid_ref, head_ref, vec_ref, enc_ref, geometry_ref, *refs):
    weights = (in_ref[...], mid_ref, head_ref, vec_ref[...])
    forward_slots([0], weights, enc_ref, geometry_ref, refs[4:], refs[:4])


def sides(values):
    below, above = ([jnp.zeros_like(values[0])], [jnp.zeros_like(values[0])])
    for q in range(len(values) - 1):
        below.append(below[-1] + values[q])
        above.append(above[-1] + values[len(values) - 1 - q])
    return (below, above[::-1])


def gather_messages(refs, store, own, rays):
    for k, ref in enumerate(refs):
        store[own ^ k] = ref[...]
    members = [from_message(store[p], rays, 4) for p in range(len(refs))]
    parts = [m[0] for m in members]
    extras = [m[1] for m in members]
    lane = lanes_of(extras[0].shape)
    depth = [jnp.sum(jnp.where(lane < 3, e, 0.0), 1, keepdims=True) for e in extras]
    onward = extras[0][:, 3:4] < 0.5
    below, above = sides(depth)
    trans = [jnp.exp(-jnp.where(onward, b, a)) for b, a in zip(below, above)]
    return (parts, depth, onward, trans)


def weighted_sum(factors, parts):
    out = []
    for k in range(len(parts[0])):
        total = factors[0] * parts[0][k]
        for factor, part in zip(factors[1:], parts[1:]):
            total = total + factor * part[k]
        out.append(total)
    return out


def inner(left, right):
    total = left[0] * right[0]
    for a, b in zip(left[1:], right[1:]):
        total = total + a * b
    return jnp.sum(total, 1, keepdims=True)


def plane_body(*refs, rays):
    *messages, out_ref, store = refs
    own = lax.rem(lax.axis_index("region"), len(messages))
    parts, depth, onward, trans = gather_messages(messages, store, own, rays)
    total = depth[0]
    for value in depth[1:]:
        total = total + value
    lane = lanes_of((rays, LANES))
    extra = jnp.where(lane == 3, jnp.where(onward, 0.0, 1.0), 0.0)
    for i, piece in enumerate(split3(total)):
        extra = jnp.where(lane == i, piece, extra)
    out_ref[...] = as_message(weighted_sum(trans, parts), extra)


def owner_body(*refs, slots, planes):
    quad_refs, plane_refs = (refs[:slots], refs[slots : slots + planes])
    target_ref, *out_refs, quad_store, plane_store, reply = refs[slots + planes :]
    rays, feat = target_ref.shape
    region = lax.axis_index("region")
    own, own_plane = (lax.rem(region, slots), lax.div(region, slots))
    parts, _, onward, trans = gather_messages(quad_refs, quad_store, own, rays)
    plane_parts, _, _, plane_trans = gather_messages(plane_refs, plane_store, own_plane, rays)
    rendered = weighted_sum(plane_trans, plane_parts)
    grads = [
        (value - target_ref[:, cut].astype(f32)).astype(bf16).astype(f32)
        for value, cut in zip(rendered, blocks(feat))
    ]

    def later(values):
        below, above = sides(values)
        return [jnp.where(onward, a, b) for b, a in zip(below, above)]

    plane_after = later([t * inner(grads, p) for t, p in zip(plane_trans, plane_parts)])
    ahead = jnp.zeros((rays, 1), f32)
    reach = jnp.zeros((rays, 1), f32)
    for z in range(planes):
        ahead = jnp.where(own_plane == z, plane_trans[z], ahead)
        reach = jnp.where(own_plane == z, plane_after[z], reach)
    trans = [ahead * t for t in trans]
    after = later([t * inner(grads, p) for t, p in zip(trans, parts)])
    lane = lanes_of((rays, LANES))
    for p in range(slots):
        extra = jnp.zeros((rays, LANES), f32)
        for i, piece in enumerate((*split3(trans[p]), *split3(after[p] + reach))):
            extra = jnp.where(lane == i, piece, extra)
        reply[p] = fold(extra)
    for k, out_ref in enumerate(out_refs):
        out_ref[...] = jnp.concatenate([*grads, reply[own ^ k]], 0).astype(bf16)


def over_rows(left, right):
    return lax.dot_general(left, right, (((0,), (0,)), ((), ())), preferred_element_type=f32)


def across(left, right):
    return lax.dot_general(left, right, (((1,), (1,)), ((), ())), preferred_element_type=f32)


def backward_body(*refs, slots, group_count, shapes, vec_share, shards):
    last = 0 not in slots
    messages, refs = (refs[: len(slots)], refs[len(slots) :])
    enc_ref, one_ref, two_ref, colour_ref, scalar_ref, mid_ref, head_ref, *refs = refs
    if last:
        earlier, refs = (refs[:5], refs[5:])
        depth_ref, *outs, head_grad_ref, second_ref, first_ref, shares = refs
    else:
        *outs, depth_ref, head_grad_ref, second_ref, first_ref = refs
    samples, ray_count = scalar_ref.shape[2:]
    feat = colour_ref.shape[2]
    spot_in_quad = lax.rem(lax.axis_index("region"), group_count)

    def group(k):
        return pl.ds(pl.multiple_of((spot_in_quad ^ k) * ray_count, ray_count), ray_count)

    if last:
        depth_ref[:, group(0)] = earlier[4][...]
    lane = lanes_of((ray_count, LANES))
    first_sum, second_sum, colour_sum = (0.0, 0.0, 0.0)
    for i, k in enumerate(slots):
        grads, extra = from_message(messages[i][...], ray_count, 6)
        grad = jnp.concatenate(grads, 1)
        extra = extra.T
        trans = extra[0:1] + extra[1:2] + extra[2:3]
        after = extra[3:4] + extra[4:5] + extra[5:6]
        if last:
            depth_ref[:, group(k)] = -after
        else:
            depth_ref[...] = -after
        sample_grad = jnp.zeros((ray_count, LANES), f32)
        for j in range(samples):
            rows = slice(ray_count * j, ray_count * (j + 1))
            product = jnp.sum(colour_ref[i, rows, :] * grad, 1, keepdims=True)
            sample_grad = jnp.where(lane == j, product, sample_grad)
        sample_grad = sample_grad.T[:samples]
        local_weight = scalar_ref[i, 0]
        weighted = local_weight * sample_grad
        later = [jnp.zeros((1, ray_count), f32)]
        for j in range(samples - 1, 0, -1):
            later.append(later[-1] + weighted[j : j + 1])
        later = jnp.concatenate(later[::-1], 0)
        optical_grad = trans * (scalar_ref[i, 1] * sample_grad - later) - after
        density_grad = optical_grad * scalar_ref[i, 2]
        columns = turned(jnp.concatenate([trans * local_weight, density_grad], 0), ray_count)
        for j in range(samples):
            rows = slice(ray_count * j, ray_count * (j + 1))
            colour = colour_ref[i, rows, :]
            colour_grad = (columns[:, j : j + 1] * grad * colour * (1.0 - colour)).astype(bf16)
            density_part = jnp.where(lane == samples + j, columns, 0.0).astype(bf16)
            head_grad_ref[i, rows, :] = jnp.concatenate([colour_grad, density_part], 1)
            colour_sum = colour_sum + jnp.sum(colour_grad.astype(f32), 0, keepdims=True)
        hidden_grad = across(head_grad_ref[i], head_ref[...])
        second = jnp.where(two_ref[i].astype(f32) > 0, hidden_grad, 0.0).astype(bf16)
        second_ref[i] = second
        second_sum = second_sum + jnp.sum(second.astype(f32), 0, keepdims=True)
        below = across(second, mid_ref[...])
        first = jnp.where(one_ref[i].astype(f32) > 0, below, 0.0).astype(bf16)
        first_ref[i] = first
        first_sum = first_sum + jnp.sum(first.astype(f32), 0, keepdims=True)

    def rows_of(ref):
        return ref[...].reshape(-1, ref.shape[2])

    encoded = enc_ref[slots[0] : slots[-1] + 1].reshape(-1, enc_ref.shape[2])
    in_grad = over_rows(encoded, rows_of(first_ref))
    mid_grad = over_rows(rows_of(one_ref), rows_of(second_ref))
    head_grad = over_rows(rows_of(two_ref), rows_of(head_grad_ref))
    density_sum = jnp.sum(head_grad[:, feat:].T, 0, keepdims=True)
    vec = jnp.concatenate([first_sum, second_sum, density_sum, colour_sum], 1)
    values = [in_grad, mid_grad, head_grad[:, :feat], vec]
    if not last:
        for value, ref in zip(values, outs):
            ref[...] = value
        return
    values = [value + ref[...] for value, ref in zip(values, earlier)]
    vec = values.pop()
    mine = lax.axis_index("rays")
    total = vec.shape[1]
    for s in range(shards):
        place = lax.rem(s + shards - mine, shards) if shards == 2 else s
        spot = 0
        for (rows, width), value in zip(shapes, values):
            for cut in blocks(width):
                shares[place, spot : spot + rows, :] = value[rows * s : rows * (s + 1), cut]
                spot += rows
        row = pltpu.roll(vec, total - vec_share * s, 1) if s else vec
        shares[place, spot : spot + 16, :] = row_block(row[:, : wide_rows(vec_share) * LANES], 16)
    if shards == 2:
        outs[0][...] = shares[0]
        outs[1][...] = shares[1]
    else:
        outs[0][...] = shares[...]


def adam_body(*refs, shards):
    grad_refs = refs[:shards]
    state_refs, out_refs = (refs[shards : shards + 4], refs[shards + 4 :])

    def update(stacked, gradient):
        first_moment = beta_one * stacked[1] + (1.0 - beta_one) * gradient
        second = beta_two * stacked[2] + (1.0 - beta_two) * gradient * gradient
        step = first_moment / first_fix / (jnp.sqrt(second / second_fix) + epsilon)
        return (stacked[0] - learn_rate * step, first_moment, second)

    def gathered(spot, rows):
        total = grad_refs[0][spot : spot + rows, :]
        for ref in grad_refs[1:]:
            total = total + ref[spot : spot + rows, :]
        return total

    spot = 0
    for ref, out in zip(state_refs[:3], out_refs[:3]):
        rows, width = ref.shape[2:]
        for cut in blocks(width):
            new = update([ref[i, 0, :, cut] for i in range(3)], gathered(spot, rows))
            spot += rows
            for i in range(3):
                out[i, 0, :, cut] = new[i]
    ref, out = (state_refs[3], out_refs[3])
    share = ref.shape[2]
    gradient = block_row(gathered(spot, 16), wide_rows(share))[:, :share]
    new = update([ref[i] for i in range(3)], gradient)
    for i in range(3):
        out[i] = new[i]


def shaped(shape, dtype):
    return jax.ShapeDtypeStruct(shape, dtype)


def swap(value, distance, size):
    return lax.ppermute(value, "region", [(i, i ^ distance) for i in range(size)])


def per_device(
    ray_codes,
    target,
    direction,
    entries,
    exits,
    depth_bins,
    in_layer,
    mid_layer,
    feat_layer,
    vectors,
):
    regions = lax.axis_size("region")
    shards = lax.axis_size("rays")
    samples, ray_count = depth_bins.shape[1:]
    quad = min(QUAD, regions)
    planes = regions // quad
    rays = ray_count // quad
    layers = (in_layer, mid_layer, feat_layer)
    states = (*layers, vectors)
    shapes = tuple(layer.shape[2:] for layer in layers)
    vec_share = vectors.shape[2]
    hidden = shapes[0][1]
    feat = shapes[2][1]
    code_width = ray_codes.shape[2]
    pack_rows = sum(rows * (width // LANES) for rows, width in shapes) + 16
    rows = samples * rays
    sizes = dict(shapes=shapes, vec_share=vec_share)
    pair = shards == 2
    flops = 2 * rows * (code_width * hidden + hidden * hidden + hidden * (feat + LANES))

    arguments = (*states, ray_codes, depth_bins, entries, exits, direction[None], target)
    pack, encoded, geometry, own_target = call(
        functools.partial(prepare_body, unit_length=depth_scale / (regions * BINS), slots=quad),
        (
            pltpu.VMEM((pack_rows, LANES), bf16),
            pltpu.VMEM((quad, rows, code_width), bf16),
            pltpu.VMEM((quad, samples + 8, rays), f32),
            pltpu.VMEM((rays, feat), bf16),
        ),
        [in_hbm(a) for a in arguments],
        16,
        scratch=[pltpu.VMEM(a.shape[1:], f32) for a in states]
        + [pltpu.VMEM(a.shape, a.dtype) for a in arguments[4:9]]
        + [
            pltpu.VMEM((samples + 8, ray_count), f32),
            pltpu.VMEM((ray_count, LANES), f32),
            pltpu.SemaphoreType.DMA((10,)),
        ],
        specs=[pl.BlockSpec(memory_space=pltpu.HBM)] * 10,
    )
    if pair:
        packs = (pack, lax.ppermute(pack, "rays", [(0, 1), (1, 0)]))
    else:
        packs = (lax.all_gather(pack, "rays", axis=0),)

    message = pltpu.VMEM((rays * (feat // LANES) + 8, LANES), bf16)

    def kept_shapes(count):
        return (
            pltpu.VMEM((count, rows, hidden), bf16),
            pltpu.VMEM((count, rows, hidden), bf16),
            pltpu.VMEM((count, rows, feat), f32),
            pltpu.VMEM((count, 3, samples, rays), f32),
        )

    def moved(count):
        return count * rows * (feat + hidden) * 4

    others = tuple(range(1, quad))
    found = call(
        functools.partial(forward_first_body, pair=pair, slots=others, **sizes),
        (
            pltpu.VMEM((shapes[0][0] * shards, hidden), bf16),
            pltpu.VMEM((hidden, hidden), bf16),
            pltpu.VMEM((hidden, feat + LANES), bf16),
            pltpu.VMEM((1, vec_share * shards), f32),
        )
        + kept_shapes(quad - 1)
        + (message,) * (quad - 1),
        [in_vmem(v) for v in (*packs, encoded, geometry)],
        16,
        scratch=[pltpu.VMEM((2, pack_rows, LANES), bf16)] if pair else (),
        flops=(quad - 1) * flops,
        moved=moved(quad - 1),
    )
    weights, kept, sent = (found[:4], found[4:8], found[8:])
    got = [swap(value, k, regions) for k, value in zip(others, sent)]
    *kept_own, own_message = call(
        forward_own_body,
        kept_shapes(1) + (message,),
        [in_vmem(v) for v in (*weights, encoded, geometry)],
        16,
        flops=flops,
        moved=moved(1),
    )
    quad_messages = [in_vmem(v) for v in (own_message, *got)]
    store = pltpu.VMEM((quad, *message.shape), bf16)
    plane_store = pltpu.VMEM((planes, *message.shape), bf16)
    plane_message = call(
        functools.partial(plane_body, rays=rays), message, quad_messages, 16, scratch=[store]
    )
    plane_messages = [plane_message] + [
        swap(plane_message, quad * k, regions) for k in range(1, planes)
    ]
    replies = call(
        functools.partial(owner_body, slots=quad, planes=planes),
        (message,) * quad,
        quad_messages + [in_vmem(v) for v in (*plane_messages, own_target)],
        16,
        scratch=[store, plane_store, pltpu.VMEM((quad, 8, LANES), f32)],
    )
    answers = [swap(value, k, regions) for k, value in zip(others, replies[1:])]

    def rows_scratch(count):
        return [
            pltpu.VMEM((count, rows, feat + LANES), bf16),
            pltpu.VMEM((count, rows, hidden), bf16),
            pltpu.VMEM((count, rows, hidden), bf16),
        ]

    earlier = call(
        functools.partial(
            backward_body, slots=(0,), group_count=quad, shards=shards, **sizes
        ),
        (
            pltpu.VMEM((shapes[0][0] * shards, hidden), f32),
            pltpu.VMEM((hidden, hidden), f32),
            pltpu.VMEM((hidden, feat), f32),
            pltpu.VMEM((1, vec_share * shards), f32),
            pltpu.VMEM((1, rays), f32),
        ),
        [in_vmem(v) for v in (replies[0], encoded, *kept_own, weights[1], weights[2])],
        16,
        scratch=rows_scratch(1),
        flops=2 * flops,
        moved=moved(1),
    )
    share = pltpu.VMEM((pack_rows, LANES), f32)
    shares = shaped((shards, pack_rows, LANES), f32)
    depth_grad, *grads = call(
        functools.partial(
            backward_body, slots=others, group_count=quad, shards=shards, **sizes
        ),
        (shaped((1, ray_count), f32),) + ((share, share) if pair else (shares,)),
        [in_vmem(v) for v in (*answers, encoded, *kept, weights[1], weights[2], *earlier)],
        24,
        scratch=rows_scratch(quad - 1) + [pltpu.VMEM((shards, pack_rows, LANES), f32)],
        flops=2 * (quad - 1) * flops,
        moved=moved(quad - 1),
    )
    if pair:
        parts = (grads[0], lax.ppermute(grads[1], "rays", [(0, 1), (1, 0)]))
    else:
        exchanged = lax.all_to_all(grads[0], "rays", 0, 0)
        parts = tuple(exchanged[s] for s in range(shards))
    new = call(
        functools.partial(adam_body, shards=shards),
        tuple(shaped(s.shape, f32) for s in states),
        (*parts, *states),
        16,
    )
    return (*new, depth_grad)


def solution(mesh):
    placed = (
        P(None, "rays", None),
        P("rays", None),
        P("rays"),
        P("region", "rays"),
        P("region", "rays"),
        P("region", None, "rays"),
        P(None, "region", "rays", None),
        P(None, "region", "rays", None),
        P(None, "region", "rays", None),
        P(None, "region", "rays"),
    )
    return jax.shard_map(
        per_device,
        mesh=mesh,
        in_specs=placed,
        out_specs=(
            P(None, "region", "rays", None),
            P(None, "region", "rays", None),
            P(None, "region", "rays", None),
            P(None, "region", "rays"),
            P("region", "rays"),
        ),
        check_vma=False,
    )
```

```python
import functools

import jax
import jax.numpy as jnp
from jax import lax
from jax.experimental import pallas as pl
from jax.experimental.pallas import tpu as pltpu
from jax.sharding import PartitionSpec as P

BINS = 64
LANES = 128
QUAD = 4

depth_scale = 4.0
beta_one = 0.9
beta_two = 0.999
learn_rate = 0.001
epsilon = 1e-08
first_fix = 1.0 - 0.9**10
second_fix = 1.0 - 0.999**10

f32 = jnp.float32
bf16 = jnp.bfloat16


def in_vmem(value):
    return pltpu.with_memory_space_constraint(value, pltpu.VMEM)


def in_hbm(value):
    return pltpu.with_memory_space_constraint(value, pltpu.HBM)


def call(body, out_shape, inputs, limit, scratch=(), specs=None, flops=1000000, moved=1000000):
    many = isinstance(out_shape, (tuple, list))
    spec = pl.BlockSpec(memory_space=pltpu.VMEM)
    return pl.pallas_call(
        body,
        out_shape=out_shape,
        in_specs=specs or [spec] * len(inputs),
        out_specs=tuple(spec for _ in out_shape) if many else spec,
        scratch_shapes=list(scratch),
        compiler_params=pltpu.CompilerParams(vmem_limit_bytes=limit * 1024 * 1024),
        cost_estimate=pl.CostEstimate(flops=flops, bytes_accessed=moved, transcendentals=0),
    )(*inputs)


def blocks(width):
    return [slice(LANES * k, LANES * (k + 1)) for k in range(width // LANES)]


def wide_rows(count):
    return -(-count // LANES)


def row_block(row, rows):
    width = row.shape[1]
    padded = wide_rows(width) * LANES
    if padded != width:
        row = jnp.concatenate([row, jnp.zeros((1, padded - width), f32)], 1)
    place = lax.broadcasted_iota(jnp.int32, (rows, LANES), 0)
    out = jnp.zeros((rows, LANES), f32)
    for k, cut in enumerate(blocks(padded)):
        out = jnp.where(place == k, jnp.broadcast_to(row[:, cut], (rows, LANES)), out)
    return out


def block_row(block, count):
    return jnp.concatenate([block[k : k + 1] for k in range(count)], 1)


def split3(value):
    high = value.astype(bf16).astype(f32)
    rest = value - high
    mid = rest.astype(bf16).astype(f32)
    return (high, mid, rest - mid)


def lanes_of(shape):
    return lax.broadcasted_iota(jnp.int32, shape, 1)


def turned(rows, ray_count):
    fill = LANES - rows.shape[0]
    return jnp.concatenate([rows, jnp.zeros((fill, ray_count), f32)], 0).T


def own_group(k, slots, rows):
    place = lax.rem(lax.axis_index("region"), slots) ^ k
    return pl.ds(pl.multiple_of(place * rows, rows), rows)


def fetch_body(*refs, slots):
    ins, (pack_ref, *refs) = (refs[:10], refs[10:])
    outs, held, sems = (refs[:6], refs[6:10], refs[10])
    target_ref = outs[5]
    copies = []

    def fetch(source, place):
        copies.append(pltpu.make_async_copy(source, place, sems.at[len(copies)]))
        copies[-1].start()

    for ref, hold in zip(ins[:4], held):
        fetch(ref.at[0], hold)
    for ref, out in zip(ins[4:9], outs):
        fetch(ref, out)
    fetch(ins[9].at[own_group(0, slots, target_ref.shape[0])], target_ref)
    spot = 0
    for copy, hold in zip(copies[:3], held[:3]):
        copy.wait()
        rows, width = hold.shape[1:]
        for cut in blocks(width):
            pack_ref[spot : spot + rows, :] = hold[0, :, cut].astype(bf16)
            spot += rows
    copies[3].wait()
    pack_ref[spot : spot + 16, :] = row_block(held[3][...], 16).astype(bf16)
    for copy in copies[4:]:
        copy.wait()


def encode_body(*refs, unit_length, slots):
    codes, bins, entry, exit_, direction, enc_ref, geometry_ref, *refs = refs
    flat_geometry, flat_position = refs
    bins = bins[0].astype(f32)
    samples, ray_count = bins.shape
    group_rows = ray_count // slots
    slot = lax.broadcasted_iota(jnp.int32, bins.shape, 0)
    following = jnp.where(slot == samples - 1, float(BINS), pltpu.roll(bins, samples - 1, 0))
    inside = ((slot >= entry[...]) & (slot < exit_[...])).astype(f32)
    flat_geometry[:samples] = (following - bins) * unit_length * inside
    flat_geometry[samples : samples + 1] = direction[...].astype(f32)
    flat_position[...] = turned((bins + 0.5) / BINS, ray_count)
    for k in range(slots):
        group = own_group(k, slots, group_rows)
        geometry_ref[k] = flat_geometry[:, group]
        code_zero = codes[0, group].astype(f32)
        code_one = codes[1, group].astype(f32)
        position = flat_position[group, :]
        for j in range(samples):
            encoded = code_zero + position[:, j : j + 1] * code_one
            enc_ref[k, group_rows * j : group_rows * (j + 1), :] = encoded.astype(bf16)


def assemble(packs, shapes, vec_share):
    shards = len(packs)
    spot = 0
    mats = []
    for rows, width in shapes:
        pieces = []
        for cut in blocks(width):
            pieces.append(jnp.concatenate([p[spot : spot + rows, :] for p in packs], 0))
            spot += rows
        mats.append(jnp.concatenate(pieces, 1))
    vec_total = vec_share * shards
    vec = jnp.zeros((1, vec_total), f32)
    for s, p in enumerate(packs):
        block = p[spot : spot + 16, :].astype(f32)
        count = wide_rows(vec_share)
        row = block_row(block, count)
        fill = vec_total - count * LANES
        if fill:
            row = jnp.concatenate([row, jnp.zeros((1, fill), f32)], 1)
        if s:
            row = pltpu.roll(row, vec_share * s, 1)
        vec = vec + row
    return (*mats, vec)


def forward_slots(slots, weights, enc_ref, geometry_ref, message_refs, kept):
    in_weight, mid_ref, head_ref, vec = weights
    one_ref, two_ref, turn_ref, scalar_ref = kept
    samples, ray_count = scalar_ref.shape[2:]
    hidden = mid_ref.shape[0]
    feat = turn_ref.shape[2]
    bias_one = vec[:, :hidden]
    bias_two = vec[:, hidden : 2 * hidden]
    half_bias = 0.5 * vec[:, 3 * hidden :]
    lane = lanes_of((ray_count, LANES))
    densities = []
    for i, k in enumerate(slots):
        one = jnp.dot(enc_ref[k], in_weight, preferred_element_type=f32) + bias_one
        one = jnp.maximum(one, 0.0).astype(bf16)
        one_ref[i] = one
        two = jnp.dot(one, mid_ref[...], preferred_element_type=f32) + bias_two
        two = jnp.maximum(two, 0.0).astype(bf16)
        two_ref[i] = two
        raw = jnp.dot(two, head_ref[...], preferred_element_type=f32)
        turn_ref[i] = jnp.tanh(raw[:, :feat] + half_bias)
        density = jnp.zeros((ray_count, LANES), f32)
        for j in range(samples):
            rows = slice(ray_count * j, ray_count * (j + 1))
            density = jnp.where(lane == j, raw[rows, feat:], density)
        densities.append(density)
    density = side_by_side([value.T[:samples] for value in densities])
    geometry = side_by_side([geometry_ref[k, :samples] for k in slots])
    direction = side_by_side([geometry_ref[k, samples : samples + 1] for k in slots])
    soft = jnp.maximum(density, 0.0) + jnp.log1p(jnp.exp(-jnp.abs(density)))
    optical = soft * geometry
    before = [jnp.zeros_like(direction)]
    for j in range(samples):
        before.append(before[-1] + optical[j : j + 1])
    depth = before.pop()
    optical_before = jnp.concatenate(before, 0)
    opacity = jnp.tanh(0.5 * optical) * (1.0 + jnp.exp(-optical))
    local_weight = jnp.exp(-optical_before) * opacity
    half_weight = 0.5 * local_weight
    half_sum = jnp.sum(half_weight, 0, keepdims=True)
    columns = turned(jnp.concatenate([half_weight, half_sum], 0), depth.shape[1])
    shared = jnp.concatenate([*split3(depth), direction], 0)
    sig = 0.5 * jnp.tanh(0.5 * density) + 0.5
    scalars = (local_weight, jnp.exp(-(optical_before + optical)), geometry * sig)
    for i, k in enumerate(slots):
        cut = slice(ray_count * i, ray_count * (i + 1))
        for q, value in enumerate(scalars):
            scalar_ref[i, q] = value[:, cut]
        own = columns[cut]
        total = jnp.zeros((ray_count, feat), f32) + own[:, samples : samples + 1]
        for j in range(samples):
            rows = slice(ray_count * j, ray_count * (j + 1))
            total = total + own[:, j : j + 1] * turn_ref[i, rows, :]
        message_refs[i][...] = as_message([total[:, k] for k in blocks(feat)], shared[:, cut])


def side_by_side(values):
    return jnp.concatenate(values, 1) if len(values) > 1 else values[0]


def as_message(parts, rows):
    count, rays = rows.shape
    if count < 8:
        rows = jnp.concatenate([rows, jnp.zeros((8 - count, rays), f32)], 0)
    if rays < LANES:
        rows = jnp.concatenate([rows, jnp.zeros((8, LANES - rays), f32)], 1)
    return jnp.concatenate([*parts, rows], 0).astype(bf16)


def from_message(value, rays):
    value = value.astype(f32)
    count = value.shape[0] // rays
    parts = [value[rays * k : rays * (k + 1)] for k in range(count)]
    return (parts, value[rays * count :, :rays])


def forward_first_body(*refs, shapes, vec_share, pair, slots):
    both = None
    if pair:
        own_ref, other_ref, *refs, both = refs
        mine = lax.axis_index("rays")
        both[mine] = own_ref[...]
        both[1 - mine] = other_ref[...]
        packs = [both.at[0], both.at[1]]
    else:
        packs_ref, *refs = refs
        packs = [packs_ref.at[s] for s in range(packs_ref.shape[0])]
    enc_ref, geometry_ref, in_ref, mid_ref, head_ref, vec_ref, *refs = refs
    hidden = mid_ref.shape[0]
    in_weight, mid_weight, feat_weight, vec = assemble(packs, shapes, vec_share)
    density_row = vec[:, 2 * hidden : 3 * hidden]
    density_cols = jnp.broadcast_to(density_row, (LANES, hidden)).T
    in_ref[...] = in_weight
    mid_ref[...] = mid_weight
    half_weight = (0.5 * feat_weight.astype(f32)).astype(bf16)
    head_ref[...] = jnp.concatenate([half_weight, density_cols.astype(bf16)], 1)
    vec_ref[...] = vec
    weights = (in_weight, mid_ref, head_ref, vec)
    forward_slots(slots, weights, enc_ref, geometry_ref, refs[4:], refs[:4])


def forward_rest_body(in_ref, mid_ref, head_ref, vec_ref, enc_ref, geometry_ref, *refs, slots):
    weights = (in_ref[...], mid_ref, head_ref, vec_ref[...])
    forward_slots(slots, weights, enc_ref, geometry_ref, refs[4:], refs[:4])


def sides(values):
    below, above = ([jnp.zeros_like(values[0])], [jnp.zeros_like(values[0])])
    for q in range(len(values) - 1):
        below.append(below[-1] + values[q])
        above.append(above[-1] + values[len(values) - 1 - q])
    return (below, above[::-1])


def gather_messages(refs, store, own, rays):
    for k, ref in enumerate(refs):
        store[own ^ k] = ref[...]
    members = [from_message(store[p], rays) for p in range(len(refs))]
    parts = [m[0] for m in members]
    depth = [m[1][0:1] + m[1][1:2] + m[1][2:3] for m in members]
    direction = members[0][1][3:4]
    below, above = sides(depth)
    trans = [jnp.exp(-jnp.where(direction < 0.5, b, a)) for b, a in zip(below, above)]
    return (parts, depth, direction, trans)


def as_columns(rows):
    columns = turned(jnp.concatenate(rows, 0), rows[0].shape[1])
    return [columns[:, i : i + 1] for i in range(len(rows))]


def weighted_sum(factors, parts):
    out = []
    for k in range(len(parts[0])):
        total = factors[0] * parts[0][k]
        for factor, part in zip(factors[1:], parts[1:]):
            total = total + factor * part[k]
        out.append(total)
    return out


def inner(left, right):
    total = left[0] * right[0]
    for a, b in zip(left[1:], right[1:]):
        total = total + a * b
    return jnp.sum(total, 1, keepdims=True)


def plane_body(*refs, rays):
    *messages, out_ref, store = refs
    own = lax.rem(lax.axis_index("region"), len(messages))
    parts, depth, direction, trans = gather_messages(messages, store, own, rays)
    total = depth[0]
    for value in depth[1:]:
        total = total + value
    rows = jnp.concatenate([*split3(total), direction], 0)
    out_ref[...] = as_message(weighted_sum(as_columns(trans), parts), rows)


def owner_body(*refs, slots, planes):
    quad_refs, plane_refs = (refs[:slots], refs[slots : slots + planes])
    target_ref, _, *out_refs, quad_store, plane_store, reply = refs[slots + planes :]
    rays, feat = target_ref.shape
    region = lax.axis_index("region")
    own, own_plane = (lax.rem(region, slots), lax.div(region, slots))
    parts, _, direction, trans = gather_messages(quad_refs, quad_store, own, rays)
    plane_parts, _, _, plane_trans = gather_messages(plane_refs, plane_store, own_plane, rays)
    rendered = weighted_sum(as_columns(plane_trans), plane_parts)
    grads = [
        (value - target_ref[:, cut].astype(f32)).astype(bf16).astype(f32)
        for value, cut in zip(rendered, blocks(feat))
    ]
    lane = lanes_of((rays, LANES))
    inners = jnp.zeros((rays, LANES), f32)
    for i, value in enumerate((*plane_parts, *parts)):
        inners = jnp.where(lane == i, inner(grads, value), inners)
    inners = inners.T

    def later(values):
        below, above = sides(values)
        return [jnp.where(direction < 0.5, a, b) for b, a in zip(below, above)]

    plane_after = later([t * inners[z : z + 1] for z, t in enumerate(plane_trans)])
    ahead = jnp.zeros((1, rays), f32)
    reach = jnp.zeros((1, rays), f32)
    for z in range(planes):
        ahead = jnp.where(own_plane == z, plane_trans[z], ahead)
        reach = jnp.where(own_plane == z, plane_after[z], reach)
    trans = [ahead * t for t in trans]
    after = later([t * inners[planes + p : planes + p + 1] for p, t in enumerate(trans)])
    for p in range(slots):
        reply[p, :6, :rays] = jnp.concatenate([*split3(trans[p]), *split3(after[p] + reach)], 0)
    for k, out_ref in enumerate(out_refs):
        out_ref[...] = as_message(grads, reply[own ^ k, :6, :rays])


def with_ones(value):
    return jnp.concatenate([value.T, jnp.ones((16, value.shape[0]), bf16)], 0)


def ready_body(*refs):
    enc_ref, mid_ref, head_ref, *refs = refs
    count = (len(refs) - 3) // 7
    sources = [refs[4 * n : 4 * n + 4] for n in range(count)]
    enc_turned, mid_turned, head_turned, *refs = refs[4 * count :]
    results = [refs[3 * n : 3 * n + 3] for n in range(count)]
    mid_turned[...] = mid_ref[...].T
    feat = sources[0][2].shape[2]
    head = head_ref[...].astype(f32)
    lane = lanes_of(head.shape)
    head_turned[...] = jnp.where(lane < feat, 2.0 * head, head).astype(bf16).T
    for k in range(enc_ref.shape[0]):
        enc_turned[k] = with_ones(enc_ref[k])
    for source, outs in zip(sources, results):
        one_ref, two_ref, turn_ref, scalar_ref = source
        one_turned, two_turned, slope_ref = outs
        samples, ray_count = scalar_ref.shape[2:]
        for i in range(one_ref.shape[0]):
            one_turned[i] = with_ones(one_ref[i])
            two_turned[i] = with_ones(two_ref[i])
            columns = turned(0.25 * scalar_ref[i, 0], ray_count)
            for j in range(samples):
                rows = slice(ray_count * j, ray_count * (j + 1))
                turn = turn_ref[i, rows, :]
                slope_ref[i, rows, :] = columns[:, j : j + 1] * (1.0 - turn * turn)


def product(left, right):
    return jnp.dot(left, right, preferred_element_type=f32)


def backward_body(*refs, slots, offset, before, last, group_count, shapes, vec_share, shards):
    begun = not before
    messages, refs = (refs[: len(slots)], refs[len(slots) :])
    one_ref, two_ref, turn_ref, scalar_ref, *refs = refs
    one_turned, two_turned, slope_ref, enc_turned, mid_turned, head_turned, *refs = refs
    if not begun:
        earlier, refs = (refs[:3], refs[3:])
    if last:
        depths, (depth_ref, *outs, shares) = (refs[: len(before)], refs[len(before) :])
    else:
        *outs, depth_ref = refs
    samples, ray_count = scalar_ref.shape[2:]
    hidden = one_ref.shape[2]
    feat = turn_ref.shape[2]
    lane = lanes_of((ray_count, LANES))
    if last:
        for ref, group in zip(depths, before):
            for i, k in enumerate(group):
                depth_ref[:, own_group(k, group_count, ray_count)] = ref[i : i + 1]
    sums = [0.0, 0.0, 0.0] if begun else [ref[...] for ref in earlier]
    grads, extras, spreads = ([], [], [])
    for i, k in enumerate(slots):
        parts, extra = from_message(messages[i][...], ray_count)
        grad = jnp.concatenate(parts, 1)
        grads.append(grad)
        extras.append(extra)
        grad_sum = jnp.sum(grad, 1, keepdims=True)
        spread = jnp.where(lane == samples, grad_sum, 0.0)
        for j in range(samples):
            rows = slice(ray_count * j, ray_count * (j + 1))
            value = jnp.sum(turn_ref[offset + i, rows, :] * grad, 1, keepdims=True)
            spread = jnp.where(lane == j, value, spread)
        spreads.append(spread.T)
    extra = side_by_side(extras)
    trans = extra[0:1] + extra[1:2] + extra[2:3]
    after = extra[3:4] + extra[4:5] + extra[5:6]
    for i, k in enumerate(slots):
        cut = slice(ray_count * i, ray_count * (i + 1))
        if last:
            depth_ref[:, own_group(k, group_count, ray_count)] = -after[:, cut]
        else:
            depth_ref[i : i + 1] = -after[:, cut]
    spread = side_by_side(spreads)
    sample_grad = 0.5 * (spread[:samples] + spread[samples : samples + 1])
    local_weight, trans_after, slope = [
        side_by_side([scalar_ref[offset + i, q] for i in range(len(slots))]) for q in range(3)
    ]
    weighted = local_weight * sample_grad
    later = [jnp.zeros_like(after)]
    for j in range(samples - 1, 0, -1):
        later.append(later[-1] + weighted[j : j + 1])
    later = jnp.concatenate(later[::-1], 0)
    optical_grad = trans * (trans_after * sample_grad - later) - after
    columns = turned(jnp.concatenate([optical_grad * slope, trans], 0), after.shape[1])
    zero = jnp.zeros((), bf16)
    for i, k in enumerate(slots):
        own = columns[ray_count * i : ray_count * (i + 1)]
        grad_ahead = grads[i] * own[:, samples : samples + 1]
        pieces = []
        for j in range(samples):
            rows = slice(ray_count * j, ray_count * (j + 1))
            colour_grad = (grad_ahead * slope_ref[offset + i, rows, :]).astype(bf16)
            density_part = jnp.where(lane == j, own, 0.0).astype(bf16)
            pieces.append(jnp.concatenate([colour_grad, density_part], 1))
        head_grad = jnp.concatenate(pieces, 0)
        second = product(head_grad, head_turned[...]).astype(bf16)
        second = jnp.where(two_ref[offset + i] > 0, second, zero)
        first = product(second, mid_turned[...]).astype(bf16)
        first = jnp.where(one_ref[offset + i] > 0, first, zero)
        sums[0] = sums[0] + product(enc_turned[k], first)
        sums[1] = sums[1] + product(one_turned[offset + i], second)
        sums[2] = sums[2] + product(two_turned[offset + i], head_grad)
    if not last:
        for value, ref in zip(sums, outs):
            ref[...] = value
        return
    values = [value[:-16] for value in sums]
    first_sum, second_sum, head_sum = [value[-16:-15] for value in sums]
    density_sum = jnp.sum(values[2][:, feat:].T, 0, keepdims=True)
    vec = jnp.concatenate([first_sum, second_sum, density_sum, head_sum[:, :feat]], 1)
    mine = lax.axis_index("rays")
    total = vec.shape[1]
    for s in range(shards):
        place = lax.rem(s + shards - mine, shards) if shards == 2 else s
        spot = 0
        for (rows, width), value in zip(shapes, values):
            for cut in blocks(width):
                shares[place, spot : spot + rows, :] = value[rows * s : rows * (s + 1), cut]
                spot += rows
        row = pltpu.roll(vec, total - vec_share * s, 1) if s else vec
        shares[place, spot : spot + 16, :] = row_block(row[:, : wide_rows(vec_share) * LANES], 16)
    if shards == 2:
        outs[0][...] = shares[0]
        outs[1][...] = shares[1]
    else:
        outs[0][...] = shares[...]


def adam_body(*refs, shards):
    grad_refs = refs[:shards]
    state_refs, out_refs = (refs[shards : shards + 4], refs[shards + 4 :])

    def update(stacked, gradient):
        first_moment = beta_one * stacked[1] + (1.0 - beta_one) * gradient
        second = beta_two * stacked[2] + (1.0 - beta_two) * gradient * gradient
        step = first_moment / first_fix / (jnp.sqrt(second / second_fix) + epsilon)
        return (stacked[0] - learn_rate * step, first_moment, second)

    def gathered(spot, rows):
        total = grad_refs[0][spot : spot + rows, :]
        for ref in grad_refs[1:]:
            total = total + ref[spot : spot + rows, :]
        return total

    spot = 0
    for ref, out in zip(state_refs[:3], out_refs[:3]):
        rows, width = ref.shape[2:]
        for cut in blocks(width):
            new = update([ref[i, 0, :, cut] for i in range(3)], gathered(spot, rows))
            spot += rows
            for i in range(3):
                out[i, 0, :, cut] = new[i]
    ref, out = (state_refs[3], out_refs[3])
    share = ref.shape[2]
    gradient = block_row(gathered(spot, 16), wide_rows(share))[:, :share]
    new = update([ref[i] for i in range(3)], gradient)
    for i in range(3):
        out[i] = new[i]


def shaped(shape, dtype):
    return jax.ShapeDtypeStruct(shape, dtype)


def swap(value, distance, size):
    return lax.ppermute(value, "region", [(i, i ^ distance) for i in range(size)])


def per_device(
    ray_codes,
    target,
    direction,
    entries,
    exits,
    depth_bins,
    in_layer,
    mid_layer,
    feat_layer,
    vectors,
):
    regions = lax.axis_size("region")
    shards = lax.axis_size("rays")
    samples, ray_count = depth_bins.shape[1:]
    quad = min(QUAD, regions)
    planes = regions // quad
    rays = ray_count // quad
    layers = (in_layer, mid_layer, feat_layer)
    states = (*layers, vectors)
    shapes = tuple(layer.shape[2:] for layer in layers)
    vec_share = vectors.shape[2]
    hidden = shapes[0][1]
    feat = shapes[2][1]
    code_width = ray_codes.shape[2]
    pack_rows = sum(rows * (width // LANES) for rows, width in shapes) + 16
    rows = samples * rays
    sizes = dict(shapes=shapes, vec_share=vec_share)
    pair = shards == 2
    flops = 2 * rows * (code_width * hidden + hidden * hidden + hidden * (feat + LANES))

    arguments = (*states, ray_codes, depth_bins, entries, exits, direction[None], target)
    pack, *geometric, own_target = call(
        functools.partial(fetch_body, slots=quad),
        (pltpu.VMEM((pack_rows, LANES), bf16),)
        + tuple(pltpu.VMEM(a.shape, a.dtype) for a in arguments[4:9])
        + (pltpu.VMEM((rays, feat), bf16),),
        [in_hbm(a) for a in arguments],
        16,
        scratch=[pltpu.VMEM(a.shape[1:], f32) for a in states]
        + [pltpu.SemaphoreType.DMA((10,))],
        specs=[pl.BlockSpec(memory_space=pltpu.HBM)] * 10,
    )
    if pair:
        packs = (pack, lax.ppermute(pack, "rays", [(0, 1), (1, 0)]))
    else:
        packs = (lax.all_gather(pack, "rays", axis=0),)
    encoded, geometry = call(
        functools.partial(encode_body, unit_length=depth_scale / (regions * BINS), slots=quad),
        (
            pltpu.VMEM((quad, rows, code_width), bf16),
            pltpu.VMEM((quad, samples + 8, rays), f32),
        ),
        [in_vmem(v) for v in geometric],
        16,
        scratch=[
            pltpu.VMEM((samples + 8, ray_count), f32),
            pltpu.VMEM((ray_count, LANES), f32),
        ],
        flops=10 * quad * rows * code_width,
        moved=quad * rows * code_width * 4,
    )

    message = pltpu.VMEM((rays * (feat // LANES) + 8, LANES), bf16)

    def kept_shapes(count):
        return (
            pltpu.VMEM((count, rows, hidden), bf16),
            pltpu.VMEM((count, rows, hidden), bf16),
            pltpu.VMEM((count, rows, feat), f32),
            pltpu.VMEM((count, 3, samples, rays), f32),
        )

    def moved(count):
        return count * rows * (feat + hidden) * 4

    weight_shapes = (
        pltpu.VMEM((shapes[0][0] * shards, hidden), bf16),
        pltpu.VMEM((hidden, hidden), bf16),
        pltpu.VMEM((hidden, feat + LANES), bf16),
        pltpu.VMEM((1, vec_share * shards), f32),
    )

    def forward(slots, inputs, first):
        if first:
            body = functools.partial(forward_first_body, pair=pair, slots=slots, **sizes)
        else:
            body = functools.partial(forward_rest_body, slots=slots)
        out = call(
            body,
            (weight_shapes if first else ())
            + kept_shapes(len(slots))
            + (message,) * len(slots),
            [in_vmem(v) for v in (*inputs, encoded, geometry)],
            16,
            scratch=[pltpu.VMEM((2, pack_rows, LANES), bf16)] if first and pair else (),
            flops=len(slots) * flops,
            moved=moved(len(slots)),
        )
        found, out = (out[:4], out[4:]) if first else (None, out)
        return (out[:4], list(out[4:]), found)

    groups = [tuple(range(1, quad)), (0,)]
    kept, sent, weights = ([], {}, None)
    for slots in groups:
        arrays, messages, found = forward(slots, packs if not kept else weights, not kept)
        weights = weights or found
        kept.append(arrays)
        for k, value in zip(slots, messages):
            sent[k] = swap(value, k, regions) if k else value
    quad_messages = [in_vmem(sent[k]) for k in range(quad)]
    store = pltpu.VMEM((quad, *message.shape), bf16)
    plane_store = pltpu.VMEM((planes, *message.shape), bf16)
    plane_message = call(
        functools.partial(plane_body, rays=rays), message, quad_messages, 16, scratch=[store]
    )
    plane_messages = [plane_message] + [
        swap(plane_message, quad * k, regions) for k in range(1, planes)
    ]
    def ready_shapes(count):
        return (
            pltpu.VMEM((count, hidden + 16, rows), bf16),
            pltpu.VMEM((count, hidden + 16, rows), bf16),
            pltpu.VMEM((count, rows, feat), f32),
        )

    enc_turned, *results = call(
        ready_body,
        (
            pltpu.VMEM((quad, code_width + 16, rows), bf16),
            pltpu.VMEM((hidden, hidden), bf16),
            pltpu.VMEM((feat + LANES, hidden), bf16),
        )
        + sum((ready_shapes(len(slots)) for slots in groups), ()),
        [in_vmem(v) for v in (encoded, weights[1], weights[2], *sum(map(list, kept), []))],
        16,
        flops=quad * flops,
        moved=2 * moved(quad),
    )
    turned_weights, results = (results[:2], results[2:])
    ready = [results[3 * n : 3 * n + 3] for n in range(len(groups))]
    replies = call(
        functools.partial(owner_body, slots=quad, planes=planes),
        (message,) * quad,
        quad_messages + [in_vmem(v) for v in (*plane_messages, own_target, turned_weights[0])],
        16,
        scratch=[store, plane_store, pltpu.VMEM((quad, 8, LANES), f32)],
    )
    answers = [replies[0]] + [swap(replies[k], k, regions) for k in range(1, quad)]
    gradient_shapes = (
        pltpu.VMEM((code_width + 16, hidden), f32),
        pltpu.VMEM((hidden + 16, hidden), f32),
        pltpu.VMEM((hidden + 16, feat + LANES), f32),
    )
    earlier, depths, before = ((), [], ())
    steps = [(1, (0,), 0), (0, (1,), 0), (0, tuple(range(2, quad)), 1)]
    for n, slots, offset in steps:
        last = slots == steps[-1][1]
        if last:
            share = pltpu.VMEM((pack_rows, LANES), f32)
            out_shape = (shaped((1, ray_count), f32), share, share)
            if not pair:
                out_shape = (out_shape[0], shaped((shards, pack_rows, LANES), f32))
        else:
            out_shape = gradient_shapes + (pltpu.VMEM((len(slots), rays), f32),)
        inputs = [answers[k] for k in slots] + [*kept[n], *ready[n], enc_turned, *turned_weights]
        inputs += [*earlier] + (depths if last else [])
        out = call(
            functools.partial(
                backward_body,
                slots=slots,
                offset=offset,
                before=before,
                last=last,
                group_count=quad,
                shards=shards,
                **sizes,
            ),
            out_shape,
            [in_vmem(v) for v in inputs],
            24,
            scratch=[pltpu.VMEM((shards, pack_rows, LANES), f32)] if last else (),
            flops=2 * len(slots) * flops,
            moved=moved(len(slots)),
        )
        earlier, before = (out[:3], before + (slots,))
        if not last:
            depths.append(out[3])
    depth_grad, *grads = out
    if pair:
        parts = (grads[0], lax.ppermute(grads[1], "rays", [(0, 1), (1, 0)]))
    else:
        exchanged = lax.all_to_all(grads[0], "rays", 0, 0)
        parts = tuple(exchanged[s] for s in range(shards))
    new = call(
        functools.partial(adam_body, shards=shards),
        tuple(shaped(s.shape, f32) for s in states),
        (*parts, *states),
        16,
    )
    return (*new, depth_grad)


def solution(mesh):
    placed = (
        P(None, "rays", None),
        P("rays", None),
        P("rays"),
        P("region", "rays"),
        P("region", "rays"),
        P("region", None, "rays"),
        P(None, "region", "rays", None),
        P(None, "region", "rays", None),
        P(None, "region", "rays", None),
        P(None, "region", "rays"),
    )
    return jax.shard_map(
        per_device,
        mesh=mesh,
        in_specs=placed,
        out_specs=(
            P(None, "region", "rays", None),
            P(None, "region", "rays", None),
            P(None, "region", "rays", None),
            P(None, "region", "rays"),
            P("region", "rays"),
        ),
        check_vma=False,
    )
```

```python
import functools

import jax
import jax.numpy as jnp
from jax import lax
from jax.experimental import pallas as pl
from jax.experimental.pallas import tpu as pltpu
from jax.sharding import PartitionSpec as P

BINS = 64
LANES = 128
QUAD = 4

depth_scale = 4.0
beta_one = 0.9
beta_two = 0.999
learn_rate = 0.001
epsilon = 1e-08
first_fix = 1.0 - 0.9**10
second_fix = 1.0 - 0.999**10

f32 = jnp.float32
bf16 = jnp.bfloat16


def in_vmem(value):
    return pltpu.with_memory_space_constraint(value, pltpu.VMEM)


def in_hbm(value):
    return pltpu.with_memory_space_constraint(value, pltpu.HBM)


def call(body, out_shape, inputs, limit, scratch=(), specs=None, flops=1000000, moved=1000000):
    many = isinstance(out_shape, (tuple, list))
    spec = pl.BlockSpec(memory_space=pltpu.VMEM)
    return pl.pallas_call(
        body,
        out_shape=out_shape,
        in_specs=specs or [spec] * len(inputs),
        out_specs=tuple(spec for _ in out_shape) if many else spec,
        scratch_shapes=list(scratch),
        compiler_params=pltpu.CompilerParams(vmem_limit_bytes=limit * 1024 * 1024),
        cost_estimate=pl.CostEstimate(flops=flops, bytes_accessed=moved, transcendentals=0),
    )(*inputs)


def blocks(width):
    return [slice(LANES * k, LANES * (k + 1)) for k in range(width // LANES)]


def wide_rows(count):
    return -(-count // LANES)


def row_block(row, rows):
    width = row.shape[1]
    padded = wide_rows(width) * LANES
    if padded != width:
        row = jnp.concatenate([row, jnp.zeros((1, padded - width), f32)], 1)
    place = lax.broadcasted_iota(jnp.int32, (rows, LANES), 0)
    out = jnp.zeros((rows, LANES), f32)
    for k, cut in enumerate(blocks(padded)):
        out = jnp.where(place == k, jnp.broadcast_to(row[:, cut], (rows, LANES)), out)
    return out


def block_row(block, count):
    return jnp.concatenate([block[k : k + 1] for k in range(count)], 1)


def split3(value):
    high = value.astype(bf16).astype(f32)
    rest = value - high
    mid = rest.astype(bf16).astype(f32)
    return (high, mid, rest - mid)


def lanes_of(shape):
    return lax.broadcasted_iota(jnp.int32, shape, 1)


def turned(rows, ray_count):
    fill = LANES - rows.shape[0]
    return jnp.concatenate([rows, jnp.zeros((fill, ray_count), f32)], 0).T


def own_group(k, slots, rows):
    place = lax.rem(lax.axis_index("region"), slots) ^ k
    return pl.ds(pl.multiple_of(place * rows, rows), rows)


def fetch_body(*refs, slots):
    ins, (pack_ref, *refs) = (refs[:10], refs[10:])
    outs, held, sems = (refs[:6], refs[6:10], refs[10])
    target_ref = outs[5]
    copies = []

    def fetch(source, place):
        copies.append(pltpu.make_async_copy(source, place, sems.at[len(copies)]))
        copies[-1].start()

    for ref, hold in zip(ins[:4], held):
        fetch(ref.at[0], hold)
    for ref, out in zip(ins[4:9], outs):
        fetch(ref, out)
    fetch(ins[9].at[own_group(0, slots, target_ref.shape[0])], target_ref)
    spot = 0
    for copy, hold in zip(copies[:3], held[:3]):
        copy.wait()
        rows, width = hold.shape[1:]
        for cut in blocks(width):
            pack_ref[spot : spot + rows, :] = hold[0, :, cut].astype(bf16)
            spot += rows
    copies[3].wait()
    pack_ref[spot : spot + 16, :] = row_block(held[3][...], 16).astype(bf16)
    for copy in copies[4:]:
        copy.wait()


def encode_body(*refs, unit_length, slots):
    codes, bins, entry, exit_, direction, enc_ref, geometry_ref, *refs = refs
    flat_geometry, flat_position = refs
    bins = bins[0].astype(f32)
    samples, ray_count = bins.shape
    group_rows = ray_count // slots
    slot = lax.broadcasted_iota(jnp.int32, bins.shape, 0)
    following = jnp.where(slot == samples - 1, float(BINS), pltpu.roll(bins, samples - 1, 0))
    inside = ((slot >= entry[...]) & (slot < exit_[...])).astype(f32)
    flat_geometry[:samples] = (following - bins) * unit_length * inside
    flat_geometry[samples : samples + 1] = direction[...].astype(f32)
    flat_position[...] = turned((bins + 0.5) / BINS, ray_count)
    for k in range(slots):
        group = own_group(k, slots, group_rows)
        geometry_ref[k] = flat_geometry[:, group]
        code_zero = codes[0, group].astype(f32)
        code_one = codes[1, group].astype(f32)
        position = flat_position[group, :]
        for j in range(samples):
            encoded = code_zero + position[:, j : j + 1] * code_one
            enc_ref[k, group_rows * j : group_rows * (j + 1), :] = encoded.astype(bf16)


def assemble(packs, shapes, vec_share):
    shards = len(packs)
    spot = 0
    mats = []
    for rows, width in shapes:
        pieces = []
        for cut in blocks(width):
            pieces.append(jnp.concatenate([p[spot : spot + rows, :] for p in packs], 0))
            spot += rows
        mats.append(jnp.concatenate(pieces, 1))
    vec_total = vec_share * shards
    vec = jnp.zeros((1, vec_total), f32)
    for s, p in enumerate(packs):
        block = p[spot : spot + 16, :].astype(f32)
        count = wide_rows(vec_share)
        row = block_row(block, count)
        fill = vec_total - count * LANES
        if fill:
            row = jnp.concatenate([row, jnp.zeros((1, fill), f32)], 1)
        if s:
            row = pltpu.roll(row, vec_share * s, 1)
        vec = vec + row
    return (*mats, vec)


def product(left, right):
    return jnp.dot(left, right, preferred_element_type=f32)


def forward_slots(slots, weights, enc_ref, geometry_ref, message_refs, kept):
    in_weight, mid_ref, head_ref, vec = weights
    one_ref, two_ref, turn_ref, scalar_ref = kept
    samples, ray_count = scalar_ref.shape[2:]
    hidden = mid_ref.shape[0]
    feat = turn_ref.shape[2]
    bias_one = vec[:, :hidden]
    bias_two = vec[:, hidden : 2 * hidden]
    half_bias = 0.5 * vec[:, 3 * hidden :]
    lane = lanes_of((ray_count, LANES))
    ones, twos, densities = ([], [], [])
    for i, k in enumerate(slots):
        one = product(enc_ref[k], in_weight) + bias_one
        ones.append(jnp.maximum(one, 0.0).astype(bf16))
        one_ref[i] = ones[i]
    for i in range(len(slots)):
        two = product(ones[i], mid_ref[...]) + bias_two
        twos.append(jnp.maximum(two, 0.0).astype(bf16))
        two_ref[i] = twos[i]
    raws = [product(two, head_ref[:, feat:]) for two in twos]
    for raw in raws:
        density = jnp.zeros((ray_count, LANES), f32)
        for j in range(samples):
            rows = slice(ray_count * j, ray_count * (j + 1))
            density = jnp.where(lane == j, raw[rows], density)
        densities.append(density)
    for i in range(len(slots)):
        turn_ref[i] = jnp.tanh(product(twos[i], head_ref[:, :feat]) + half_bias)
    density = side_by_side([value.T[:samples] for value in densities])
    geometry = side_by_side([geometry_ref[k, :samples] for k in slots])
    direction = side_by_side([geometry_ref[k, samples : samples + 1] for k in slots])
    soft = jnp.maximum(density, 0.0) + jnp.log1p(jnp.exp(-jnp.abs(density)))
    optical = soft * geometry
    before = [jnp.zeros_like(direction)]
    for j in range(samples):
        before.append(before[-1] + optical[j : j + 1])
    depth = before.pop()
    optical_before = jnp.concatenate(before, 0)
    opacity = jnp.tanh(0.5 * optical) * (1.0 + jnp.exp(-optical))
    local_weight = jnp.exp(-optical_before) * opacity
    half_weight = 0.5 * local_weight
    half_sum = jnp.sum(half_weight, 0, keepdims=True)
    columns = turned(jnp.concatenate([half_weight, half_sum], 0), depth.shape[1])
    shared = jnp.concatenate([*split3(depth), direction], 0)
    sig = 0.5 * jnp.tanh(0.5 * density) + 0.5
    scalars = (local_weight, jnp.exp(-(optical_before + optical)), geometry * sig)
    for i, k in enumerate(slots):
        cut = slice(ray_count * i, ray_count * (i + 1))
        for q, value in enumerate(scalars):
            scalar_ref[i, q] = value[:, cut]
        own = columns[cut]
        total = jnp.zeros((ray_count, feat), f32) + own[:, samples : samples + 1]
        for j in range(samples):
            rows = slice(ray_count * j, ray_count * (j + 1))
            total = total + own[:, j : j + 1] * turn_ref[i, rows, :]
        message_refs[i][...] = as_message([total[:, k] for k in blocks(feat)], shared[:, cut])


def side_by_side(values):
    return jnp.concatenate(values, 1) if len(values) > 1 else values[0]


def as_message(parts, rows):
    count, rays = rows.shape
    if count < 8:
        rows = jnp.concatenate([rows, jnp.zeros((8 - count, rays), f32)], 0)
    if rays < LANES:
        rows = jnp.concatenate([rows, jnp.zeros((8, LANES - rays), f32)], 1)
    return jnp.concatenate([*parts, rows], 0).astype(bf16)


def from_message(value, rays):
    value = value.astype(f32)
    count = value.shape[0] // rays
    parts = [value[rays * k : rays * (k + 1)] for k in range(count)]
    return (parts, value[rays * count :, :rays])


def forward_first_body(*refs, shapes, vec_share, pair, slots):
    both = None
    if pair:
        own_ref, other_ref, *refs, both = refs
        mine = lax.axis_index("rays")
        both[mine] = own_ref[...]
        both[1 - mine] = other_ref[...]
        packs = [both.at[0], both.at[1]]
    else:
        packs_ref, *refs = refs
        packs = [packs_ref.at[s] for s in range(packs_ref.shape[0])]
    enc_ref, geometry_ref, in_ref, mid_ref, head_ref, vec_ref, *refs = refs
    hidden = mid_ref.shape[0]
    in_weight, mid_weight, feat_weight, vec = assemble(packs, shapes, vec_share)
    density_row = vec[:, 2 * hidden : 3 * hidden]
    density_cols = jnp.broadcast_to(density_row, (LANES, hidden)).T
    in_ref[...] = in_weight
    mid_ref[...] = mid_weight
    half_weight = (0.5 * feat_weight.astype(f32)).astype(bf16)
    head_ref[...] = jnp.concatenate([half_weight, density_cols.astype(bf16)], 1)
    vec_ref[...] = vec
    weights = (in_weight, mid_ref, head_ref, vec)
    forward_slots(slots, weights, enc_ref, geometry_ref, refs[4:], refs[:4])


def forward_rest_body(in_ref, mid_ref, head_ref, vec_ref, enc_ref, geometry_ref, *refs, slots):
    weights = (in_ref[...], mid_ref, head_ref, vec_ref[...])
    forward_slots(slots, weights, enc_ref, geometry_ref, refs[4:], refs[:4])


def sides(values):
    below, above = ([jnp.zeros_like(values[0])], [jnp.zeros_like(values[0])])
    for q in range(len(values) - 1):
        below.append(below[-1] + values[q])
        above.append(above[-1] + values[len(values) - 1 - q])
    return (below, above[::-1])


def gather_messages(refs, store, own, rays):
    for k, ref in enumerate(refs):
        store[own ^ k] = ref[...]
    members = [from_message(store[p], rays) for p in range(len(refs))]
    parts = [m[0] for m in members]
    depth = [m[1][0:1] + m[1][1:2] + m[1][2:3] for m in members]
    direction = members[0][1][3:4]
    below, above = sides(depth)
    trans = [jnp.exp(-jnp.where(direction < 0.5, b, a)) for b, a in zip(below, above)]
    return (parts, depth, direction, trans)


def as_columns(rows):
    columns = turned(jnp.concatenate(rows, 0), rows[0].shape[1])
    return [columns[:, i : i + 1] for i in range(len(rows))]


def weighted_sum(factors, parts):
    out = []
    for k in range(len(parts[0])):
        total = factors[0] * parts[0][k]
        for factor, part in zip(factors[1:], parts[1:]):
            total = total + factor * part[k]
        out.append(total)
    return out


def inner(left, right):
    total = left[0] * right[0]
    for a, b in zip(left[1:], right[1:]):
        total = total + a * b
    return jnp.sum(total, 1, keepdims=True)


def plane_body(*refs, rays):
    *messages, out_ref, store = refs
    own = lax.rem(lax.axis_index("region"), len(messages))
    parts, depth, direction, trans = gather_messages(messages, store, own, rays)
    total = depth[0]
    for value in depth[1:]:
        total = total + value
    rows = jnp.concatenate([*split3(total), direction], 0)
    out_ref[...] = as_message(weighted_sum(as_columns(trans), parts), rows)


def owner_body(*refs, slots, planes):
    quad_refs, plane_refs = (refs[:slots], refs[slots : slots + planes])
    target_ref, _, *out_refs, quad_store, plane_store, reply = refs[slots + planes :]
    rays, feat = target_ref.shape
    region = lax.axis_index("region")
    own, own_plane = (lax.rem(region, slots), lax.div(region, slots))
    parts, _, direction, trans = gather_messages(quad_refs, quad_store, own, rays)
    plane_parts, _, _, plane_trans = gather_messages(plane_refs, plane_store, own_plane, rays)
    rendered = weighted_sum(as_columns(plane_trans), plane_parts)
    grads = [
        (value - target_ref[:, cut].astype(f32)).astype(bf16).astype(f32)
        for value, cut in zip(rendered, blocks(feat))
    ]
    lane = lanes_of((rays, LANES))
    inners = jnp.zeros((rays, LANES), f32)
    for i, value in enumerate((*plane_parts, *parts)):
        inners = jnp.where(lane == i, inner(grads, value), inners)
    inners = inners.T

    def later(values):
        below, above = sides(values)
        return [jnp.where(direction < 0.5, a, b) for b, a in zip(below, above)]

    plane_after = later([t * inners[z : z + 1] for z, t in enumerate(plane_trans)])
    ahead = jnp.zeros((1, rays), f32)
    reach = jnp.zeros((1, rays), f32)
    for z in range(planes):
        ahead = jnp.where(own_plane == z, plane_trans[z], ahead)
        reach = jnp.where(own_plane == z, plane_after[z], reach)
    trans = [ahead * t for t in trans]
    after = later([t * inners[planes + p : planes + p + 1] for p, t in enumerate(trans)])
    for p in range(slots):
        reply[p, :6, :rays] = jnp.concatenate([*split3(trans[p]), *split3(after[p] + reach)], 0)
    for k, out_ref in enumerate(out_refs):
        out_ref[...] = as_message(grads, reply[own ^ k, :6, :rays])


def with_ones(value):
    return jnp.concatenate([value.T, jnp.ones((16, value.shape[0]), bf16)], 0)


def ready_body(*refs):
    *refs, sems = refs
    states, (enc_ref, mid_ref, head_ref, *refs) = (refs[:4], refs[4:])
    count = (len(refs) - 7) // 7
    sources = [refs[4 * n : 4 * n + 4] for n in range(count)]
    fetched, refs = (refs[4 * count : 4 * count + 4], refs[4 * count + 4 :])
    enc_turned, mid_turned, head_turned, *refs = refs
    results = [refs[3 * n : 3 * n + 3] for n in range(count)]
    copies = []
    for n, (source, place) in enumerate(zip(states, fetched)):
        copies.append(pltpu.make_async_copy(source, place, sems.at[n]))
        copies[-1].start()
    mid_turned[...] = mid_ref[...].T
    feat = sources[0][2].shape[2]
    head = head_ref[...].astype(f32)
    lane = lanes_of(head.shape)
    head_turned[...] = jnp.where(lane < feat, 2.0 * head, head).astype(bf16).T
    for k in range(enc_ref.shape[0]):
        enc_turned[k] = with_ones(enc_ref[k])
    for source, outs in zip(sources, results):
        one_ref, two_ref, turn_ref, scalar_ref = source
        one_turned, two_turned, slope_ref = outs
        samples, ray_count = scalar_ref.shape[2:]
        for i in range(one_ref.shape[0]):
            one_turned[i] = with_ones(one_ref[i])
            two_turned[i] = with_ones(two_ref[i])
            columns = turned(0.25 * scalar_ref[i, 0], ray_count)
            for j in range(samples):
                rows = slice(ray_count * j, ray_count * (j + 1))
                turn = turn_ref[i, rows, :]
                slope_ref[i, rows, :] = columns[:, j : j + 1] * (1.0 - turn * turn)
    for copy in copies:
        copy.wait()


def backward_body(*refs, slots, offset, before, last, group_count, shapes, vec_share, shards):
    begun = not before
    messages, refs = (refs[: len(slots)], refs[len(slots) :])
    one_ref, two_ref, turn_ref, scalar_ref, *refs = refs
    one_turned, two_turned, slope_ref, enc_turned, mid_turned, head_turned, *refs = refs
    if not begun:
        earlier, refs = (refs[:3], refs[3:])
    if last:
        depths, (depth_ref, *outs, shares) = (refs[: len(before)], refs[len(before) :])
    else:
        *outs, depth_ref = refs
    samples, ray_count = scalar_ref.shape[2:]
    hidden = one_ref.shape[2]
    feat = turn_ref.shape[2]
    lane = lanes_of((ray_count, LANES))
    if last:
        for ref, group in zip(depths, before):
            for i, k in enumerate(group):
                depth_ref[:, own_group(k, group_count, ray_count)] = ref[i : i + 1]
    sums = [0.0, 0.0, 0.0] if begun else [ref[...] for ref in earlier]
    grads, extras, spreads = ([], [], [])
    for i, k in enumerate(slots):
        parts, extra = from_message(messages[i][...], ray_count)
        grad = jnp.concatenate(parts, 1)
        grads.append(grad)
        extras.append(extra)
        grad_sum = jnp.sum(grad, 1, keepdims=True)
        spread = jnp.where(lane == samples, grad_sum, 0.0)
        for j in range(samples):
            rows = slice(ray_count * j, ray_count * (j + 1))
            value = jnp.sum(turn_ref[offset + i, rows, :] * grad, 1, keepdims=True)
            spread = jnp.where(lane == j, value, spread)
        spreads.append(spread.T)
    extra = side_by_side(extras)
    trans = extra[0:1] + extra[1:2] + extra[2:3]
    after = extra[3:4] + extra[4:5] + extra[5:6]
    for i, k in enumerate(slots):
        cut = slice(ray_count * i, ray_count * (i + 1))
        if last:
            depth_ref[:, own_group(k, group_count, ray_count)] = -after[:, cut]
        else:
            depth_ref[i : i + 1] = -after[:, cut]
    spread = side_by_side(spreads)
    sample_grad = 0.5 * (spread[:samples] + spread[samples : samples + 1])
    local_weight, trans_after, slope = [
        side_by_side([scalar_ref[offset + i, q] for i in range(len(slots))]) for q in range(3)
    ]
    weighted = local_weight * sample_grad
    later = [jnp.zeros_like(after)]
    for j in range(samples - 1, 0, -1):
        later.append(later[-1] + weighted[j : j + 1])
    later = jnp.concatenate(later[::-1], 0)
    optical_grad = trans * (trans_after * sample_grad - later) - after
    columns = turned(jnp.concatenate([optical_grad * slope, trans], 0), after.shape[1])
    zero = jnp.zeros((), bf16)
    for i, k in enumerate(slots):
        own = columns[ray_count * i : ray_count * (i + 1)]
        grad_ahead = grads[i] * own[:, samples : samples + 1]
        pieces = []
        for j in range(samples):
            rows = slice(ray_count * j, ray_count * (j + 1))
            colour_grad = (grad_ahead * slope_ref[offset + i, rows, :]).astype(bf16)
            density_part = jnp.where(lane == j, own, 0.0).astype(bf16)
            pieces.append(jnp.concatenate([colour_grad, density_part], 1))
        head_grad = jnp.concatenate(pieces, 0)
        second = product(head_grad, head_turned[...]).astype(bf16)
        sums[2] = sums[2] + product(two_turned[offset + i], head_grad)
        second = jnp.where(two_ref[offset + i] > 0, second, zero)
        first = product(second, mid_turned[...]).astype(bf16)
        sums[1] = sums[1] + product(one_turned[offset + i], second)
        first = jnp.where(one_ref[offset + i] > 0, first, zero)
        sums[0] = sums[0] + product(enc_turned[k], first)
    if not last:
        for value, ref in zip(sums, outs):
            ref[...] = value
        return
    values = [value[:-16] for value in sums]
    first_sum, second_sum, head_sum = [value[-16:-15] for value in sums]
    density_sum = jnp.sum(values[2][:, feat:].T, 0, keepdims=True)
    vec = jnp.concatenate([first_sum, second_sum, density_sum, head_sum[:, :feat]], 1)
    mine = lax.axis_index("rays")
    total = vec.shape[1]
    for s in range(shards):
        place = lax.rem(s + shards - mine, shards) if shards == 2 else s
        spot = 0
        for (rows, width), value in zip(shapes, values):
            for cut in blocks(width):
                shares[place, spot : spot + rows, :] = value[rows * s : rows * (s + 1), cut]
                spot += rows
        row = pltpu.roll(vec, total - vec_share * s, 1) if s else vec
        shares[place, spot : spot + 16, :] = row_block(row[:, : wide_rows(vec_share) * LANES], 16)
    if shards == 2:
        outs[0][...] = shares[0]
        outs[1][...] = shares[1]
    else:
        outs[0][...] = shares[...]


def adam_body(*refs, shards):
    grad_refs, (depth_ref, *refs) = (refs[:shards], refs[shards:])
    state_refs, out_refs, depth_out = (refs[:4], refs[4:8], refs[8])
    depth_out[...] = depth_ref[...]

    def update(stacked, gradient):
        first_moment = beta_one * stacked[1] + (1.0 - beta_one) * gradient
        second = beta_two * stacked[2] + (1.0 - beta_two) * gradient * gradient
        step = first_moment / first_fix / (jnp.sqrt(second / second_fix) + epsilon)
        return (stacked[0] - learn_rate * step, first_moment, second)

    def gathered(spot, rows):
        total = grad_refs[0][spot : spot + rows, :]
        for ref in grad_refs[1:]:
            total = total + ref[spot : spot + rows, :]
        return total

    spot = 0
    for ref, out in zip(state_refs[:3], out_refs[:3]):
        rows, width = ref.shape[2:]
        for cut in blocks(width):
            new = update([ref[i, 0, :, cut] for i in range(3)], gathered(spot, rows))
            spot += rows
            for i in range(3):
                out[i, 0, :, cut] = new[i]
    ref, out = (state_refs[3], out_refs[3])
    share = ref.shape[2]
    gradient = block_row(gathered(spot, 16), wide_rows(share))[:, :share]
    new = update([ref[i] for i in range(3)], gradient)
    for i in range(3):
        out[i] = new[i]


def shaped(shape, dtype):
    return jax.ShapeDtypeStruct(shape, dtype)


def swap(value, distance, size):
    return lax.ppermute(value, "region", [(i, i ^ distance) for i in range(size)])


def per_device(
    ray_codes,
    target,
    direction,
    entries,
    exits,
    depth_bins,
    in_layer,
    mid_layer,
    feat_layer,
    vectors,
):
    regions = lax.axis_size("region")
    shards = lax.axis_size("rays")
    samples, ray_count = depth_bins.shape[1:]
    quad = min(QUAD, regions)
    planes = regions // quad
    rays = ray_count // quad
    layers = (in_layer, mid_layer, feat_layer)
    states = (*layers, vectors)
    shapes = tuple(layer.shape[2:] for layer in layers)
    vec_share = vectors.shape[2]
    hidden = shapes[0][1]
    feat = shapes[2][1]
    code_width = ray_codes.shape[2]
    pack_rows = sum(rows * (width // LANES) for rows, width in shapes) + 16
    rows = samples * rays
    sizes = dict(shapes=shapes, vec_share=vec_share)
    pair = shards == 2
    flops = 2 * rows * (code_width * hidden + hidden * hidden + hidden * (feat + LANES))

    arguments = (*states, ray_codes, depth_bins, entries, exits, direction[None], target)
    pack, *geometric, own_target = call(
        functools.partial(fetch_body, slots=quad),
        (pltpu.VMEM((pack_rows, LANES), bf16),)
        + tuple(pltpu.VMEM(a.shape, a.dtype) for a in arguments[4:9])
        + (pltpu.VMEM((rays, feat), bf16),),
        [in_hbm(a) for a in arguments],
        16,
        scratch=[pltpu.VMEM(a.shape[1:], f32) for a in states]
        + [pltpu.SemaphoreType.DMA((10,))],
        specs=[pl.BlockSpec(memory_space=pltpu.HBM)] * 10,
    )
    if pair:
        packs = (pack, lax.ppermute(pack, "rays", [(0, 1), (1, 0)]))
    else:
        packs = (lax.all_gather(pack, "rays", axis=0),)
    encoded, geometry = call(
        functools.partial(encode_body, unit_length=depth_scale / (regions * BINS), slots=quad),
        (
            pltpu.VMEM((quad, rows, code_width), bf16),
            pltpu.VMEM((quad, samples + 8, rays), f32),
        ),
        [in_vmem(v) for v in geometric],
        16,
        scratch=[
            pltpu.VMEM((samples + 8, ray_count), f32),
            pltpu.VMEM((ray_count, LANES), f32),
        ],
        flops=10 * quad * rows * code_width,
        moved=quad * rows * code_width * 4,
    )

    message = pltpu.VMEM((rays * (feat // LANES) + 8, LANES), bf16)

    def kept_shapes(count):
        return (
            pltpu.VMEM((count, rows, hidden), bf16),
            pltpu.VMEM((count, rows, hidden), bf16),
            pltpu.VMEM((count, rows, feat), f32),
            pltpu.VMEM((count, 3, samples, rays), f32),
        )

    def moved(count):
        return count * rows * (feat + hidden) * 4

    weight_shapes = (
        pltpu.VMEM((shapes[0][0] * shards, hidden), bf16),
        pltpu.VMEM((hidden, hidden), bf16),
        pltpu.VMEM((hidden, feat + LANES), bf16),
        pltpu.VMEM((1, vec_share * shards), f32),
    )

    def forward(slots, inputs, first):
        if first:
            body = functools.partial(forward_first_body, pair=pair, slots=slots, **sizes)
        else:
            body = functools.partial(forward_rest_body, slots=slots)
        out = call(
            body,
            (weight_shapes if first else ())
            + kept_shapes(len(slots))
            + (message,) * len(slots),
            [in_vmem(v) for v in (*inputs, encoded, geometry)],
            16,
            scratch=[pltpu.VMEM((2, pack_rows, LANES), bf16)] if first and pair else (),
            flops=len(slots) * flops,
            moved=moved(len(slots)),
        )
        found, out = (out[:4], out[4:]) if first else (None, out)
        return (out[:4], list(out[4:]), found)

    groups = [tuple(range(1, quad)), (0,)]
    kept, sent, weights = ([], {}, None)
    for slots in groups:
        arrays, messages, found = forward(slots, packs if not kept else weights, not kept)
        weights = weights or found
        kept.append(arrays)
        for k, value in zip(slots, messages):
            sent[k] = swap(value, k, regions) if k else value
    quad_messages = [in_vmem(sent[k]) for k in range(quad)]
    store = pltpu.VMEM((quad, *message.shape), bf16)
    plane_store = pltpu.VMEM((planes, *message.shape), bf16)
    plane_message = call(
        functools.partial(plane_body, rays=rays), message, quad_messages, 16, scratch=[store]
    )
    plane_messages = [plane_message] + [
        swap(plane_message, quad * k, regions) for k in range(1, planes)
    ]
    def ready_shapes(count):
        return (
            pltpu.VMEM((count, hidden + 16, rows), bf16),
            pltpu.VMEM((count, hidden + 16, rows), bf16),
            pltpu.VMEM((count, rows, feat), f32),
        )

    hbm, vmem = (pl.BlockSpec(memory_space=m) for m in (pltpu.HBM, pltpu.VMEM))
    local = [encoded, weights[1], weights[2], *sum(map(list, kept), [])]
    results = call(
        ready_body,
        tuple(pltpu.VMEM(s.shape, f32) for s in states)
        + (
            pltpu.VMEM((quad, code_width + 16, rows), bf16),
            pltpu.VMEM((hidden, hidden), bf16),
            pltpu.VMEM((feat + LANES, hidden), bf16),
        )
        + sum((ready_shapes(len(slots)) for slots in groups), ()),
        [in_hbm(s) for s in states] + [in_vmem(v) for v in local],
        16,
        scratch=[pltpu.SemaphoreType.DMA((4,))],
        specs=[hbm] * 4 + [vmem] * len(local),
        flops=quad * flops,
        moved=2 * moved(quad),
    )
    states_near, enc_turned, turned_weights = (results[:4], results[4], results[5:7])
    results = results[7:]
    ready = [results[3 * n : 3 * n + 3] for n in range(len(groups))]
    replies = call(
        functools.partial(owner_body, slots=quad, planes=planes),
        (message,) * quad,
        quad_messages + [in_vmem(v) for v in (*plane_messages, own_target, turned_weights[0])],
        16,
        scratch=[store, plane_store, pltpu.VMEM((quad, 8, LANES), f32)],
    )
    answers = [replies[0]] + [swap(replies[k], k, regions) for k in range(1, quad)]
    gradient_shapes = (
        pltpu.VMEM((code_width + 16, hidden), f32),
        pltpu.VMEM((hidden + 16, hidden), f32),
        pltpu.VMEM((hidden + 16, feat + LANES), f32),
    )
    earlier, depths, before = ((), [], ())
    steps = [(1, (0,), 0), (0, (1,), 0), (0, tuple(range(2, quad)), 1)]
    for n, slots, offset in steps:
        last = slots == steps[-1][1]
        if last:
            share = pltpu.VMEM((pack_rows, LANES), f32)
            out_shape = (pltpu.VMEM((1, ray_count), f32), share, share)
            if not pair:
                out_shape = (out_shape[0], shaped((shards, pack_rows, LANES), f32))
        else:
            out_shape = gradient_shapes + (pltpu.VMEM((len(slots), rays), f32),)
        inputs = [answers[k] for k in slots] + [*kept[n], *ready[n], enc_turned, *turned_weights]
        inputs += [*earlier] + (depths if last else [])
        out = call(
            functools.partial(
                backward_body,
                slots=slots,
                offset=offset,
                before=before,
                last=last,
                group_count=quad,
                shards=shards,
                **sizes,
            ),
            out_shape,
            [in_vmem(v) for v in inputs],
            24,
            scratch=[pltpu.VMEM((shards, pack_rows, LANES), f32)] if last else (),
            flops=2 * len(slots) * flops,
            moved=moved(len(slots)),
        )
        earlier, before = (out[:3], before + (slots,))
        if not last:
            depths.append(out[3])
    depth_grad, *grads = out
    if pair:
        parts = (grads[0], lax.ppermute(grads[1], "rays", [(0, 1), (1, 0)]))
    else:
        exchanged = lax.all_to_all(grads[0], "rays", 0, 0)
        parts = tuple(exchanged[s] for s in range(shards))
    return call(
        functools.partial(adam_body, shards=shards),
        tuple(shaped(s.shape, f32) for s in states) + (shaped(depth_grad.shape, f32),),
        [in_vmem(v) for v in (*parts, depth_grad, *states_near)],
        16,
    )


def solution(mesh):
    placed = (
        P(None, "rays", None),
        P("rays", None),
        P("rays"),
        P("region", "rays"),
        P("region", "rays"),
        P("region", None, "rays"),
        P(None, "region", "rays", None),
        P(None, "region", "rays", None),
        P(None, "region", "rays", None),
        P(None, "region", "rays"),
    )
    return jax.shard_map(
        per_device,
        mesh=mesh,
        in_specs=placed,
        out_specs=(
            P(None, "region", "rays", None),
            P(None, "region", "rays", None),
            P(None, "region", "rays", None),
            P(None, "region", "rays"),
            P("region", "rays"),
        ),
        check_vma=False,
    )
```

```python
import functools

import jax
import jax.numpy as jnp
from jax import lax
from jax.experimental import pallas as pl
from jax.experimental.pallas import tpu as pltpu
from jax.sharding import PartitionSpec as P

BINS = 64
LANES = 128
QUAD = 4

depth_scale = 4.0
beta_one = 0.9
beta_two = 0.999
learn_rate = 0.001
epsilon = 1e-08
first_fix = 1.0 - 0.9**10
second_fix = 1.0 - 0.999**10

f32 = jnp.float32
bf16 = jnp.bfloat16


def in_vmem(value):
    return pltpu.with_memory_space_constraint(value, pltpu.VMEM)


def in_hbm(value):
    return pltpu.with_memory_space_constraint(value, pltpu.HBM)


def call(body, out_shape, inputs, limit, scratch=(), specs=None, flops=1000000, moved=1000000):
    many = isinstance(out_shape, (tuple, list))
    spec = pl.BlockSpec(memory_space=pltpu.VMEM)
    return pl.pallas_call(
        body,
        out_shape=out_shape,
        in_specs=specs or [spec] * len(inputs),
        out_specs=tuple(spec for _ in out_shape) if many else spec,
        scratch_shapes=list(scratch),
        compiler_params=pltpu.CompilerParams(vmem_limit_bytes=limit * 1024 * 1024),
        cost_estimate=pl.CostEstimate(flops=flops, bytes_accessed=moved, transcendentals=0),
    )(*inputs)


def blocks(width):
    return [slice(LANES * k, LANES * (k + 1)) for k in range(width // LANES)]


def wide_rows(count):
    return -(-count // LANES)


def row_block(row, rows):
    width = row.shape[1]
    padded = wide_rows(width) * LANES
    if padded != width:
        row = jnp.concatenate([row, jnp.zeros((1, padded - width), f32)], 1)
    place = lax.broadcasted_iota(jnp.int32, (rows, LANES), 0)
    out = jnp.zeros((rows, LANES), f32)
    for k, cut in enumerate(blocks(padded)):
        out = jnp.where(place == k, jnp.broadcast_to(row[:, cut], (rows, LANES)), out)
    return out


def block_row(block, count):
    return jnp.concatenate([block[k : k + 1] for k in range(count)], 1)


def split3(value):
    high = value.astype(bf16).astype(f32)
    rest = value - high
    mid = rest.astype(bf16).astype(f32)
    return (high, mid, rest - mid)


def lanes_of(shape):
    return lax.broadcasted_iota(jnp.int32, shape, 1)


def turned(rows, ray_count):
    fill = LANES - rows.shape[0]
    return jnp.concatenate([rows, jnp.zeros((fill, ray_count), f32)], 0).T


def own_group(k, slots, rows):
    place = lax.rem(lax.axis_index("region"), slots) ^ k
    return pl.ds(pl.multiple_of(place * rows, rows), rows)


def fetch_body(*refs, slots):
    ins, (pack_ref, *refs) = (refs[:10], refs[10:])
    outs, held, sems = (refs[:6], refs[6:10], refs[10])
    target_ref = outs[5]
    copies = []

    def fetch(source, place):
        copies.append(pltpu.make_async_copy(source, place, sems.at[len(copies)]))
        copies[-1].start()

    for ref, hold in zip(ins[:4], held):
        fetch(ref.at[0], hold)
    for ref, out in zip(ins[4:9], outs):
        fetch(ref, out)
    fetch(ins[9].at[own_group(0, slots, target_ref.shape[0])], target_ref)
    spot = 0
    for copy, hold in zip(copies[:3], held[:3]):
        copy.wait()
        rows, width = hold.shape[1:]
        for cut in blocks(width):
            pack_ref[spot : spot + rows, :] = hold[0, :, cut].astype(bf16)
            spot += rows
    copies[3].wait()
    pack_ref[spot : spot + 16, :] = row_block(held[3][...], 16).astype(bf16)
    for copy in copies[4:]:
        copy.wait()


def encode_body(*refs, unit_length, slots):
    codes, bins, entry, exit_, direction, enc_ref, geometry_ref, *refs = refs
    flat_geometry, flat_position = refs
    bins = bins[0].astype(f32)
    samples, ray_count = bins.shape
    group_rows = ray_count // slots
    slot = lax.broadcasted_iota(jnp.int32, bins.shape, 0)
    following = jnp.where(slot == samples - 1, float(BINS), pltpu.roll(bins, samples - 1, 0))
    inside = ((slot >= entry[...]) & (slot < exit_[...])).astype(f32)
    flat_geometry[:samples] = (following - bins) * unit_length * inside
    flat_geometry[samples : samples + 1] = direction[...].astype(f32)
    flat_position[...] = turned((bins + 0.5) / BINS, ray_count)
    for k in range(slots):
        group = own_group(k, slots, group_rows)
        geometry_ref[k] = flat_geometry[:, group]
        code_zero = codes[0, group].astype(f32)
        code_one = codes[1, group].astype(f32)
        position = flat_position[group, :]
        for j in range(samples):
            encoded = code_zero + position[:, j : j + 1] * code_one
            enc_ref[k, group_rows * j : group_rows * (j + 1), :] = encoded.astype(bf16)


def assemble(packs, shapes, vec_share):
    shards = len(packs)
    spot = 0
    mats = []
    for rows, width in shapes:
        pieces = []
        for cut in blocks(width):
            pieces.append(jnp.concatenate([p[spot : spot + rows, :] for p in packs], 0))
            spot += rows
        mats.append(jnp.concatenate(pieces, 1))
    vec_total = vec_share * shards
    vec = jnp.zeros((1, vec_total), f32)
    for s, p in enumerate(packs):
        block = p[spot : spot + 16, :].astype(f32)
        count = wide_rows(vec_share)
        row = block_row(block, count)
        fill = vec_total - count * LANES
        if fill:
            row = jnp.concatenate([row, jnp.zeros((1, fill), f32)], 1)
        if s:
            row = pltpu.roll(row, vec_share * s, 1)
        vec = vec + row
    return (*mats, vec)


def product(left, right):
    return jnp.dot(left, right, preferred_element_type=f32)


def forward_slots(slots, weights, enc_ref, geometry_ref, message_refs, kept):
    in_weight, mid_ref, head_ref, vec = weights
    one_ref, two_ref, turn_ref, scalar_ref = kept
    samples, ray_count = scalar_ref.shape[2:]
    hidden = mid_ref.shape[0]
    feat = turn_ref.shape[2]
    bias_one = vec[:, :hidden]
    bias_two = vec[:, hidden : 2 * hidden]
    half_bias = 0.5 * vec[:, 3 * hidden :]
    lane = lanes_of((ray_count, LANES))
    ones, twos, densities = ([], [], [])
    for i, k in enumerate(slots):
        one = product(enc_ref[k], in_weight) + bias_one
        ones.append(jnp.maximum(one, 0.0).astype(bf16))
        one_ref[i] = ones[i]
    for i in range(len(slots)):
        two = product(ones[i], mid_ref[...]) + bias_two
        twos.append(jnp.maximum(two, 0.0).astype(bf16))
        two_ref[i] = twos[i]
    raws = [product(two, head_ref[:, feat:]) for two in twos]
    for raw in raws:
        density = jnp.zeros((ray_count, LANES), f32)
        for j in range(samples):
            rows = slice(ray_count * j, ray_count * (j + 1))
            density = jnp.where(lane == j, raw[rows], density)
        densities.append(density)
    for i in range(len(slots)):
        turn_ref[i] = jnp.tanh(product(twos[i], head_ref[:, :feat]) + half_bias)
    density = side_by_side([value.T[:samples] for value in densities])
    geometry = side_by_side([geometry_ref[k, :samples] for k in slots])
    direction = side_by_side([geometry_ref[k, samples : samples + 1] for k in slots])
    soft = jnp.maximum(density, 0.0) + jnp.log1p(jnp.exp(-jnp.abs(density)))
    optical = soft * geometry
    before = [jnp.zeros_like(direction)]
    for j in range(samples):
        before.append(before[-1] + optical[j : j + 1])
    depth = before.pop()
    optical_before = jnp.concatenate(before, 0)
    opacity = jnp.tanh(0.5 * optical) * (1.0 + jnp.exp(-optical))
    local_weight = jnp.exp(-optical_before) * opacity
    half_weight = 0.5 * local_weight
    half_sum = jnp.sum(half_weight, 0, keepdims=True)
    columns = turned(jnp.concatenate([half_weight, half_sum], 0), depth.shape[1])
    shared = jnp.concatenate([*split3(depth), direction], 0)
    sig = 0.5 * jnp.tanh(0.5 * density) + 0.5
    scalars = (local_weight, jnp.exp(-(optical_before + optical)), geometry * sig)
    for i, k in enumerate(slots):
        cut = slice(ray_count * i, ray_count * (i + 1))
        for q, value in enumerate(scalars):
            scalar_ref[i, q] = value[:, cut]
        own = columns[cut]
        total = jnp.zeros((ray_count, feat), f32) + own[:, samples : samples + 1]
        for j in range(samples):
            rows = slice(ray_count * j, ray_count * (j + 1))
            total = total + own[:, j : j + 1] * turn_ref[i, rows, :]
        message_refs[i][...] = as_message([total[:, k] for k in blocks(feat)], shared[:, cut])


def side_by_side(values):
    return jnp.concatenate(values, 1) if len(values) > 1 else values[0]


def as_message(parts, rows):
    count, rays = rows.shape
    if count < 8:
        rows = jnp.concatenate([rows, jnp.zeros((8 - count, rays), f32)], 0)
    if rays < LANES:
        rows = jnp.concatenate([rows, jnp.zeros((8, LANES - rays), f32)], 1)
    return jnp.concatenate([*parts, rows], 0).astype(bf16)


def from_message(value, rays):
    value = value.astype(f32)
    count = value.shape[0] // rays
    parts = [value[rays * k : rays * (k + 1)] for k in range(count)]
    return (parts, value[rays * count :, :rays])


def forward_first_body(*refs, shapes, vec_share, pair, slots):
    both = None
    if pair:
        own_ref, other_ref, *refs, both = refs
        mine = lax.axis_index("rays")
        both[mine] = own_ref[...]
        both[1 - mine] = other_ref[...]
        packs = [both.at[0], both.at[1]]
    else:
        packs_ref, *refs = refs
        packs = [packs_ref.at[s] for s in range(packs_ref.shape[0])]
    enc_ref, geometry_ref, in_ref, mid_ref, head_ref, vec_ref, *refs = refs
    hidden = mid_ref.shape[0]
    in_weight, mid_weight, feat_weight, vec = assemble(packs, shapes, vec_share)
    density_row = vec[:, 2 * hidden : 3 * hidden]
    density_cols = jnp.broadcast_to(density_row, (LANES, hidden)).T
    in_ref[...] = in_weight
    mid_ref[...] = mid_weight
    half_weight = (0.5 * feat_weight.astype(f32)).astype(bf16)
    head_ref[...] = jnp.concatenate([half_weight, density_cols.astype(bf16)], 1)
    vec_ref[...] = vec
    weights = (in_weight, mid_ref, head_ref, vec)
    forward_slots(slots, weights, enc_ref, geometry_ref, refs[4:], refs[:4])


def forward_rest_body(in_ref, mid_ref, head_ref, vec_ref, *refs, slots):
    enc_ref, geometry_ref, *refs = refs[1:] if slots == (0,) else refs
    weights = (in_ref[...], mid_ref, head_ref, vec_ref[...])
    forward_slots(slots, weights, enc_ref, geometry_ref, refs[4:], refs[:4])


def sides(values):
    below, above = ([jnp.zeros_like(values[0])], [jnp.zeros_like(values[0])])
    for q in range(len(values) - 1):
        below.append(below[-1] + values[q])
        above.append(above[-1] + values[len(values) - 1 - q])
    return (below, above[::-1])


def gather_messages(refs, store, own, rays):
    for k, ref in enumerate(refs):
        store[own ^ k] = ref[...]
    members = [from_message(store[p], rays) for p in range(len(refs))]
    parts = [m[0] for m in members]
    depth = [m[1][0:1] + m[1][1:2] + m[1][2:3] for m in members]
    direction = members[0][1][3:4]
    below, above = sides(depth)
    trans = [jnp.exp(-jnp.where(direction < 0.5, b, a)) for b, a in zip(below, above)]
    return (parts, depth, direction, trans)


def member_at(level, quad):
    region = lax.axis_index("region")
    if level == 0:
        return lax.rem(region, quad)
    return lax.rem(lax.div(region, quad << (level - 1)), 2)


def as_columns(rows):
    columns = turned(jnp.concatenate(rows, 0), rows[0].shape[1])
    return [columns[:, i : i + 1] for i in range(len(rows))]


def weighted_sum(factors, parts):
    out = []
    for k in range(len(parts[0])):
        total = factors[0] * parts[0][k]
        for factor, part in zip(factors[1:], parts[1:]):
            total = total + factor * part[k]
        out.append(total)
    return out


def inner(left, right):
    total = left[0] * right[0]
    for a, b in zip(left[1:], right[1:]):
        total = total + a * b
    return jnp.sum(total, 1, keepdims=True)


def combine_body(*refs, rays, level, quad):
    *messages, out_ref, store = refs
    messages = messages[: quad if level == 0 else 2]
    own = member_at(level, quad)
    parts, depth, direction, trans = gather_messages(messages, store, own, rays)
    total = depth[0]
    for value in depth[1:]:
        total = total + value
    rows = jnp.concatenate([*split3(total), direction], 0)
    out_ref[...] = as_message(weighted_sum(as_columns(trans), parts), rows)


def owner_body(*refs, counts, quad):
    levels = []
    for count in counts:
        messages, refs = (refs[:count], refs[count:])
        levels.append(messages)
    target_ref, _, *refs = refs
    out_refs, stores, reply = (refs[:quad], refs[quad:-1], refs[-1])
    rays, feat = target_ref.shape
    own = [member_at(n, quad) for n in range(len(counts))]
    found = [
        gather_messages(messages, stores[n], own[n], rays) for n, messages in enumerate(levels)
    ]
    direction = found[0][2]
    parts, _, _, trans = found[-1]
    rendered = weighted_sum(as_columns(trans), parts)
    grads = [
        (value - target_ref[:, cut].astype(f32)).astype(bf16).astype(f32)
        for value, cut in zip(rendered, blocks(feat))
    ]
    lane = lanes_of((rays, LANES))
    inners = jnp.zeros((rays, LANES), f32)
    for i, value in enumerate(sum((f[0] for f in found), [])):
        inners = jnp.where(lane == i, inner(grads, value), inners)
    inners = inners.T

    def picked(values, place):
        out = values[0]
        for n, value in enumerate(values[1:]):
            out = jnp.where(place == n + 1, value, out)
        return out

    ahead = jnp.ones((1, rays), f32)
    reach = jnp.zeros((1, rays), f32)
    for n in range(len(counts) - 1, -1, -1):
        first = sum(counts[:n])
        trans = [ahead * t for t in found[n][3]]
        below, above = sides([t * inners[first + p : first + p + 1] for p, t in enumerate(trans)])
        after = [reach + jnp.where(direction < 0.5, a, b) for b, a in zip(below, above)]
        if n:
            ahead, reach = (picked(trans, own[n]), picked(after, own[n]))
    for p in range(quad):
        reply[p, :6, :rays] = jnp.concatenate([*split3(trans[p]), *split3(after[p])], 0)
    for k, out_ref in enumerate(out_refs):
        out_ref[...] = as_message(grads, reply[own[0] ^ k, :6, :rays])


def with_ones(value):
    return jnp.concatenate([value.T, jnp.ones((16, value.shape[0]), bf16)], 0)


def ready_shared_body(*refs):
    states, (enc_ref, mid_ref, head_ref, *refs) = (refs[:4], refs[4:])
    source, fetched, refs = (refs[:4], refs[4:8], refs[8:])
    enc_turned, mid_turned, head_turned, *results, sems = refs
    copies = []
    for n, (ref, place) in enumerate(zip(states, fetched)):
        copies.append(pltpu.make_async_copy(ref, place, sems.at[n]))
        copies[-1].start()
    feat = source[2].shape[2]
    mid_turned[...] = mid_ref[...].T
    head = head_ref[...].astype(f32)
    lane = lanes_of(head.shape)
    head_turned[...] = jnp.where(lane < feat, 2.0 * head, head).astype(bf16).T
    for k in range(enc_ref.shape[0]):
        enc_turned[k] = with_ones(enc_ref[k])
    ready_slots(source, results)
    for copy in copies:
        copy.wait()


def ready_body(*refs):
    count = len(refs) // 7
    for n in range(count):
        ready_slots(refs[4 * n : 4 * n + 4], refs[4 * count + 3 * n : 4 * count + 3 * n + 3])


def ready_slots(source, results):
    one_ref, two_ref, turn_ref, scalar_ref = source
    one_turned, two_turned, slope_ref = results
    samples, ray_count = scalar_ref.shape[2:]
    for i in range(one_ref.shape[0]):
        one_turned[i] = with_ones(one_ref[i])
        two_turned[i] = with_ones(two_ref[i])
        columns = turned(0.25 * scalar_ref[i, 0], ray_count)
        for j in range(samples):
            rows = slice(ray_count * j, ray_count * (j + 1))
            turn = turn_ref[i, rows, :]
            slope_ref[i, rows, :] = columns[:, j : j + 1] * (1.0 - turn * turn)


def backward_body(*refs, slots, places, sources, before, last, group_count, shapes, vec_share, shards):
    begun = not before
    messages, refs = (refs[: len(slots)], refs[len(slots) :])
    held = [[ref.at[at] for ref in refs[7 * n : 7 * n + 7]] for n, at in places]
    refs = refs[7 * sources :]
    enc_turned, mid_turned, head_turned, *refs = refs
    if not begun:
        earlier, refs = (refs[:3], refs[3:])
    if last:
        depths, (depth_ref, *outs) = (refs[: len(before)], refs[len(before) :])
    else:
        *outs, depth_ref = refs
    samples, ray_count = held[0][3].shape[1:]
    hidden = held[0][0].shape[1]
    feat = held[0][2].shape[1]
    lane = lanes_of((ray_count, LANES))
    if last:
        for ref, group in zip(depths, before):
            for i, k in enumerate(group):
                depth_ref[:, own_group(k, group_count, ray_count)] = ref[i : i + 1]
    sums = [0.0, 0.0, 0.0] if begun else [ref[...] for ref in earlier]
    grads, extras, spreads = ([], [], [])
    for i, k in enumerate(slots):
        parts, extra = from_message(messages[i][...], ray_count)
        grad = jnp.concatenate(parts, 1)
        grads.append(grad)
        extras.append(extra)
        grad_sum = jnp.sum(grad, 1, keepdims=True)
        spread = jnp.where(lane == samples, grad_sum, 0.0)
        for j in range(samples):
            rows = slice(ray_count * j, ray_count * (j + 1))
            value = jnp.sum(held[i][2][rows, :] * grad, 1, keepdims=True)
            spread = jnp.where(lane == j, value, spread)
        spreads.append(spread.T)
    extra = side_by_side(extras)
    trans = extra[0:1] + extra[1:2] + extra[2:3]
    after = extra[3:4] + extra[4:5] + extra[5:6]
    for i, k in enumerate(slots):
        cut = slice(ray_count * i, ray_count * (i + 1))
        if last:
            depth_ref[:, own_group(k, group_count, ray_count)] = -after[:, cut]
        else:
            depth_ref[i : i + 1] = -after[:, cut]
    spread = side_by_side(spreads)
    sample_grad = 0.5 * (spread[:samples] + spread[samples : samples + 1])
    local_weight, trans_after, slope = [
        side_by_side([refs_of[3][q] for refs_of in held]) for q in range(3)
    ]
    weighted = local_weight * sample_grad
    later = [jnp.zeros_like(after)]
    for j in range(samples - 1, 0, -1):
        later.append(later[-1] + weighted[j : j + 1])
    later = jnp.concatenate(later[::-1], 0)
    optical_grad = trans * (trans_after * sample_grad - later) - after
    columns = turned(jnp.concatenate([optical_grad * slope, trans], 0), after.shape[1])
    zero = jnp.zeros((), bf16)
    for i, k in enumerate(slots):
        one_ref, two_ref, _, _, one_turned, two_turned, slope_ref = held[i]
        own = columns[ray_count * i : ray_count * (i + 1)]
        grad_ahead = grads[i] * own[:, samples : samples + 1]
        pieces = []
        for j in range(samples):
            rows = slice(ray_count * j, ray_count * (j + 1))
            colour_grad = (grad_ahead * slope_ref[rows, :]).astype(bf16)
            density_part = jnp.where(lane == j, own, 0.0).astype(bf16)
            pieces.append(jnp.concatenate([colour_grad, density_part], 1))
        head_grad = jnp.concatenate(pieces, 0)
        second = product(head_grad, head_turned[...]).astype(bf16)
        sums[2] = sums[2] + product(two_turned[...], head_grad)
        second = jnp.where(two_ref[...] > 0, second, zero)
        first = product(second, mid_turned[...]).astype(bf16)
        sums[1] = sums[1] + product(one_turned[...], second)
        first = jnp.where(one_ref[...] > 0, first, zero)
        sums[0] = sums[0] + product(enc_turned[k], first)
    if not last:
        for value, ref in zip(sums, outs):
            ref[...] = value
        return
    values = [value[:-16] for value in sums]
    first_sum, second_sum, head_sum = [value[-16:-15] for value in sums]
    density_sum = jnp.sum(values[2][:, feat:].T, 0, keepdims=True)
    vec = jnp.concatenate([first_sum, second_sum, density_sum, head_sum[:, :feat]], 1)
    total = vec.shape[1]

    def write(s, ref):
        spot = 0
        for (rows, width), value in zip(shapes, values):
            for cut in blocks(width):
                ref[spot : spot + rows, :] = value[rows * s : rows * (s + 1), cut]
                spot += rows
        row = pltpu.roll(vec, total - vec_share * s, 1) if s else vec
        ref[spot : spot + 16, :] = row_block(row[:, : wide_rows(vec_share) * LANES], 16)

    if shards != 2:
        for s in range(shards):
            write(s, outs[0].at[s])
        return
    mine = lax.axis_index("rays")
    for s in range(2):

        @pl.when(mine == s)
        def _():
            write(s, outs[0])
            write(1 - s, outs[1])


def adam_body(*refs, shards):
    grad_refs, (depth_ref, *refs) = (refs[:shards], refs[shards:])
    state_refs, out_refs, depth_out = (refs[:4], refs[4:8], refs[8])
    depth_out[...] = depth_ref[...]

    def update(stacked, gradient):
        first_moment = beta_one * stacked[1] + (1.0 - beta_one) * gradient
        second = beta_two * stacked[2] + (1.0 - beta_two) * gradient * gradient
        step = first_moment / first_fix / (jnp.sqrt(second / second_fix) + epsilon)
        return (stacked[0] - learn_rate * step, first_moment, second)

    def gathered(spot, rows):
        total = grad_refs[0][spot : spot + rows, :]
        for ref in grad_refs[1:]:
            total = total + ref[spot : spot + rows, :]
        return total

    spot = 0
    for ref, out in zip(state_refs[:3], out_refs[:3]):
        rows, width = ref.shape[2:]
        for cut in blocks(width):
            new = update([ref[i, 0, :, cut] for i in range(3)], gathered(spot, rows))
            spot += rows
            for i in range(3):
                out[i, 0, :, cut] = new[i]
    ref, out = (state_refs[3], out_refs[3])
    share = ref.shape[2]
    gradient = block_row(gathered(spot, 16), wide_rows(share))[:, :share]
    new = update([ref[i] for i in range(3)], gradient)
    for i in range(3):
        out[i] = new[i]


def shaped(shape, dtype):
    return jax.ShapeDtypeStruct(shape, dtype)


def swap(value, distance, size):
    return lax.ppermute(value, "region", [(i, i ^ distance) for i in range(size)])


def per_device(
    ray_codes,
    target,
    direction,
    entries,
    exits,
    depth_bins,
    in_layer,
    mid_layer,
    feat_layer,
    vectors,
):
    regions = lax.axis_size("region")
    shards = lax.axis_size("rays")
    samples, ray_count = depth_bins.shape[1:]
    quad = min(QUAD, regions)
    planes = regions // quad
    rays = ray_count // quad
    layers = (in_layer, mid_layer, feat_layer)
    states = (*layers, vectors)
    shapes = tuple(layer.shape[2:] for layer in layers)
    vec_share = vectors.shape[2]
    hidden = shapes[0][1]
    feat = shapes[2][1]
    code_width = ray_codes.shape[2]
    pack_rows = sum(rows * (width // LANES) for rows, width in shapes) + 16
    rows = samples * rays
    sizes = dict(shapes=shapes, vec_share=vec_share)
    pair = shards == 2
    flops = 2 * rows * (code_width * hidden + hidden * hidden + hidden * (feat + LANES))

    arguments = (*states, ray_codes, depth_bins, entries, exits, direction[None], target)
    pack, *geometric, own_target = call(
        functools.partial(fetch_body, slots=quad),
        (pltpu.VMEM((pack_rows, LANES), bf16),)
        + tuple(pltpu.VMEM(a.shape, a.dtype) for a in arguments[4:9])
        + (pltpu.VMEM((rays, feat), bf16),),
        [in_hbm(a) for a in arguments],
        16,
        scratch=[pltpu.VMEM(a.shape[1:], f32) for a in states]
        + [pltpu.SemaphoreType.DMA((10,))],
        specs=[pl.BlockSpec(memory_space=pltpu.HBM)] * 10,
    )
    if pair:
        packs = (pack, lax.ppermute(pack, "rays", [(0, 1), (1, 0)]))
    else:
        packs = (lax.all_gather(pack, "rays", axis=0),)
    encoded, geometry = call(
        functools.partial(encode_body, unit_length=depth_scale / (regions * BINS), slots=quad),
        (
            pltpu.VMEM((quad, rows, code_width), bf16),
            pltpu.VMEM((quad, samples + 8, rays), f32),
        ),
        [in_vmem(v) for v in geometric],
        16,
        scratch=[
            pltpu.VMEM((samples + 8, ray_count), f32),
            pltpu.VMEM((ray_count, LANES), f32),
        ],
        flops=10 * quad * rows * code_width,
        moved=quad * rows * code_width * 4,
    )

    message = pltpu.VMEM((rays * (feat // LANES) + 8, LANES), bf16)

    def kept_shapes(count):
        return (
            pltpu.VMEM((count, rows, hidden), bf16),
            pltpu.VMEM((count, rows, hidden), bf16),
            pltpu.VMEM((count, rows, feat), f32),
            pltpu.VMEM((count, 3, samples, rays), f32),
        )

    def moved(count):
        return count * rows * (feat + hidden) * 4

    weight_shapes = (
        pltpu.VMEM((shapes[0][0] * shards, hidden), bf16),
        pltpu.VMEM((hidden, hidden), bf16),
        pltpu.VMEM((hidden, feat + LANES), bf16),
        pltpu.VMEM((1, vec_share * shards), f32),
    )

    def forward(slots, inputs, first):
        if first:
            body = functools.partial(forward_first_body, pair=pair, slots=slots, **sizes)
        else:
            body = functools.partial(forward_rest_body, slots=slots)
        out = call(
            body,
            (weight_shapes if first else ())
            + kept_shapes(len(slots))
            + (message,) * len(slots),
            [in_vmem(v) for v in (*inputs, encoded, geometry)],
            16,
            scratch=[pltpu.VMEM((2, pack_rows, LANES), bf16)] if first and pair else (),
            flops=len(slots) * flops,
            moved=moved(len(slots)),
        )
        found, out = (out[:4], out[4:]) if first else (None, out)
        return (out[:4], list(out[4:]), found)

    groups = [(quad - 1,), tuple(range(1, quad - 1)), (0,)]
    kept, sent, weights = ([], {}, None)
    for slots in groups:
        inputs = packs if not kept else (*weights, sent[quad - 1]) if slots == (0,) else weights
        arrays, messages, found = forward(slots, inputs, not kept)
        weights = weights or found
        kept.append(arrays)
        for k, value in zip(slots, messages):
            sent[k] = swap(value, k, regions) if k else value
    quad_messages = [in_vmem(sent[k]) for k in range(quad)]
    def ready_shapes(count):
        return (
            pltpu.VMEM((count, hidden + 16, rows), bf16),
            pltpu.VMEM((count, hidden + 16, rows), bf16),
            pltpu.VMEM((count, rows, feat), f32),
        )

    hbm, vmem = (pl.BlockSpec(memory_space=m) for m in (pltpu.HBM, pltpu.VMEM))
    local = [encoded, weights[1], weights[2], *kept[0]]
    results = call(
        ready_shared_body,
        tuple(pltpu.VMEM(s.shape, f32) for s in states)
        + (
            pltpu.VMEM((quad, code_width + 16, rows), bf16),
            pltpu.VMEM((hidden, hidden), bf16),
            pltpu.VMEM((feat + LANES, hidden), bf16),
        )
        + ready_shapes(len(groups[0])),
        [in_hbm(s) for s in states] + [in_vmem(v) for v in local],
        16,
        scratch=[pltpu.SemaphoreType.DMA((4,))],
        specs=[hbm] * 4 + [vmem] * len(local),
        flops=flops,
        moved=2 * moved(1),
    )
    states_near, enc_turned, turned_weights = (results[:4], results[4], results[5:7])
    ready = [results[7:]]
    results = call(
        ready_body,
        sum((ready_shapes(len(slots)) for slots in groups[1:]), ()),
        [in_vmem(v) for v in sum(map(list, kept[1:]), [])],
        16,
        flops=(quad - 1) * flops,
        moved=2 * moved(quad - 1),
    )
    ready += [results[3 * n : 3 * n + 3] for n in range(len(groups) - 1)]
    ahead = {1: [in_vmem(turned_weights[0])]}
    levels = [quad_messages]
    for level in range(planes.bit_length() - 1):
        composite = call(
            functools.partial(combine_body, rays=rays, level=level, quad=quad),
            message,
            levels[-1] + ahead.get(level, []),
            16,
            scratch=[pltpu.VMEM((len(levels[-1]), *message.shape), bf16)],
        )
        levels.append([in_vmem(composite), in_vmem(swap(composite, quad << level, regions))])
    counts = tuple(len(level) for level in levels)
    replies = call(
        functools.partial(owner_body, counts=counts, quad=quad),
        (message,) * quad,
        sum(levels, []) + [in_vmem(v) for v in (own_target, results[0])],
        16,
        scratch=[pltpu.VMEM((count, *message.shape), bf16) for count in counts]
        + [pltpu.VMEM((quad, 8, LANES), f32)],
    )
    answers = [replies[0]] + [swap(replies[k], k, regions) for k in range(1, quad)]
    gradient_shapes = (
        pltpu.VMEM((code_width + 16, hidden), f32),
        pltpu.VMEM((hidden + 16, hidden), f32),
        pltpu.VMEM((hidden + 16, feat + LANES), f32),
    )
    earlier, depths, before = ((), [], ())
    place = {k: (n, slots.index(k)) for n, slots in enumerate(groups) for k in slots}
    steps = [(0,), (1,), tuple(range(2, quad))]
    for slots in steps:
        last = slots == steps[-1]
        if last:
            share = pltpu.VMEM((pack_rows, LANES), f32)
            out_shape = (pltpu.VMEM((1, ray_count), f32), share, share)
            if not pair:
                out_shape = (out_shape[0], shaped((shards, pack_rows, LANES), f32))
        else:
            out_shape = gradient_shapes + (pltpu.VMEM((len(slots), rays), f32),)
        used = sorted({place[k][0] for k in slots})
        inputs = [answers[k] for k in slots]
        inputs += sum(([*kept[n], *ready[n]] for n in used), [])
        inputs += [enc_turned, *turned_weights, *earlier] + (depths if last else [])
        out = call(
            functools.partial(
                backward_body,
                slots=slots,
                places=tuple((used.index(place[k][0]), place[k][1]) for k in slots),
                sources=len(used),
                before=before,
                last=last,
                group_count=quad,
                shards=shards,
                **sizes,
            ),
            out_shape,
            [in_vmem(v) for v in inputs],
            24,
            flops=2 * len(slots) * flops,
            moved=moved(len(slots)),
        )
        earlier, before = (out[:3], before + (slots,))
        if not last:
            depths.append(out[3])
    depth_grad, *grads = out
    if pair:
        parts = (grads[0], lax.ppermute(grads[1], "rays", [(0, 1), (1, 0)]))
    else:
        exchanged = lax.all_to_all(grads[0], "rays", 0, 0)
        parts = tuple(exchanged[s] for s in range(shards))
    return call(
        functools.partial(adam_body, shards=shards),
        tuple(shaped(s.shape, f32) for s in states) + (shaped(depth_grad.shape, f32),),
        [in_vmem(v) for v in (*parts, depth_grad, *states_near)],
        16,
    )


def solution(mesh):
    placed = (
        P(None, "rays", None),
        P("rays", None),
        P("rays"),
        P("region", "rays"),
        P("region", "rays"),
        P("region", None, "rays"),
        P(None, "region", "rays", None),
        P(None, "region", "rays", None),
        P(None, "region", "rays", None),
        P(None, "region", "rays"),
    )
    return jax.shard_map(
        per_device,
        mesh=mesh,
        in_specs=placed,
        out_specs=(
            P(None, "region", "rays", None),
            P(None, "region", "rays", None),
            P(None, "region", "rays", None),
            P(None, "region", "rays"),
            P("region", "rays"),
        ),
        check_vma=False,
    )
```

```python
import functools

import jax
import jax.numpy as jnp
from jax import lax
from jax.experimental import pallas as pl
from jax.experimental.pallas import tpu as pltpu
from jax.sharding import PartitionSpec as P

BINS = 64
LANES = 128
QUAD = 4

depth_scale = 4.0
beta_one = 0.9
beta_two = 0.999
learn_rate = 0.001
epsilon = 1e-08
first_fix = 1.0 - 0.9**10
second_fix = 1.0 - 0.999**10

f32 = jnp.float32
bf16 = jnp.bfloat16


def in_vmem(value):
    return pltpu.with_memory_space_constraint(value, pltpu.VMEM)


def in_hbm(value):
    return pltpu.with_memory_space_constraint(value, pltpu.HBM)


def call(body, out_shape, inputs, limit, scratch=(), specs=None, flops=1000000, moved=1000000):
    many = isinstance(out_shape, (tuple, list))
    spec = pl.BlockSpec(memory_space=pltpu.VMEM)
    return pl.pallas_call(
        body,
        out_shape=out_shape,
        in_specs=specs or [spec] * len(inputs),
        out_specs=tuple(spec for _ in out_shape) if many else spec,
        scratch_shapes=list(scratch),
        compiler_params=pltpu.CompilerParams(vmem_limit_bytes=limit * 1024 * 1024),
        cost_estimate=pl.CostEstimate(flops=flops, bytes_accessed=moved, transcendentals=0),
    )(*inputs)


def blocks(width):
    return [slice(LANES * k, LANES * (k + 1)) for k in range(width // LANES)]


def wide_rows(count):
    return -(-count // LANES)


def row_block(row, rows):
    width = row.shape[1]
    padded = wide_rows(width) * LANES
    if padded != width:
        row = jnp.concatenate([row, jnp.zeros((1, padded - width), f32)], 1)
    place = lax.broadcasted_iota(jnp.int32, (rows, LANES), 0)
    out = jnp.zeros((rows, LANES), f32)
    for k, cut in enumerate(blocks(padded)):
        out = jnp.where(place == k, jnp.broadcast_to(row[:, cut], (rows, LANES)), out)
    return out


def block_row(block, count):
    return jnp.concatenate([block[k : k + 1] for k in range(count)], 1)


def split3(value):
    high = value.astype(bf16).astype(f32)
    rest = value - high
    mid = rest.astype(bf16).astype(f32)
    return (high, mid, rest - mid)


def lanes_of(shape):
    return lax.broadcasted_iota(jnp.int32, shape, 1)


def turned(rows, ray_count):
    fill = LANES - rows.shape[0]
    return jnp.concatenate([rows, jnp.zeros((fill, ray_count), f32)], 0).T


def own_group(k, slots, rows):
    place = lax.rem(lax.axis_index("region"), slots) ^ k
    return pl.ds(pl.multiple_of(place * rows, rows), rows)


def fetch_body(*refs, slots):
    ins, (pack_ref, *refs) = (refs[:10], refs[10:])
    outs, held, sems = (refs[:6], refs[6:10], refs[10])
    target_ref = outs[5]
    copies = []

    def fetch(source, place):
        copies.append(pltpu.make_async_copy(source, place, sems.at[len(copies)]))
        copies[-1].start()

    for ref, hold in zip(ins[:4], held):
        fetch(ref.at[0], hold)
    for ref, out in zip(ins[4:9], outs):
        fetch(ref, out)
    fetch(ins[9].at[own_group(0, slots, target_ref.shape[0])], target_ref)
    spot = 0
    for copy, hold in zip(copies[:3], held[:3]):
        copy.wait()
        rows, width = hold.shape[1:]
        for cut in blocks(width):
            pack_ref[spot : spot + rows, :] = hold[0, :, cut].astype(bf16)
            spot += rows
    copies[3].wait()
    pack_ref[spot : spot + 16, :] = row_block(held[3][...], 16).astype(bf16)
    for copy in copies[4:]:
        copy.wait()


def encode_body(*refs, unit_length, slots):
    codes, bins, entry, exit_, direction, enc_ref, geometry_ref, *refs = refs
    flat_geometry, flat_position = refs
    bins = bins[0].astype(f32)
    samples, ray_count = bins.shape
    group_rows = ray_count // slots
    slot = lax.broadcasted_iota(jnp.int32, bins.shape, 0)
    following = jnp.where(slot == samples - 1, float(BINS), pltpu.roll(bins, samples - 1, 0))
    inside = ((slot >= entry[...]) & (slot < exit_[...])).astype(f32)
    flat_geometry[:samples] = (following - bins) * unit_length * inside
    flat_geometry[samples : samples + 1] = direction[...].astype(f32)
    flat_position[...] = turned((bins + 0.5) / BINS, ray_count)
    for k in range(slots):
        group = own_group(k, slots, group_rows)
        geometry_ref[k] = flat_geometry[:, group]
        code_zero = codes[0, group].astype(f32)
        code_one = codes[1, group].astype(f32)
        position = flat_position[group, :]
        for j in range(samples):
            encoded = code_zero + position[:, j : j + 1] * code_one
            enc_ref[k, group_rows * j : group_rows * (j + 1), :] = encoded.astype(bf16)


def assemble(packs, shapes, vec_share):
    shards = len(packs)
    spot = 0
    mats = []
    for rows, width in shapes:
        pieces = []
        for cut in blocks(width):
            pieces.append(jnp.concatenate([p[spot : spot + rows, :] for p in packs], 0))
            spot += rows
        mats.append(jnp.concatenate(pieces, 1))
    vec_total = vec_share * shards
    vec = jnp.zeros((1, vec_total), f32)
    for s, p in enumerate(packs):
        block = p[spot : spot + 16, :].astype(f32)
        count = wide_rows(vec_share)
        row = block_row(block, count)
        fill = vec_total - count * LANES
        if fill:
            row = jnp.concatenate([row, jnp.zeros((1, fill), f32)], 1)
        if s:
            row = pltpu.roll(row, vec_share * s, 1)
        vec = vec + row
    return (*mats, vec)


def product(left, right):
    return jnp.dot(left, right, preferred_element_type=f32)


def forward_slots(slots, weights, enc_ref, geometry_ref, message_refs, kept):
    in_weight, mid_ref, head_ref, vec = weights
    one_ref, two_ref, turn_ref, scalar_ref = kept
    samples, ray_count = scalar_ref.shape[2:]
    hidden = mid_ref.shape[0]
    feat = turn_ref.shape[2]
    bias_one = vec[:, :hidden]
    bias_two = vec[:, hidden : 2 * hidden]
    half_bias = 0.5 * vec[:, 3 * hidden :]
    lane = lanes_of((ray_count, LANES))
    ones, twos, densities = ([], [], [])
    for i, k in enumerate(slots):
        one = product(enc_ref[k], in_weight) + bias_one
        ones.append(jnp.maximum(one, 0.0).astype(bf16))
        one_ref[i] = ones[i]
    for i in range(len(slots)):
        two = product(ones[i], mid_ref[...]) + bias_two
        twos.append(jnp.maximum(two, 0.0).astype(bf16))
        two_ref[i] = twos[i]
    raws = [product(two, head_ref[:, feat:]) for two in twos]
    for raw in raws:
        density = jnp.zeros((ray_count, LANES), f32)
        for j in range(samples):
            rows = slice(ray_count * j, ray_count * (j + 1))
            density = jnp.where(lane == j, raw[rows], density)
        densities.append(density)
    for i in range(len(slots)):
        turn_ref[i] = jnp.tanh(product(twos[i], head_ref[:, :feat]) + half_bias)
    density = side_by_side([value.T[:samples] for value in densities])
    geometry = side_by_side([geometry_ref[k, :samples] for k in slots])
    direction = side_by_side([geometry_ref[k, samples : samples + 1] for k in slots])
    soft = jnp.maximum(density, 0.0) + jnp.log1p(jnp.exp(-jnp.abs(density)))
    optical = soft * geometry
    before = [jnp.zeros_like(direction)]
    for j in range(samples):
        before.append(before[-1] + optical[j : j + 1])
    depth = before.pop()
    optical_before = jnp.concatenate(before, 0)
    opacity = jnp.tanh(0.5 * optical) * (1.0 + jnp.exp(-optical))
    local_weight = jnp.exp(-optical_before) * opacity
    half_weight = 0.5 * local_weight
    half_sum = jnp.sum(half_weight, 0, keepdims=True)
    columns = turned(jnp.concatenate([half_weight, half_sum], 0), depth.shape[1])
    shared = jnp.concatenate([*split3(depth), direction], 0)
    sig = 0.5 * jnp.tanh(0.5 * density) + 0.5
    scalars = (local_weight, jnp.exp(-(optical_before + optical)), geometry * sig)
    for i, k in enumerate(slots):
        cut = slice(ray_count * i, ray_count * (i + 1))
        for q, value in enumerate(scalars):
            scalar_ref[i, q] = value[:, cut]
        own = columns[cut]
        total = jnp.zeros((ray_count, feat), f32) + own[:, samples : samples + 1]
        for j in range(samples):
            rows = slice(ray_count * j, ray_count * (j + 1))
            total = total + own[:, j : j + 1] * turn_ref[i, rows, :]
        message_refs[i][...] = as_message([total[:, k] for k in blocks(feat)], shared[:, cut])


def side_by_side(values):
    return jnp.concatenate(values, 1) if len(values) > 1 else values[0]


def as_message(parts, rows):
    count, rays = rows.shape
    if count < 8:
        rows = jnp.concatenate([rows, jnp.zeros((8 - count, rays), f32)], 0)
    if rays < LANES:
        rows = jnp.concatenate([rows, jnp.zeros((8, LANES - rays), f32)], 1)
    return jnp.concatenate([*parts, rows], 0).astype(bf16)


def from_message(value, rays):
    value = value.astype(f32)
    count = value.shape[0] // rays
    parts = [value[rays * k : rays * (k + 1)] for k in range(count)]
    return (parts, value[rays * count :, :rays])


def forward_first_body(*refs, shapes, vec_share, pair, slots):
    both = None
    if pair:
        own_ref, other_ref, *refs, both = refs
        mine = lax.axis_index("rays")
        both[mine] = own_ref[...]
        both[1 - mine] = other_ref[...]
        packs = [both.at[0], both.at[1]]
    else:
        packs_ref, *refs = refs
        packs = [packs_ref.at[s] for s in range(packs_ref.shape[0])]
    enc_ref, geometry_ref, in_ref, mid_ref, head_ref, vec_ref, *refs = refs
    hidden = mid_ref.shape[0]
    in_weight, mid_weight, feat_weight, vec = assemble(packs, shapes, vec_share)
    density_row = vec[:, 2 * hidden : 3 * hidden]
    density_cols = jnp.broadcast_to(density_row, (LANES, hidden)).T
    in_ref[...] = in_weight
    mid_ref[...] = mid_weight
    half_weight = (0.5 * feat_weight.astype(f32)).astype(bf16)
    head_ref[...] = jnp.concatenate([half_weight, density_cols.astype(bf16)], 1)
    vec_ref[...] = vec
    weights = (in_weight, mid_ref, head_ref, vec)
    forward_slots(slots, weights, enc_ref, geometry_ref, refs[4:], refs[:4])


def forward_rest_body(in_ref, mid_ref, head_ref, vec_ref, *refs, slots):
    enc_ref, geometry_ref, *refs = refs[1:] if slots == (0,) else refs
    weights = (in_ref[...], mid_ref, head_ref, vec_ref[...])
    forward_slots(slots, weights, enc_ref, geometry_ref, refs[4:], refs[:4])


def sides(values):
    below, above = ([jnp.zeros_like(values[0])], [jnp.zeros_like(values[0])])
    for q in range(len(values) - 1):
        below.append(below[-1] + values[q])
        above.append(above[-1] + values[len(values) - 1 - q])
    return (below, above[::-1])


def gather_messages(refs, store, own, rays):
    for k, ref in enumerate(refs):
        store[own ^ k] = ref[...]
    members = [from_message(store[p], rays) for p in range(len(refs))]
    parts = [m[0] for m in members]
    depth = [m[1][0:1] + m[1][1:2] + m[1][2:3] for m in members]
    direction = members[0][1][3:4]
    below, above = sides(depth)
    trans = [jnp.exp(-jnp.where(direction < 0.5, b, a)) for b, a in zip(below, above)]
    return (parts, depth, direction, trans)


def member_at(level, quad):
    region = lax.axis_index("region")
    if level == 0:
        return lax.rem(region, quad)
    return lax.rem(lax.div(region, quad << (level - 1)), 2)


def as_columns(rows):
    columns = turned(jnp.concatenate(rows, 0), rows[0].shape[1])
    return [columns[:, i : i + 1] for i in range(len(rows))]


def weighted_sum(factors, parts):
    out = []
    for k in range(len(parts[0])):
        total = factors[0] * parts[0][k]
        for factor, part in zip(factors[1:], parts[1:]):
            total = total + factor * part[k]
        out.append(total)
    return out


def inner(left, right):
    total = left[0] * right[0]
    for a, b in zip(left[1:], right[1:]):
        total = total + a * b
    return jnp.sum(total, 1, keepdims=True)


def combine_body(*refs, rays, level, quad):
    *messages, out_ref, store = refs
    messages = messages[: quad if level == 0 else 2]
    own = member_at(level, quad)
    parts, depth, direction, trans = gather_messages(messages, store, own, rays)
    total = depth[0]
    for value in depth[1:]:
        total = total + value
    rows = jnp.concatenate([*split3(total), direction], 0)
    out_ref[...] = as_message(weighted_sum(as_columns(trans), parts), rows)


def owner_body(*refs, counts, quad):
    levels = []
    for count in counts:
        messages, refs = (refs[:count], refs[count:])
        levels.append(messages)
    target_ref, _, *refs = refs
    out_refs, stores, reply = (refs[:quad], refs[quad:-1], refs[-1])
    rays, feat = target_ref.shape
    own = [member_at(n, quad) for n in range(len(counts))]
    found = [
        gather_messages(messages, stores[n], own[n], rays) for n, messages in enumerate(levels)
    ]
    direction = found[0][2]
    parts, _, _, trans = found[-1]
    rendered = weighted_sum(as_columns(trans), parts)
    grads = [
        (value - target_ref[:, cut].astype(f32)).astype(bf16).astype(f32)
        for value, cut in zip(rendered, blocks(feat))
    ]
    lane = lanes_of((rays, LANES))
    inners = jnp.zeros((rays, LANES), f32)
    for i, value in enumerate(sum((f[0] for f in found), [])):
        inners = jnp.where(lane == i, inner(grads, value), inners)
    inners = inners.T

    def picked(values, place):
        out = values[0]
        for n, value in enumerate(values[1:]):
            out = jnp.where(place == n + 1, value, out)
        return out

    ahead = jnp.ones((1, rays), f32)
    reach = jnp.zeros((1, rays), f32)
    for n in range(len(counts) - 1, -1, -1):
        first = sum(counts[:n])
        trans = [ahead * t for t in found[n][3]]
        below, above = sides([t * inners[first + p : first + p + 1] for p, t in enumerate(trans)])
        after = [reach + jnp.where(direction < 0.5, a, b) for b, a in zip(below, above)]
        if n:
            ahead, reach = (picked(trans, own[n]), picked(after, own[n]))
    for p in range(quad):
        reply[p, :6, :rays] = jnp.concatenate([*split3(trans[p]), *split3(after[p])], 0)
    for k, out_ref in enumerate(out_refs):
        out_ref[...] = as_message(grads, reply[own[0] ^ k, :6, :rays])


def with_ones(value):
    return jnp.concatenate([value.T, jnp.ones((16, value.shape[0]), bf16)], 0)


def ready_shared_body(*refs):
    states, (enc_ref, mid_ref, head_ref, *refs) = (refs[:4], refs[4:])
    source, fetched, refs = (refs[:4], refs[4:8], refs[8:])
    enc_turned, mid_turned, head_turned, *results, sems = refs
    copies = []
    for n, (ref, place) in enumerate(zip(states, fetched)):
        copies.append(pltpu.make_async_copy(ref, place, sems.at[n]))
        copies[-1].start()
    feat = source[2].shape[2]
    mid_turned[...] = mid_ref[...].T
    head = head_ref[...].astype(f32)
    lane = lanes_of(head.shape)
    head_turned[...] = jnp.where(lane < feat, 2.0 * head, head).astype(bf16).T
    for k in range(enc_ref.shape[0]):
        enc_turned[k] = with_ones(enc_ref[k])
    ready_slots(source, results)
    for copy in copies:
        copy.wait()


def ready_body(*refs):
    count = len(refs) // 7
    for n in range(count):
        ready_slots(refs[4 * n : 4 * n + 4], refs[4 * count + 3 * n : 4 * count + 3 * n + 3])


def ready_slots(source, results):
    one_ref, two_ref, turn_ref, scalar_ref = source
    one_turned, two_turned, slope_ref = results
    samples, ray_count = scalar_ref.shape[2:]
    for i in range(one_ref.shape[0]):
        one_turned[i] = with_ones(one_ref[i])
        two_turned[i] = with_ones(two_ref[i])
        columns = turned(0.25 * scalar_ref[i, 0], ray_count)
        for j in range(samples):
            rows = slice(ray_count * j, ray_count * (j + 1))
            turn = turn_ref[i, rows, :]
            slope_ref[i, rows, :] = columns[:, j : j + 1] * (1.0 - turn * turn)


def backward_body(*refs, slots, places, sources, before, last, group_count, shapes, vec_share, shards):
    begun = not before
    messages, refs = (refs[: len(slots)], refs[len(slots) :])
    held = [[ref.at[at] for ref in refs[7 * n : 7 * n + 7]] for n, at in places]
    refs = refs[7 * sources :]
    enc_turned, mid_turned, head_turned, *refs = refs
    if not begun:
        earlier, refs = (refs[:3], refs[3:])
    if last:
        depths, (depth_ref, *outs) = (refs[: len(before)], refs[len(before) :])
    else:
        *outs, depth_ref = refs
    samples, ray_count = held[0][3].shape[1:]
    hidden = held[0][0].shape[1]
    feat = held[0][2].shape[1]
    lane = lanes_of((ray_count, LANES))
    if last:
        for ref, group in zip(depths, before):
            for i, k in enumerate(group):
                depth_ref[:, own_group(k, group_count, ray_count)] = ref[i : i + 1]
    sums = [0.0, 0.0, 0.0] if begun else [ref[...] for ref in earlier]
    grads, extras, spreads = ([], [], [])
    for i, k in enumerate(slots):
        parts, extra = from_message(messages[i][...], ray_count)
        grad = jnp.concatenate(parts, 1)
        grads.append(grad)
        extras.append(extra)
        grad_sum = jnp.sum(grad, 1, keepdims=True)
        spread = jnp.where(lane == samples, grad_sum, 0.0)
        for j in range(samples):
            rows = slice(ray_count * j, ray_count * (j + 1))
            value = jnp.sum(held[i][2][rows, :] * grad, 1, keepdims=True)
            spread = jnp.where(lane == j, value, spread)
        spreads.append(spread.T)
    extra = side_by_side(extras)
    trans = extra[0:1] + extra[1:2] + extra[2:3]
    after = extra[3:4] + extra[4:5] + extra[5:6]
    for i, k in enumerate(slots):
        cut = slice(ray_count * i, ray_count * (i + 1))
        if last:
            depth_ref[:, own_group(k, group_count, ray_count)] = -after[:, cut]
        else:
            depth_ref[i : i + 1] = -after[:, cut]
    spread = side_by_side(spreads)
    sample_grad = 0.5 * (spread[:samples] + spread[samples : samples + 1])
    local_weight, trans_after, slope = [
        side_by_side([refs_of[3][q] for refs_of in held]) for q in range(3)
    ]
    weighted = local_weight * sample_grad
    later = [jnp.zeros_like(after)]
    for j in range(samples - 1, 0, -1):
        later.append(later[-1] + weighted[j : j + 1])
    later = jnp.concatenate(later[::-1], 0)
    optical_grad = trans * (trans_after * sample_grad - later) - after
    columns = turned(jnp.concatenate([optical_grad * slope, trans], 0), after.shape[1])
    zero = jnp.zeros((), bf16)
    for i, k in enumerate(slots):
        one_ref, two_ref, _, _, one_turned, two_turned, slope_ref = held[i]
        own = columns[ray_count * i : ray_count * (i + 1)]
        grad_ahead = grads[i] * own[:, samples : samples + 1]
        pieces = []
        for j in range(samples):
            rows = slice(ray_count * j, ray_count * (j + 1))
            colour_grad = (grad_ahead * slope_ref[rows, :]).astype(bf16)
            density_part = jnp.where(lane == j, own, 0.0).astype(bf16)
            pieces.append(jnp.concatenate([colour_grad, density_part], 1))
        head_grad = jnp.concatenate(pieces, 0)
        second = product(head_grad, head_turned[...]).astype(bf16)
        sums[2] = sums[2] + product(two_turned[...], head_grad)
        second = jnp.where(two_ref[...] > 0, second, zero)
        first = product(second, mid_turned[...]).astype(bf16)
        sums[1] = sums[1] + product(one_turned[...], second)
        first = jnp.where(one_ref[...] > 0, first, zero)
        sums[0] = sums[0] + product(enc_turned[k], first)
    if not last:
        for value, ref in zip(sums, outs):
            ref[...] = value
        return
    values = [value[:-16] for value in sums]
    first_sum, second_sum, head_sum = [value[-16:-15] for value in sums]
    density_sum = jnp.sum(values[2][:, feat:].T, 0, keepdims=True)
    vec = jnp.concatenate([first_sum, second_sum, density_sum, head_sum[:, :feat]], 1)
    total = vec.shape[1]

    def write(s, ref):
        spot = 0
        for (rows, width), value in zip(shapes, values):
            for cut in blocks(width):
                ref[spot : spot + rows, :] = value[rows * s : rows * (s + 1), cut]
                spot += rows
        row = pltpu.roll(vec, total - vec_share * s, 1) if s else vec
        ref[spot : spot + 16, :] = row_block(row[:, : wide_rows(vec_share) * LANES], 16)

    if shards != 2:
        for s in range(shards):
            write(s, outs[0].at[s])
        return
    mine = lax.axis_index("rays")
    for s in range(2):

        @pl.when(mine == s)
        def _():
            write(s, outs[0])
            write(1 - s, outs[1])


def adam_body(*refs, shards):
    grad_refs, (depth_ref, *refs) = (refs[:shards], refs[shards:])
    state_refs, out_refs, depth_out = (refs[:4], refs[4:8], refs[8])
    depth_out[...] = depth_ref[...]

    def update(stacked, gradient):
        first_moment = beta_one * stacked[1] + (1.0 - beta_one) * gradient
        second = beta_two * stacked[2] + (1.0 - beta_two) * gradient * gradient
        step = first_moment / (jnp.sqrt(second * (1.0 / second_fix)) + epsilon)
        return (stacked[0] - (learn_rate / first_fix) * step, first_moment, second)

    def gathered(spot, rows):
        total = grad_refs[0][spot : spot + rows, :]
        for ref in grad_refs[1:]:
            total = total + ref[spot : spot + rows, :]
        return total

    spot = 0
    for ref, out in zip(state_refs[:3], out_refs[:3]):
        rows, width = ref.shape[2:]
        for cut in blocks(width):
            new = update([ref[i, 0, :, cut] for i in range(3)], gathered(spot, rows))
            spot += rows
            for i in range(3):
                out[i, 0, :, cut] = new[i]
    ref, out = (state_refs[3], out_refs[3])
    share = ref.shape[2]
    gradient = block_row(gathered(spot, 16), wide_rows(share))[:, :share]
    new = update([ref[i] for i in range(3)], gradient)
    for i in range(3):
        out[i] = new[i]


def shaped(shape, dtype):
    return jax.ShapeDtypeStruct(shape, dtype)


def swap(value, distance, size):
    return lax.ppermute(value, "region", [(i, i ^ distance) for i in range(size)])


def per_device(
    ray_codes,
    target,
    direction,
    entries,
    exits,
    depth_bins,
    in_layer,
    mid_layer,
    feat_layer,
    vectors,
):
    regions = lax.axis_size("region")
    shards = lax.axis_size("rays")
    samples, ray_count = depth_bins.shape[1:]
    quad = min(QUAD, regions)
    planes = regions // quad
    rays = ray_count // quad
    layers = (in_layer, mid_layer, feat_layer)
    states = (*layers, vectors)
    shapes = tuple(layer.shape[2:] for layer in layers)
    vec_share = vectors.shape[2]
    hidden = shapes[0][1]
    feat = shapes[2][1]
    code_width = ray_codes.shape[2]
    pack_rows = sum(rows * (width // LANES) for rows, width in shapes) + 16
    rows = samples * rays
    sizes = dict(shapes=shapes, vec_share=vec_share)
    pair = shards == 2
    flops = 2 * rows * (code_width * hidden + hidden * hidden + hidden * (feat + LANES))

    arguments = (*states, ray_codes, depth_bins, entries, exits, direction[None], target)
    pack, *geometric, own_target = call(
        functools.partial(fetch_body, slots=quad),
        (pltpu.VMEM((pack_rows, LANES), bf16),)
        + tuple(pltpu.VMEM(a.shape, a.dtype) for a in arguments[4:9])
        + (pltpu.VMEM((rays, feat), bf16),),
        [in_hbm(a) for a in arguments],
        16,
        scratch=[pltpu.VMEM(a.shape[1:], f32) for a in states]
        + [pltpu.SemaphoreType.DMA((10,))],
        specs=[pl.BlockSpec(memory_space=pltpu.HBM)] * 10,
    )
    if pair:
        packs = (pack, lax.ppermute(pack, "rays", [(0, 1), (1, 0)]))
    else:
        packs = (lax.all_gather(pack, "rays", axis=0),)
    encoded, geometry = call(
        functools.partial(encode_body, unit_length=depth_scale / (regions * BINS), slots=quad),
        (
            pltpu.VMEM((quad, rows, code_width), bf16),
            pltpu.VMEM((quad, samples + 8, rays), f32),
        ),
        [in_vmem(v) for v in geometric],
        16,
        scratch=[
            pltpu.VMEM((samples + 8, ray_count), f32),
            pltpu.VMEM((ray_count, LANES), f32),
        ],
        flops=10 * quad * rows * code_width,
        moved=quad * rows * code_width * 4,
    )

    message = pltpu.VMEM((rays * (feat // LANES) + 8, LANES), bf16)

    def kept_shapes(count):
        return (
            pltpu.VMEM((count, rows, hidden), bf16),
            pltpu.VMEM((count, rows, hidden), bf16),
            pltpu.VMEM((count, rows, feat), f32),
            pltpu.VMEM((count, 3, samples, rays), f32),
        )

    def moved(count):
        return count * rows * (feat + hidden) * 4

    weight_shapes = (
        pltpu.VMEM((shapes[0][0] * shards, hidden), bf16),
        pltpu.VMEM((hidden, hidden), bf16),
        pltpu.VMEM((hidden, feat + LANES), bf16),
        pltpu.VMEM((1, vec_share * shards), f32),
    )

    def forward(slots, inputs, first):
        if first:
            body = functools.partial(forward_first_body, pair=pair, slots=slots, **sizes)
        else:
            body = functools.partial(forward_rest_body, slots=slots)
        out = call(
            body,
            (weight_shapes if first else ())
            + kept_shapes(len(slots))
            + (message,) * len(slots),
            [in_vmem(v) for v in (*inputs, encoded, geometry)],
            16,
            scratch=[pltpu.VMEM((2, pack_rows, LANES), bf16)] if first and pair else (),
            flops=len(slots) * flops,
            moved=moved(len(slots)),
        )
        found, out = (out[:4], out[4:]) if first else (None, out)
        return (out[:4], list(out[4:]), found)

    groups = [(quad - 1,), tuple(range(1, quad - 1)), (0,)]
    kept, sent, weights = ([], {}, None)
    for slots in groups:
        inputs = packs if not kept else (*weights, sent[quad - 1]) if slots == (0,) else weights
        arrays, messages, found = forward(slots, inputs, not kept)
        weights = weights or found
        kept.append(arrays)
        for k, value in zip(slots, messages):
            sent[k] = swap(value, k, regions) if k else value
    quad_messages = [in_vmem(sent[k]) for k in range(quad)]
    def ready_shapes(count):
        return (
            pltpu.VMEM((count, hidden + 16, rows), bf16),
            pltpu.VMEM((count, hidden + 16, rows), bf16),
            pltpu.VMEM((count, rows, feat), f32),
        )

    hbm, vmem = (pl.BlockSpec(memory_space=m) for m in (pltpu.HBM, pltpu.VMEM))
    local = [encoded, weights[1], weights[2], *kept[0]]
    results = call(
        ready_shared_body,
        tuple(pltpu.VMEM(s.shape, f32) for s in states)
        + (
            pltpu.VMEM((quad, code_width + 16, rows), bf16),
            pltpu.VMEM((hidden, hidden), bf16),
            pltpu.VMEM((feat + LANES, hidden), bf16),
        )
        + ready_shapes(len(groups[0])),
        [in_hbm(s) for s in states] + [in_vmem(v) for v in local],
        16,
        scratch=[pltpu.SemaphoreType.DMA((4,))],
        specs=[hbm] * 4 + [vmem] * len(local),
        flops=flops,
        moved=2 * moved(1),
    )
    states_near, enc_turned, turned_weights = (results[:4], results[4], results[5:7])
    ready = [results[7:]]
    results = call(
        ready_body,
        sum((ready_shapes(len(slots)) for slots in groups[1:]), ()),
        [in_vmem(v) for v in sum(map(list, kept[1:]), [])],
        16,
        flops=(quad - 1) * flops,
        moved=2 * moved(quad - 1),
    )
    ready += [results[3 * n : 3 * n + 3] for n in range(len(groups) - 1)]
    ahead = {1: [in_vmem(turned_weights[0])]}
    levels = [quad_messages]
    for level in range(planes.bit_length() - 1):
        composite = call(
            functools.partial(combine_body, rays=rays, level=level, quad=quad),
            message,
            levels[-1] + ahead.get(level, []),
            16,
            scratch=[pltpu.VMEM((len(levels[-1]), *message.shape), bf16)],
        )
        levels.append([in_vmem(composite), in_vmem(swap(composite, quad << level, regions))])
    counts = tuple(len(level) for level in levels)
    replies = call(
        functools.partial(owner_body, counts=counts, quad=quad),
        (message,) * quad,
        sum(levels, []) + [in_vmem(v) for v in (own_target, results[0])],
        16,
        scratch=[pltpu.VMEM((count, *message.shape), bf16) for count in counts]
        + [pltpu.VMEM((quad, 8, LANES), f32)],
    )
    answers = [replies[0]] + [swap(replies[k], k, regions) for k in range(1, quad)]
    gradient_shapes = (
        pltpu.VMEM((code_width + 16, hidden), f32),
        pltpu.VMEM((hidden + 16, hidden), f32),
        pltpu.VMEM((hidden + 16, feat + LANES), f32),
    )
    earlier, depths, before = ((), [], ())
    place = {k: (n, slots.index(k)) for n, slots in enumerate(groups) for k in slots}
    steps = [(0,), (2, 1), (3,)]
    for slots in steps:
        last = slots == steps[-1]
        if last:
            share = pltpu.VMEM((pack_rows, LANES), f32)
            out_shape = (pltpu.VMEM((1, ray_count), f32), share, share)
            if not pair:
                out_shape = (out_shape[0], shaped((shards, pack_rows, LANES), f32))
        else:
            out_shape = gradient_shapes + (pltpu.VMEM((len(slots), rays), f32),)
        used = sorted({place[k][0] for k in slots})
        inputs = [answers[k] for k in slots]
        inputs += sum(([*kept[n], *ready[n]] for n in used), [])
        inputs += [enc_turned, *turned_weights, *earlier] + (depths if last else [])
        out = call(
            functools.partial(
                backward_body,
                slots=slots,
                places=tuple((used.index(place[k][0]), place[k][1]) for k in slots),
                sources=len(used),
                before=before,
                last=last,
                group_count=quad,
                shards=shards,
                **sizes,
            ),
            out_shape,
            [in_vmem(v) for v in inputs],
            24,
            flops=2 * len(slots) * flops,
            moved=moved(len(slots)),
        )
        earlier, before = (out[:3], before + (slots,))
        if not last:
            depths.append(out[3])
    depth_grad, *grads = out
    if pair:
        parts = (grads[0], lax.ppermute(grads[1], "rays", [(0, 1), (1, 0)]))
    else:
        exchanged = lax.all_to_all(grads[0], "rays", 0, 0)
        parts = tuple(exchanged[s] for s in range(shards))
    return call(
        functools.partial(adam_body, shards=shards),
        tuple(shaped(s.shape, f32) for s in states) + (shaped(depth_grad.shape, f32),),
        [in_vmem(v) for v in (*parts, depth_grad, *states_near)],
        16,
    )


def solution(mesh):
    placed = (
        P(None, "rays", None),
        P("rays", None),
        P("rays"),
        P("region", "rays"),
        P("region", "rays"),
        P("region", None, "rays"),
        P(None, "region", "rays", None),
        P(None, "region", "rays", None),
        P(None, "region", "rays", None),
        P(None, "region", "rays"),
    )
    return jax.shard_map(
        per_device,
        mesh=mesh,
        in_specs=placed,
        out_specs=(
            P(None, "region", "rays", None),
            P(None, "region", "rays", None),
            P(None, "region", "rays", None),
            P(None, "region", "rays"),
            P("region", "rays"),
        ),
        check_vma=False,
    )
```

```python
import functools

import jax
import jax.numpy as jnp
from jax import lax
from jax.experimental import pallas as pl
from jax.experimental.pallas import tpu as pltpu
from jax.sharding import PartitionSpec as P

BINS = 64
LANES = 128
QUAD = 4

depth_scale = 4.0
beta_one = 0.9
beta_two = 0.999
learn_rate = 0.001
epsilon = 1e-08
first_fix = 1.0 - 0.9**10
second_fix = 1.0 - 0.999**10

f32 = jnp.float32
bf16 = jnp.bfloat16


def in_vmem(value):
    return pltpu.with_memory_space_constraint(value, pltpu.VMEM)


def in_hbm(value):
    return pltpu.with_memory_space_constraint(value, pltpu.HBM)


def call(body, out_shape, inputs, limit, scratch=(), specs=None, flops=1000000, moved=1000000):
    many = isinstance(out_shape, (tuple, list))
    spec = pl.BlockSpec(memory_space=pltpu.VMEM)
    return pl.pallas_call(
        body,
        out_shape=out_shape,
        in_specs=specs or [spec] * len(inputs),
        out_specs=tuple(spec for _ in out_shape) if many else spec,
        scratch_shapes=list(scratch),
        compiler_params=pltpu.CompilerParams(vmem_limit_bytes=limit * 1024 * 1024),
        cost_estimate=pl.CostEstimate(flops=flops, bytes_accessed=moved, transcendentals=0),
    )(*inputs)


def blocks(width):
    return [slice(LANES * k, LANES * (k + 1)) for k in range(width // LANES)]


def wide_rows(count):
    return -(-count // LANES)


def row_block(row, rows):
    width = row.shape[1]
    padded = wide_rows(width) * LANES
    if padded != width:
        row = jnp.concatenate([row, jnp.zeros((1, padded - width), f32)], 1)
    place = lax.broadcasted_iota(jnp.int32, (rows, LANES), 0)
    out = jnp.zeros((rows, LANES), f32)
    for k, cut in enumerate(blocks(padded)):
        out = jnp.where(place == k, jnp.broadcast_to(row[:, cut], (rows, LANES)), out)
    return out


def block_row(block, count):
    return jnp.concatenate([block[k : k + 1] for k in range(count)], 1)


def split3(value):
    high = value.astype(bf16).astype(f32)
    rest = value - high
    mid = rest.astype(bf16).astype(f32)
    return (high, mid, rest - mid)


def lanes_of(shape):
    return lax.broadcasted_iota(jnp.int32, shape, 1)


def turned(rows, ray_count):
    fill = LANES - rows.shape[0]
    return jnp.concatenate([rows, jnp.zeros((fill, ray_count), f32)], 0).T


def own_group(k, slots, rows):
    place = lax.rem(lax.axis_index("region"), slots) ^ k
    return pl.ds(pl.multiple_of(place * rows, rows), rows)


def fetch_body(*refs, slots):
    ins, (pack_ref, *refs) = (refs[:10], refs[10:])
    outs, held, sems = (refs[:6], refs[6:10], refs[10])
    target_ref = outs[5]
    copies = []

    def fetch(source, place):
        copies.append(pltpu.make_async_copy(source, place, sems.at[len(copies)]))
        copies[-1].start()

    for ref, hold in zip(ins[:4], held):
        fetch(ref.at[0], hold)
    for ref, out in zip(ins[4:9], outs):
        fetch(ref, out)
    fetch(ins[9].at[own_group(0, slots, target_ref.shape[0])], target_ref)
    spot = 0
    for copy, hold in zip(copies[:3], held[:3]):
        copy.wait()
        rows, width = hold.shape[1:]
        for cut in blocks(width):
            pack_ref[spot : spot + rows, :] = hold[0, :, cut].astype(bf16)
            spot += rows
    copies[3].wait()
    pack_ref[spot : spot + 16, :] = row_block(held[3][...], 16).astype(bf16)
    for copy in copies[4:]:
        copy.wait()


def encode_body(*refs, unit_length, slots):
    codes, bins, entry, exit_, direction, enc_ref, geometry_ref, *refs = refs
    flat_geometry, flat_position = refs
    bins = bins[0].astype(f32)
    samples, ray_count = bins.shape
    group_rows = ray_count // slots
    slot = lax.broadcasted_iota(jnp.int32, bins.shape, 0)
    following = jnp.where(slot == samples - 1, float(BINS), pltpu.roll(bins, samples - 1, 0))
    inside = ((slot >= entry[...]) & (slot < exit_[...])).astype(f32)
    flat_geometry[:samples] = (following - bins) * unit_length * inside
    flat_geometry[samples : samples + 1] = direction[...].astype(f32)
    flat_position[...] = turned((bins + 0.5) / BINS, ray_count)
    for k in range(slots):
        group = own_group(k, slots, group_rows)
        geometry_ref[k] = flat_geometry[:, group]
        code_zero = codes[0, group].astype(f32)
        code_one = codes[1, group].astype(f32)
        position = flat_position[group, :]
        for j in range(samples):
            encoded = code_zero + position[:, j : j + 1] * code_one
            enc_ref[k, group_rows * j : group_rows * (j + 1), :] = encoded.astype(bf16)


def assemble(packs, shapes, vec_share):
    shards = len(packs)
    spot = 0
    mats = []
    for rows, width in shapes:
        pieces = []
        for cut in blocks(width):
            pieces.append(jnp.concatenate([p[spot : spot + rows, :] for p in packs], 0))
            spot += rows
        mats.append(jnp.concatenate(pieces, 1))
    vec_total = vec_share * shards
    vec = jnp.zeros((1, vec_total), f32)
    for s, p in enumerate(packs):
        block = p[spot : spot + 16, :].astype(f32)
        count = wide_rows(vec_share)
        row = block_row(block, count)
        fill = vec_total - count * LANES
        if fill:
            row = jnp.concatenate([row, jnp.zeros((1, fill), f32)], 1)
        if s:
            row = pltpu.roll(row, vec_share * s, 1)
        vec = vec + row
    return (*mats, vec)


def product(left, right):
    return jnp.dot(left, right, preferred_element_type=f32)


def forward_slots(slots, weights, enc_ref, geometry_ref, message_refs, kept):
    in_weight, mid_ref, head_ref, vec = weights
    one_ref, two_ref, turn_ref, scalar_ref = kept
    samples, ray_count = scalar_ref.shape[2:]
    hidden = mid_ref.shape[0]
    feat = turn_ref.shape[2]
    bias_one = vec[:, :hidden]
    bias_two = vec[:, hidden : 2 * hidden]
    half_bias = 0.5 * vec[:, 3 * hidden :]
    lane = lanes_of((ray_count, LANES))
    ones, twos, densities = ([], [], [])
    for i, k in enumerate(slots):
        one = product(enc_ref[k], in_weight) + bias_one
        ones.append(jnp.maximum(one, 0.0).astype(bf16))
        one_ref[i] = ones[i]
    for i in range(len(slots)):
        two = product(ones[i], mid_ref[...]) + bias_two
        twos.append(jnp.maximum(two, 0.0).astype(bf16))
        two_ref[i] = twos[i]
    raws = [product(two, head_ref[:, feat:]) for two in twos]
    for raw in raws:
        density = jnp.zeros((ray_count, LANES), f32)
        for j in range(samples):
            rows = slice(ray_count * j, ray_count * (j + 1))
            density = jnp.where(lane == j, raw[rows], density)
        densities.append(density)
    for i in range(len(slots)):
        turn_ref[i] = jnp.tanh(product(twos[i], head_ref[:, :feat]) + half_bias)
    density = side_by_side([value.T[:samples] for value in densities])
    geometry = side_by_side([geometry_ref[k, :samples] for k in slots])
    direction = side_by_side([geometry_ref[k, samples : samples + 1] for k in slots])
    soft = jnp.maximum(density, 0.0) + jnp.log1p(jnp.exp(-jnp.abs(density)))
    optical = soft * geometry
    before = [jnp.zeros_like(direction)]
    for j in range(samples):
        before.append(before[-1] + optical[j : j + 1])
    depth = before.pop()
    optical_before = jnp.concatenate(before, 0)
    opacity = jnp.tanh(0.5 * optical) * (1.0 + jnp.exp(-optical))
    local_weight = jnp.exp(-optical_before) * opacity
    half_weight = 0.5 * local_weight
    half_sum = jnp.sum(half_weight, 0, keepdims=True)
    columns = turned(jnp.concatenate([half_weight, half_sum], 0), depth.shape[1])
    shared = jnp.concatenate([*split3(depth), direction], 0)
    sig = 0.5 * jnp.tanh(0.5 * density) + 0.5
    scalars = (local_weight, jnp.exp(-(optical_before + optical)), geometry * sig)
    for i, k in enumerate(slots):
        cut = slice(ray_count * i, ray_count * (i + 1))
        for q, value in enumerate(scalars):
            scalar_ref[i, q] = value[:, cut]
        own = columns[cut]
        total = jnp.zeros((ray_count, feat), f32) + own[:, samples : samples + 1]
        for j in range(samples):
            rows = slice(ray_count * j, ray_count * (j + 1))
            total = total + own[:, j : j + 1] * turn_ref[i, rows, :]
        message_refs[i][...] = as_message([total[:, k] for k in blocks(feat)], shared[:, cut])


def side_by_side(values):
    return jnp.concatenate(values, 1) if len(values) > 1 else values[0]


def as_message(parts, rows):
    count, rays = rows.shape
    if count < 8:
        rows = jnp.concatenate([rows, jnp.zeros((8 - count, rays), f32)], 0)
    if rays < LANES:
        rows = jnp.concatenate([rows, jnp.zeros((8, LANES - rays), f32)], 1)
    return jnp.concatenate([*parts, rows], 0).astype(bf16)


def from_message(value, rays):
    value = value.astype(f32)
    count = value.shape[0] // rays
    parts = [value[rays * k : rays * (k + 1)] for k in range(count)]
    return (parts, value[rays * count :, :rays])


def forward_first_body(*refs, shapes, vec_share, pair, slots):
    both = None
    if pair:
        own_ref, other_ref, *refs, both = refs
        mine = lax.axis_index("rays")
        both[mine] = own_ref[...]
        both[1 - mine] = other_ref[...]
        packs = [both.at[0], both.at[1]]
    else:
        packs_ref, *refs = refs
        packs = [packs_ref.at[s] for s in range(packs_ref.shape[0])]
    enc_ref, geometry_ref, in_ref, mid_ref, head_ref, vec_ref, *refs = refs
    hidden = mid_ref.shape[0]
    in_weight, mid_weight, feat_weight, vec = assemble(packs, shapes, vec_share)
    density_row = vec[:, 2 * hidden : 3 * hidden]
    density_cols = jnp.broadcast_to(density_row, (LANES, hidden)).T
    in_ref[...] = in_weight
    mid_ref[...] = mid_weight
    half_weight = (0.5 * feat_weight.astype(f32)).astype(bf16)
    head_ref[...] = jnp.concatenate([half_weight, density_cols.astype(bf16)], 1)
    vec_ref[...] = vec
    weights = (in_weight, mid_ref, head_ref, vec)
    forward_slots(slots, weights, enc_ref, geometry_ref, refs[4:], refs[:4])


def forward_rest_body(in_ref, mid_ref, head_ref, vec_ref, *refs, slots):
    enc_ref, geometry_ref, *refs = refs[1:] if slots == (0,) else refs
    weights = (in_ref[...], mid_ref, head_ref, vec_ref[...])
    forward_slots(slots, weights, enc_ref, geometry_ref, refs[4:], refs[:4])


def sides(values):
    below, above = ([jnp.zeros_like(values[0])], [jnp.zeros_like(values[0])])
    for q in range(len(values) - 1):
        below.append(below[-1] + values[q])
        above.append(above[-1] + values[len(values) - 1 - q])
    return (below, above[::-1])


def gather_messages(refs, store, own, rays):
    for k, ref in enumerate(refs):
        store[own ^ k] = ref[...]
    members = [from_message(store[p], rays) for p in range(len(refs))]
    parts = [m[0] for m in members]
    depth = [m[1][0:1] + m[1][1:2] + m[1][2:3] for m in members]
    direction = members[0][1][3:4]
    below, above = sides(depth)
    trans = [jnp.exp(-jnp.where(direction < 0.5, b, a)) for b, a in zip(below, above)]
    return (parts, depth, direction, trans)


def member_at(level, quad):
    region = lax.axis_index("region")
    if level == 0:
        return lax.rem(region, quad)
    return lax.rem(lax.div(region, quad << (level - 1)), 2)


def as_columns(rows):
    columns = turned(jnp.concatenate(rows, 0), rows[0].shape[1])
    return [columns[:, i : i + 1] for i in range(len(rows))]


def weighted_sum(factors, parts):
    out = []
    for k in range(len(parts[0])):
        total = factors[0] * parts[0][k]
        for factor, part in zip(factors[1:], parts[1:]):
            total = total + factor * part[k]
        out.append(total)
    return out


def inner(left, right):
    total = left[0] * right[0]
    for a, b in zip(left[1:], right[1:]):
        total = total + a * b
    return jnp.sum(total, 1, keepdims=True)


def combine_body(*refs, rays, level, quad):
    *messages, out_ref, store = refs
    messages = messages[: quad if level == 0 else 2]
    own = member_at(level, quad)
    parts, depth, direction, trans = gather_messages(messages, store, own, rays)
    total = depth[0]
    for value in depth[1:]:
        total = total + value
    rows = jnp.concatenate([*split3(total), direction], 0)
    out_ref[...] = as_message(weighted_sum(as_columns(trans), parts), rows)


def owner_body(*refs, counts, quad):
    levels = []
    for count in counts:
        messages, refs = (refs[:count], refs[count:])
        levels.append(messages)
    target_ref, _, *refs = refs
    out_refs, stores, reply = (refs[:quad], refs[quad:-1], refs[-1])
    rays, feat = target_ref.shape
    own = [member_at(n, quad) for n in range(len(counts))]
    found = [
        gather_messages(messages, stores[n], own[n], rays) for n, messages in enumerate(levels)
    ]
    direction = found[0][2]
    parts, _, _, trans = found[-1]
    rendered = weighted_sum(as_columns(trans), parts)
    grads = [
        (value - target_ref[:, cut].astype(f32)).astype(bf16).astype(f32)
        for value, cut in zip(rendered, blocks(feat))
    ]
    lane = lanes_of((rays, LANES))
    inners = jnp.zeros((rays, LANES), f32)
    for i, value in enumerate(sum((f[0] for f in found), [])):
        inners = jnp.where(lane == i, inner(grads, value), inners)
    inners = inners.T

    def picked(values, place):
        out = values[0]
        for n, value in enumerate(values[1:]):
            out = jnp.where(place == n + 1, value, out)
        return out

    ahead = jnp.ones((1, rays), f32)
    reach = jnp.zeros((1, rays), f32)
    for n in range(len(counts) - 1, -1, -1):
        first = sum(counts[:n])
        trans = [ahead * t for t in found[n][3]]
        below, above = sides([t * inners[first + p : first + p + 1] for p, t in enumerate(trans)])
        after = [reach + jnp.where(direction < 0.5, a, b) for b, a in zip(below, above)]
        if n:
            ahead, reach = (picked(trans, own[n]), picked(after, own[n]))
    for p in range(quad):
        reply[p, :6, :rays] = jnp.concatenate([*split3(trans[p]), *split3(after[p])], 0)
    for k, out_ref in enumerate(out_refs):
        out_ref[...] = as_message(grads, reply[own[0] ^ k, :6, :rays])


def with_ones(value):
    return jnp.concatenate([value.T, jnp.ones((16, value.shape[0]), bf16)], 0)


def ready_shared_body(*refs):
    states, (enc_ref, mid_ref, head_ref, *refs) = (refs[:4], refs[4:])
    source, fetched, refs = (refs[:4], refs[4:8], refs[8:])
    enc_turned, mid_turned, head_turned, *results, sems = refs
    copies = []
    for n, (ref, place) in enumerate(zip(states, fetched)):
        copies.append(pltpu.make_async_copy(ref, place, sems.at[n]))
        copies[-1].start()
    feat = source[2].shape[2]
    mid_turned[...] = mid_ref[...].T
    head = head_ref[...].astype(f32)
    lane = lanes_of(head.shape)
    head_turned[...] = jnp.where(lane < feat, 2.0 * head, head).astype(bf16).T
    for k in range(enc_ref.shape[0]):
        enc_turned[k] = with_ones(enc_ref[k])
    ready_slots(source, results)
    for copy in copies:
        copy.wait()


def ready_body(*refs):
    count = len(refs) // 7
    for n in range(count):
        ready_slots(refs[4 * n : 4 * n + 4], refs[4 * count + 3 * n : 4 * count + 3 * n + 3])


def ready_slots(source, results):
    one_ref, two_ref, turn_ref, scalar_ref = source
    one_turned, two_turned, slope_ref = results
    samples, ray_count = scalar_ref.shape[2:]
    for i in range(one_ref.shape[0]):
        one_turned[i] = with_ones(one_ref[i])
        two_turned[i] = with_ones(two_ref[i])
        columns = turned(0.25 * scalar_ref[i, 0], ray_count)
        for j in range(samples):
            rows = slice(ray_count * j, ray_count * (j + 1))
            turn = turn_ref[i, rows, :]
            slope_ref[i, rows, :] = columns[:, j : j + 1] * (1.0 - turn * turn)


def backward_body(*refs, slots, places, sources, before, last, group_count, shapes, vec_share, shards):
    begun = not before
    messages, refs = (refs[: len(slots)], refs[len(slots) :])
    held = [[ref.at[at] for ref in refs[7 * n : 7 * n + 7]] for n, at in places]
    refs = refs[7 * sources :]
    enc_turned, mid_turned, head_turned, *refs = refs
    if not begun:
        earlier, refs = (refs[:3], refs[3:])
    if last:
        depths, (depth_ref, *outs) = (refs[: len(before)], refs[len(before) :])
    else:
        *outs, depth_ref = refs
    samples, ray_count = held[0][3].shape[1:]
    hidden = held[0][0].shape[1]
    feat = held[0][2].shape[1]
    lane = lanes_of((ray_count, LANES))
    if last:
        for ref, group in zip(depths, before):
            for i, k in enumerate(group):
                depth_ref[:, own_group(k, group_count, ray_count)] = ref[i : i + 1]
    sums = [0.0, 0.0, 0.0] if begun else [ref[...] for ref in earlier]
    grads, extras, spreads = ([], [], [])
    for i, k in enumerate(slots):
        parts, extra = from_message(messages[i][...], ray_count)
        grad = jnp.concatenate(parts, 1)
        grads.append(grad)
        extras.append(extra)
        grad_sum = jnp.sum(grad, 1, keepdims=True)
        spread = jnp.where(lane == samples, grad_sum, 0.0)
        for j in range(samples):
            rows = slice(ray_count * j, ray_count * (j + 1))
            value = jnp.sum(held[i][2][rows, :] * grad, 1, keepdims=True)
            spread = jnp.where(lane == j, value, spread)
        spreads.append(spread.T)
    extra = side_by_side(extras)
    trans = extra[0:1] + extra[1:2] + extra[2:3]
    after = extra[3:4] + extra[4:5] + extra[5:6]
    for i, k in enumerate(slots):
        cut = slice(ray_count * i, ray_count * (i + 1))
        if last:
            depth_ref[:, own_group(k, group_count, ray_count)] = -after[:, cut]
        else:
            depth_ref[i : i + 1] = -after[:, cut]
    spread = side_by_side(spreads)
    sample_grad = 0.5 * (spread[:samples] + spread[samples : samples + 1])
    local_weight, trans_after, slope = [
        side_by_side([refs_of[3][q] for refs_of in held]) for q in range(3)
    ]
    weighted = local_weight * sample_grad
    later = [jnp.zeros_like(after)]
    for j in range(samples - 1, 0, -1):
        later.append(later[-1] + weighted[j : j + 1])
    later = jnp.concatenate(later[::-1], 0)
    optical_grad = trans * (trans_after * sample_grad - later) - after
    columns = turned(jnp.concatenate([optical_grad * slope, trans], 0), after.shape[1])
    zero = jnp.zeros((), bf16)
    for i, k in enumerate(slots):
        one_ref, two_ref, _, _, one_turned, two_turned, slope_ref = held[i]
        own = columns[ray_count * i : ray_count * (i + 1)]
        grad_ahead = grads[i] * own[:, samples : samples + 1]
        pieces = []
        for j in range(samples):
            rows = slice(ray_count * j, ray_count * (j + 1))
            colour_grad = (grad_ahead * slope_ref[rows, :]).astype(bf16)
            density_part = jnp.where(lane == j, own, 0.0).astype(bf16)
            pieces.append(jnp.concatenate([colour_grad, density_part], 1))
        head_grad = jnp.concatenate(pieces, 0)
        second = product(head_grad, head_turned[...]).astype(bf16)
        sums[2] = sums[2] + product(two_turned[...], head_grad)
        second = jnp.where(two_ref[...] > 0, second, zero)
        first = product(second, mid_turned[...]).astype(bf16)
        sums[1] = sums[1] + product(one_turned[...], second)
        first = jnp.where(one_ref[...] > 0, first, zero)
        sums[0] = sums[0] + product(enc_turned[k], first)
    if not last:
        for value, ref in zip(sums, outs):
            ref[...] = value
        return
    values = [value[:-16] for value in sums]
    first_sum, second_sum, head_sum = [value[-16:-15] for value in sums]
    density_sum = jnp.sum(values[2][:, feat:].T, 0, keepdims=True)
    vec = jnp.concatenate([first_sum, second_sum, density_sum, head_sum[:, :feat]], 1)
    total = vec.shape[1]

    def write(s, ref, rest=None):
        spot = 0
        for n, ((rows, width), value) in enumerate(zip(shapes, values)):
            if n == 2 and rest is not None:
                ref, spot = (rest, 0)
            for cut in blocks(width):
                ref[spot : spot + rows, :] = value[rows * s : rows * (s + 1), cut]
                spot += rows
        row = pltpu.roll(vec, total - vec_share * s, 1) if s else vec
        ref[spot : spot + 16, :] = row_block(row[:, : wide_rows(vec_share) * LANES], 16)

    if shards != 2:
        for s in range(shards):
            write(s, outs[0].at[s])
        return
    mine = lax.axis_index("rays")
    for s in range(2):

        @pl.when(mine == s)
        def _():
            write(s, outs[0])
            write(1 - s, outs[1], outs[2])


def adam_body(*refs, shards):
    count = 3 if shards == 2 else shards
    grad_refs, (depth_ref, *refs) = (refs[:count], refs[count:])
    split = grad_refs[1].shape[0]
    state_refs, out_refs, depth_out = (refs[:4], refs[4:8], refs[8])
    depth_out[...] = depth_ref[...]

    def update(stacked, gradient):
        first_moment = beta_one * stacked[1] + (1.0 - beta_one) * gradient
        second = beta_two * stacked[2] + (1.0 - beta_two) * gradient * gradient
        step = first_moment / (jnp.sqrt(second * (1.0 / second_fix)) + epsilon)
        return (stacked[0] - (learn_rate / first_fix) * step, first_moment, second)

    def gathered(spot, rows):
        total = grad_refs[0][spot : spot + rows, :]
        if shards == 2:
            ref, first = (grad_refs[1], spot) if spot < split else (grad_refs[2], spot - split)
            return total + ref[first : first + rows, :]
        for ref in grad_refs[1:]:
            total = total + ref[spot : spot + rows, :]
        return total

    spot = 0
    for ref, out in zip(state_refs[:3], out_refs[:3]):
        rows, width = ref.shape[2:]
        for cut in blocks(width):
            new = update([ref[i, 0, :, cut] for i in range(3)], gathered(spot, rows))
            spot += rows
            for i in range(3):
                out[i, 0, :, cut] = new[i]
    ref, out = (state_refs[3], out_refs[3])
    share = ref.shape[2]
    gradient = block_row(gathered(spot, 16), wide_rows(share))[:, :share]
    new = update([ref[i] for i in range(3)], gradient)
    for i in range(3):
        out[i] = new[i]


def shaped(shape, dtype):
    return jax.ShapeDtypeStruct(shape, dtype)


def swap(value, distance, size):
    return lax.ppermute(value, "region", [(i, i ^ distance) for i in range(size)])


def per_device(
    ray_codes,
    target,
    direction,
    entries,
    exits,
    depth_bins,
    in_layer,
    mid_layer,
    feat_layer,
    vectors,
):
    regions = lax.axis_size("region")
    shards = lax.axis_size("rays")
    samples, ray_count = depth_bins.shape[1:]
    quad = min(QUAD, regions)
    planes = regions // quad
    rays = ray_count // quad
    layers = (in_layer, mid_layer, feat_layer)
    states = (*layers, vectors)
    shapes = tuple(layer.shape[2:] for layer in layers)
    vec_share = vectors.shape[2]
    hidden = shapes[0][1]
    feat = shapes[2][1]
    code_width = ray_codes.shape[2]
    pack_rows = sum(rows * (width // LANES) for rows, width in shapes) + 16
    rows = samples * rays
    sizes = dict(shapes=shapes, vec_share=vec_share)
    pair = shards == 2
    flops = 2 * rows * (code_width * hidden + hidden * hidden + hidden * (feat + LANES))

    arguments = (*states, ray_codes, depth_bins, entries, exits, direction[None], target)
    pack, *geometric, own_target = call(
        functools.partial(fetch_body, slots=quad),
        (pltpu.VMEM((pack_rows, LANES), bf16),)
        + tuple(pltpu.VMEM(a.shape, a.dtype) for a in arguments[4:9])
        + (pltpu.VMEM((rays, feat), bf16),),
        [in_hbm(a) for a in arguments],
        16,
        scratch=[pltpu.VMEM(a.shape[1:], f32) for a in states]
        + [pltpu.SemaphoreType.DMA((10,))],
        specs=[pl.BlockSpec(memory_space=pltpu.HBM)] * 10,
    )
    if pair:
        packs = (pack, lax.ppermute(pack, "rays", [(0, 1), (1, 0)]))
    else:
        packs = (lax.all_gather(pack, "rays", axis=0),)
    encoded, geometry = call(
        functools.partial(encode_body, unit_length=depth_scale / (regions * BINS), slots=quad),
        (
            pltpu.VMEM((quad, rows, code_width), bf16),
            pltpu.VMEM((quad, samples + 8, rays), f32),
        ),
        [in_vmem(v) for v in geometric],
        16,
        scratch=[
            pltpu.VMEM((samples + 8, ray_count), f32),
            pltpu.VMEM((ray_count, LANES), f32),
        ],
        flops=10 * quad * rows * code_width,
        moved=quad * rows * code_width * 4,
    )

    message = pltpu.VMEM((rays * (feat // LANES) + 8, LANES), bf16)

    def kept_shapes(count):
        return (
            pltpu.VMEM((count, rows, hidden), bf16),
            pltpu.VMEM((count, rows, hidden), bf16),
            pltpu.VMEM((count, rows, feat), f32),
            pltpu.VMEM((count, 3, samples, rays), f32),
        )

    def moved(count):
        return count * rows * (feat + hidden) * 4

    weight_shapes = (
        pltpu.VMEM((shapes[0][0] * shards, hidden), bf16),
        pltpu.VMEM((hidden, hidden), bf16),
        pltpu.VMEM((hidden, feat + LANES), bf16),
        pltpu.VMEM((1, vec_share * shards), f32),
    )

    def forward(slots, inputs, first):
        if first:
            body = functools.partial(forward_first_body, pair=pair, slots=slots, **sizes)
        else:
            body = functools.partial(forward_rest_body, slots=slots)
        out = call(
            body,
            (weight_shapes if first else ())
            + kept_shapes(len(slots))
            + (message,) * len(slots),
            [in_vmem(v) for v in (*inputs, encoded, geometry)],
            16,
            scratch=[pltpu.VMEM((2, pack_rows, LANES), bf16)] if first and pair else (),
            flops=len(slots) * flops,
            moved=moved(len(slots)),
        )
        found, out = (out[:4], out[4:]) if first else (None, out)
        return (out[:4], list(out[4:]), found)

    groups = [(quad - 1,), tuple(range(1, quad - 1)), (0,)]
    kept, sent, weights = ([], {}, None)
    for slots in groups:
        inputs = packs if not kept else (*weights, sent[quad - 1]) if slots == (0,) else weights
        arrays, messages, found = forward(slots, inputs, not kept)
        weights = weights or found
        kept.append(arrays)
        for k, value in zip(slots, messages):
            sent[k] = swap(value, k, regions) if k else value
    quad_messages = [in_vmem(sent[k]) for k in range(quad)]
    def ready_shapes(count):
        return (
            pltpu.VMEM((count, hidden + 16, rows), bf16),
            pltpu.VMEM((count, hidden + 16, rows), bf16),
            pltpu.VMEM((count, rows, feat), f32),
        )

    hbm, vmem = (pl.BlockSpec(memory_space=m) for m in (pltpu.HBM, pltpu.VMEM))
    local = [encoded, weights[1], weights[2], *kept[0]]
    results = call(
        ready_shared_body,
        tuple(pltpu.VMEM(s.shape, f32) for s in states)
        + (
            pltpu.VMEM((quad, code_width + 16, rows), bf16),
            pltpu.VMEM((hidden, hidden), bf16),
            pltpu.VMEM((feat + LANES, hidden), bf16),
        )
        + ready_shapes(len(groups[0])),
        [in_hbm(s) for s in states] + [in_vmem(v) for v in local],
        16,
        scratch=[pltpu.SemaphoreType.DMA((4,))],
        specs=[hbm] * 4 + [vmem] * len(local),
        flops=flops,
        moved=2 * moved(1),
    )
    states_near, enc_turned, turned_weights = (results[:4], results[4], results[5:7])
    ready = [results[7:]]
    results = call(
        ready_body,
        sum((ready_shapes(len(slots)) for slots in groups[1:]), ()),
        [in_vmem(v) for v in sum(map(list, kept[1:]), [])],
        16,
        flops=(quad - 1) * flops,
        moved=2 * moved(quad - 1),
    )
    ready += [results[3 * n : 3 * n + 3] for n in range(len(groups) - 1)]
    ahead = {1: [in_vmem(turned_weights[0])]}
    levels = [quad_messages]
    for level in range(planes.bit_length() - 1):
        composite = call(
            functools.partial(combine_body, rays=rays, level=level, quad=quad),
            message,
            levels[-1] + ahead.get(level, []),
            16,
            scratch=[pltpu.VMEM((len(levels[-1]), *message.shape), bf16)],
        )
        levels.append([in_vmem(composite), in_vmem(swap(composite, quad << level, regions))])
    counts = tuple(len(level) for level in levels)
    replies = call(
        functools.partial(owner_body, counts=counts, quad=quad),
        (message,) * quad,
        sum(levels, []) + [in_vmem(v) for v in (own_target, results[0])],
        16,
        scratch=[pltpu.VMEM((count, *message.shape), bf16) for count in counts]
        + [pltpu.VMEM((quad, 8, LANES), f32)],
    )
    answers = [replies[0]] + [swap(replies[k], k, regions) for k in range(1, quad)]
    gradient_shapes = (
        pltpu.VMEM((code_width + 16, hidden), f32),
        pltpu.VMEM((hidden + 16, hidden), f32),
        pltpu.VMEM((hidden + 16, feat + LANES), f32),
    )
    earlier, depths, before = ((), [], ())
    place = {k: (n, slots.index(k)) for n, slots in enumerate(groups) for k in slots}
    steps = [(0,), (2, 1), (3,)]
    for slots in steps:
        last = slots == steps[-1]
        if last:
            share = pltpu.VMEM((pack_rows, LANES), f32)
            near_rows = sum(rows * (width // LANES) for rows, width in shapes[:2])
            sent_shapes = [
                pltpu.VMEM((n, LANES), f32) for n in (near_rows, pack_rows - near_rows)
            ]
            out_shape = (pltpu.VMEM((1, ray_count), f32), share, *sent_shapes)
            if not pair:
                out_shape = (out_shape[0], shaped((shards, pack_rows, LANES), f32))
        else:
            out_shape = gradient_shapes + (pltpu.VMEM((len(slots), rays), f32),)
        used = sorted({place[k][0] for k in slots})
        inputs = [answers[k] for k in slots]
        inputs += sum(([*kept[n], *ready[n]] for n in used), [])
        inputs += [enc_turned, *turned_weights, *earlier] + (depths if last else [])
        out = call(
            functools.partial(
                backward_body,
                slots=slots,
                places=tuple((used.index(place[k][0]), place[k][1]) for k in slots),
                sources=len(used),
                before=before,
                last=last,
                group_count=quad,
                shards=shards,
                **sizes,
            ),
            out_shape,
            [in_vmem(v) for v in inputs],
            24,
            flops=2 * len(slots) * flops,
            moved=moved(len(slots)),
        )
        earlier, before = (out[:3], before + (slots,))
        if not last:
            depths.append(out[3])
    depth_grad, *grads = out
    if pair:
        parts = [grads[0]]
        parts += [lax.ppermute(value, "rays", [(0, 1), (1, 0)]) for value in grads[1:]]
    else:
        exchanged = lax.all_to_all(grads[0], "rays", 0, 0)
        parts = tuple(exchanged[s] for s in range(shards))
    return call(
        functools.partial(adam_body, shards=shards),
        tuple(shaped(s.shape, f32) for s in states) + (shaped(depth_grad.shape, f32),),
        [in_vmem(v) for v in (*parts, depth_grad, *states_near)],
        16,
    )


def solution(mesh):
    placed = (
        P(None, "rays", None),
        P("rays", None),
        P("rays"),
        P("region", "rays"),
        P("region", "rays"),
        P("region", None, "rays"),
        P(None, "region", "rays", None),
        P(None, "region", "rays", None),
        P(None, "region", "rays", None),
        P(None, "region", "rays"),
    )
    return jax.shard_map(
        per_device,
        mesh=mesh,
        in_specs=placed,
        out_specs=(
            P(None, "region", "rays", None),
            P(None, "region", "rays", None),
            P(None, "region", "rays", None),
            P(None, "region", "rays"),
            P("region", "rays"),
        ),
        check_vma=False,
    )
```

```python
import functools

import jax
import jax.numpy as jnp
from jax import lax
from jax.experimental import pallas as pl
from jax.experimental.pallas import tpu as pltpu
from jax.sharding import PartitionSpec as P

BINS = 64
LANES = 128
QUAD = 4

depth_scale = 4.0
beta_one = 0.9
beta_two = 0.999
learn_rate = 0.001
epsilon = 1e-08
first_fix = 1.0 - 0.9**10
second_fix = 1.0 - 0.999**10

f32 = jnp.float32
bf16 = jnp.bfloat16


def in_vmem(value):
    return pltpu.with_memory_space_constraint(value, pltpu.VMEM)


def in_hbm(value):
    return pltpu.with_memory_space_constraint(value, pltpu.HBM)


def call(body, out_shape, inputs, limit, scratch=(), specs=None, flops=1000000, moved=1000000):
    many = isinstance(out_shape, (tuple, list))
    spec = pl.BlockSpec(memory_space=pltpu.VMEM)
    return pl.pallas_call(
        body,
        out_shape=out_shape,
        in_specs=specs or [spec] * len(inputs),
        out_specs=tuple(spec for _ in out_shape) if many else spec,
        scratch_shapes=list(scratch),
        compiler_params=pltpu.CompilerParams(vmem_limit_bytes=limit * 1024 * 1024),
        cost_estimate=pl.CostEstimate(flops=flops, bytes_accessed=moved, transcendentals=0),
    )(*inputs)


def blocks(width):
    return [slice(LANES * k, LANES * (k + 1)) for k in range(width // LANES)]


def wide_rows(count):
    return -(-count // LANES)


def row_block(row, rows):
    width = row.shape[1]
    padded = wide_rows(width) * LANES
    if padded != width:
        row = jnp.concatenate([row, jnp.zeros((1, padded - width), f32)], 1)
    place = lax.broadcasted_iota(jnp.int32, (rows, LANES), 0)
    out = jnp.zeros((rows, LANES), f32)
    for k, cut in enumerate(blocks(padded)):
        out = jnp.where(place == k, jnp.broadcast_to(row[:, cut], (rows, LANES)), out)
    return out


def block_row(block, count):
    return jnp.concatenate([block[k : k + 1] for k in range(count)], 1)


def split3(value):
    high = value.astype(bf16).astype(f32)
    rest = value - high
    mid = rest.astype(bf16).astype(f32)
    return (high, mid, rest - mid)


def lanes_of(shape):
    return lax.broadcasted_iota(jnp.int32, shape, 1)


def turned(rows, ray_count):
    fill = LANES - rows.shape[0]
    return jnp.concatenate([rows, jnp.zeros((fill, ray_count), f32)], 0).T


def own_group(k, slots, rows):
    place = lax.rem(lax.axis_index("region"), slots) ^ k
    return pl.ds(pl.multiple_of(place * rows, rows), rows)


def fetch_body(*refs, slots):
    ins, (pack_ref, *refs) = (refs[:10], refs[10:])
    outs, held, sems = (refs[:6], refs[6:10], refs[10])
    target_ref = outs[5]
    copies = []

    def fetch(source, place):
        copies.append(pltpu.make_async_copy(source, place, sems.at[len(copies)]))
        copies[-1].start()

    for ref, hold in zip(ins[:4], held):
        fetch(ref.at[0], hold)
    for ref, out in zip(ins[4:9], outs):
        fetch(ref, out)
    fetch(ins[9].at[own_group(0, slots, target_ref.shape[0])], target_ref)
    spot = 0
    for copy, hold in zip(copies[:3], held[:3]):
        copy.wait()
        rows, width = hold.shape[1:]
        for cut in blocks(width):
            pack_ref[spot : spot + rows, :] = hold[0, :, cut].astype(bf16)
            spot += rows
    copies[3].wait()
    pack_ref[spot : spot + 16, :] = row_block(held[3][...], 16).astype(bf16)
    for copy in copies[4:]:
        copy.wait()


def encode_body(*refs, unit_length, slots):
    codes, bins, entry, exit_, direction, enc_ref, geometry_ref, *refs = refs
    flat_geometry, flat_position = refs
    bins = bins[0].astype(f32)
    samples, ray_count = bins.shape
    group_rows = ray_count // slots
    slot = lax.broadcasted_iota(jnp.int32, bins.shape, 0)
    following = jnp.where(slot == samples - 1, float(BINS), pltpu.roll(bins, samples - 1, 0))
    inside = ((slot >= entry[...]) & (slot < exit_[...])).astype(f32)
    flat_geometry[:samples] = (following - bins) * unit_length * inside
    flat_geometry[samples : samples + 1] = direction[...].astype(f32)
    flat_position[...] = turned((bins + 0.5) / BINS, ray_count)
    for k in range(slots):
        group = own_group(k, slots, group_rows)
        geometry_ref[k] = flat_geometry[:, group]
        code_zero = codes[0, group].astype(f32)
        code_one = codes[1, group].astype(f32)
        position = flat_position[group, :]
        for j in range(samples):
            encoded = code_zero + position[:, j : j + 1] * code_one
            enc_ref[k, group_rows * j : group_rows * (j + 1), :] = encoded.astype(bf16)


def assemble(packs, shapes, vec_share):
    shards = len(packs)
    spot = 0
    mats = []
    for rows, width in shapes:
        pieces = []
        for cut in blocks(width):
            pieces.append(jnp.concatenate([p[spot : spot + rows, :] for p in packs], 0))
            spot += rows
        mats.append(jnp.concatenate(pieces, 1))
    vec_total = vec_share * shards
    vec = jnp.zeros((1, vec_total), f32)
    for s, p in enumerate(packs):
        block = p[spot : spot + 16, :].astype(f32)
        count = wide_rows(vec_share)
        row = block_row(block, count)
        fill = vec_total - count * LANES
        if fill:
            row = jnp.concatenate([row, jnp.zeros((1, fill), f32)], 1)
        if s:
            row = pltpu.roll(row, vec_share * s, 1)
        vec = vec + row
    return (*mats, vec)


def product(left, right):
    return jnp.dot(left, right, preferred_element_type=f32)


def forward_slots(slots, weights, enc_ref, geometry_ref, message_refs, kept):
    in_weight, mid_ref, head_ref, vec = weights
    one_ref, two_ref, turn_ref, scalar_ref = kept
    samples, ray_count = scalar_ref.shape[2:]
    hidden = mid_ref.shape[0]
    feat = turn_ref.shape[2]
    bias_one = vec[:, :hidden]
    bias_two = vec[:, hidden : 2 * hidden]
    half_bias = 0.5 * vec[:, 3 * hidden :]
    lane = lanes_of((ray_count, LANES))
    ones, twos, densities = ([], [], [])
    for i, k in enumerate(slots):
        one = product(enc_ref[k], in_weight) + bias_one
        ones.append(jnp.maximum(one, 0.0).astype(bf16))
        one_ref[i] = ones[i]
    for i in range(len(slots)):
        two = product(ones[i], mid_ref[...]) + bias_two
        twos.append(jnp.maximum(two, 0.0).astype(bf16))
        two_ref[i] = twos[i]
    raws = [product(two, head_ref[:, feat:]) for two in twos]
    for raw in raws:
        density = jnp.zeros((ray_count, LANES), f32)
        for j in range(samples):
            rows = slice(ray_count * j, ray_count * (j + 1))
            density = jnp.where(lane == j, raw[rows], density)
        densities.append(density)
    for i in range(len(slots)):
        turn_ref[i] = jnp.tanh(product(twos[i], head_ref[:, :feat]) + half_bias)
    density = side_by_side([value.T[:samples] for value in densities])
    geometry = side_by_side([geometry_ref[k, :samples] for k in slots])
    direction = side_by_side([geometry_ref[k, samples : samples + 1] for k in slots])
    soft = jnp.maximum(density, 0.0) + jnp.log1p(jnp.exp(-jnp.abs(density)))
    optical = soft * geometry
    before = [jnp.zeros_like(direction)]
    for j in range(samples):
        before.append(before[-1] + optical[j : j + 1])
    depth = before.pop()
    optical_before = jnp.concatenate(before, 0)
    opacity = jnp.tanh(0.5 * optical) * (1.0 + jnp.exp(-optical))
    local_weight = jnp.exp(-optical_before) * opacity
    half_weight = 0.5 * local_weight
    half_sum = jnp.sum(half_weight, 0, keepdims=True)
    columns = turned(jnp.concatenate([half_weight, half_sum], 0), depth.shape[1])
    shared = jnp.concatenate([*split3(depth), direction], 0)
    sig = 0.5 * jnp.tanh(0.5 * density) + 0.5
    scalars = (local_weight, jnp.exp(-(optical_before + optical)), geometry * sig)
    for i, k in enumerate(slots):
        cut = slice(ray_count * i, ray_count * (i + 1))
        for q, value in enumerate(scalars):
            scalar_ref[i, q] = value[:, cut]
        own = columns[cut]
        total = jnp.zeros((ray_count, feat), f32) + own[:, samples : samples + 1]
        for j in range(samples):
            rows = slice(ray_count * j, ray_count * (j + 1))
            total = total + own[:, j : j + 1] * turn_ref[i, rows, :]
        message_refs[i][...] = as_message([total[:, k] for k in blocks(feat)], shared[:, cut])


def side_by_side(values):
    return jnp.concatenate(values, 1) if len(values) > 1 else values[0]


def as_message(parts, rows):
    count, rays = rows.shape
    if count < 8:
        rows = jnp.concatenate([rows, jnp.zeros((8 - count, rays), f32)], 0)
    if rays < LANES:
        rows = jnp.concatenate([rows, jnp.zeros((8, LANES - rays), f32)], 1)
    return jnp.concatenate([*parts, rows], 0).astype(bf16)


def from_message(value, rays):
    value = value.astype(f32)
    count = value.shape[0] // rays
    parts = [value[rays * k : rays * (k + 1)] for k in range(count)]
    return (parts, value[rays * count :, :rays])


def forward_first_body(*refs, shapes, vec_share, pair, slots):
    both = None
    if pair:
        own_ref, other_ref, *refs, both = refs
        mine = lax.axis_index("rays")
        both[mine] = own_ref[...]
        both[1 - mine] = other_ref[...]
        packs = [both.at[0], both.at[1]]
    else:
        packs_ref, *refs = refs
        packs = [packs_ref.at[s] for s in range(packs_ref.shape[0])]
    enc_ref, geometry_ref, in_ref, mid_ref, head_ref, vec_ref, *refs = refs
    hidden = mid_ref.shape[0]
    in_weight, mid_weight, feat_weight, vec = assemble(packs, shapes, vec_share)
    density_row = vec[:, 2 * hidden : 3 * hidden]
    density_cols = jnp.broadcast_to(density_row, (LANES, hidden)).T
    in_ref[...] = in_weight
    mid_ref[...] = mid_weight
    half_weight = (0.5 * feat_weight.astype(f32)).astype(bf16)
    head_ref[...] = jnp.concatenate([half_weight, density_cols.astype(bf16)], 1)
    vec_ref[...] = vec
    weights = (in_weight, mid_ref, head_ref, vec)
    forward_slots(slots, weights, enc_ref, geometry_ref, refs[4:], refs[:4])


def forward_rest_body(in_ref, mid_ref, head_ref, vec_ref, *refs, slots):
    enc_ref, geometry_ref, *refs = refs
    weights = (in_ref[...], mid_ref, head_ref, vec_ref[...])
    forward_slots(slots, weights, enc_ref, geometry_ref, refs[4:], refs[:4])


def sides(values):
    below, above = ([jnp.zeros_like(values[0])], [jnp.zeros_like(values[0])])
    for q in range(len(values) - 1):
        below.append(below[-1] + values[q])
        above.append(above[-1] + values[len(values) - 1 - q])
    return (below, above[::-1])


def gather_messages(refs, store, own, rays):
    for k, ref in enumerate(refs):
        store[own ^ k] = ref[...]
    members = [from_message(store[p], rays) for p in range(len(refs))]
    parts = [m[0] for m in members]
    depth = [m[1][0:1] + m[1][1:2] + m[1][2:3] for m in members]
    direction = members[0][1][3:4]
    below, above = sides(depth)
    trans = [jnp.exp(-jnp.where(direction < 0.5, b, a)) for b, a in zip(below, above)]
    return (parts, depth, direction, trans)


def member_at(level, quad):
    region = lax.axis_index("region")
    if level == 0:
        return lax.rem(region, quad)
    return lax.rem(lax.div(region, quad << (level - 1)), 2)


def as_columns(rows):
    columns = turned(jnp.concatenate(rows, 0), rows[0].shape[1])
    return [columns[:, i : i + 1] for i in range(len(rows))]


def weighted_sum(factors, parts):
    out = []
    for k in range(len(parts[0])):
        total = factors[0] * parts[0][k]
        for factor, part in zip(factors[1:], parts[1:]):
            total = total + factor * part[k]
        out.append(total)
    return out


def inner(left, right):
    total = left[0] * right[0]
    for a, b in zip(left[1:], right[1:]):
        total = total + a * b
    return jnp.sum(total, 1, keepdims=True)


def combine_body(*refs, rays, level, quad):
    *messages, out_ref, store = refs
    messages = messages[: quad if level == 0 else 2]
    own = member_at(level, quad)
    parts, depth, direction, trans = gather_messages(messages, store, own, rays)
    total = depth[0]
    for value in depth[1:]:
        total = total + value
    rows = jnp.concatenate([*split3(total), direction], 0)
    out_ref[...] = as_message(weighted_sum(as_columns(trans), parts), rows)


def owner_body(*refs, counts, quad):
    levels = []
    for count in counts:
        messages, refs = (refs[:count], refs[count:])
        levels.append(messages)
    target_ref, _, *refs = refs
    out_refs, stores, reply = (refs[:quad], refs[quad:-1], refs[-1])
    rays, feat = target_ref.shape
    own = [member_at(n, quad) for n in range(len(counts))]
    found = [
        gather_messages(messages, stores[n], own[n], rays) for n, messages in enumerate(levels)
    ]
    direction = found[0][2]
    parts, _, _, trans = found[-1]
    rendered = weighted_sum(as_columns(trans), parts)
    grads = [
        (value - target_ref[:, cut].astype(f32)).astype(bf16).astype(f32)
        for value, cut in zip(rendered, blocks(feat))
    ]
    lane = lanes_of((rays, LANES))
    inners = jnp.zeros((rays, LANES), f32)
    for i, value in enumerate(sum((f[0] for f in found), [])):
        inners = jnp.where(lane == i, inner(grads, value), inners)
    inners = inners.T

    def picked(values, place):
        out = values[0]
        for n, value in enumerate(values[1:]):
            out = jnp.where(place == n + 1, value, out)
        return out

    ahead = jnp.ones((1, rays), f32)
    reach = jnp.zeros((1, rays), f32)
    for n in range(len(counts) - 1, -1, -1):
        first = sum(counts[:n])
        trans = [ahead * t for t in found[n][3]]
        below, above = sides([t * inners[first + p : first + p + 1] for p, t in enumerate(trans)])
        after = [reach + jnp.where(direction < 0.5, a, b) for b, a in zip(below, above)]
        if n:
            ahead, reach = (picked(trans, own[n]), picked(after, own[n]))
    for p in range(quad):
        reply[p, :6, :rays] = jnp.concatenate([*split3(trans[p]), *split3(after[p])], 0)
    for k, out_ref in enumerate(out_refs):
        out_ref[...] = as_message(grads, reply[own[0] ^ k, :6, :rays])


def with_ones(value):
    return jnp.concatenate([value.T, jnp.ones((16, value.shape[0]), bf16)], 0)


def ready_shared_body(*refs):
    states, (enc_ref, mid_ref, head_ref, *refs) = (refs[:4], refs[4:])
    source, fetched, refs = (refs[:4], refs[4:8], refs[8:])
    enc_turned, mid_turned, head_turned, *results, sems = refs
    copies = []
    for n, (ref, place) in enumerate(zip(states, fetched)):
        copies.append(pltpu.make_async_copy(ref, place, sems.at[n]))
        copies[-1].start()
    feat = source[2].shape[2]
    mid_turned[...] = mid_ref[...].T
    head = head_ref[...].astype(f32)
    lane = lanes_of(head.shape)
    head_turned[...] = jnp.where(lane < feat, 2.0 * head, head).astype(bf16).T
    for k in range(enc_ref.shape[0]):
        enc_turned[k] = with_ones(enc_ref[k])
    ready_slots(source, results)
    for copy in copies:
        copy.wait()


def ready_body(*refs):
    count = len(refs) // 7
    for n in range(count):
        ready_slots(refs[4 * n : 4 * n + 4], refs[4 * count + 3 * n : 4 * count + 3 * n + 3])


def ready_slots(source, results):
    one_ref, two_ref, turn_ref, scalar_ref = source
    one_turned, two_turned, slope_ref = results
    samples, ray_count = scalar_ref.shape[2:]
    for i in range(one_ref.shape[0]):
        one_turned[i] = with_ones(one_ref[i])
        two_turned[i] = with_ones(two_ref[i])
        columns = turned(0.25 * scalar_ref[i, 0], ray_count)
        for j in range(samples):
            rows = slice(ray_count * j, ray_count * (j + 1))
            turn = turn_ref[i, rows, :]
            slope_ref[i, rows, :] = columns[:, j : j + 1] * (1.0 - turn * turn)


def backward_body(*refs, slots, places, sources, before, last, group_count, shapes, vec_share, shards):
    begun = not before
    messages, refs = (refs[: len(slots)], refs[len(slots) :])
    held = [[ref.at[at] for ref in refs[7 * n : 7 * n + 7]] for n, at in places]
    refs = refs[7 * sources :]
    enc_turned, mid_turned, head_turned, *refs = refs
    if not begun:
        earlier, refs = (refs[:3], refs[3:])
    if last:
        depths, (depth_ref, *outs) = (refs[: len(before)], refs[len(before) :])
    else:
        *outs, depth_ref = refs
    samples, ray_count = held[0][3].shape[1:]
    hidden = held[0][0].shape[1]
    feat = held[0][2].shape[1]
    lane = lanes_of((ray_count, LANES))
    if last:
        for ref, group in zip(depths, before):
            for i, k in enumerate(group):
                depth_ref[:, own_group(k, group_count, ray_count)] = ref[i : i + 1]
    sums = [0.0, 0.0, 0.0] if begun else [ref[...] for ref in earlier]
    grads, extras, spreads = ([], [], [])
    for i, k in enumerate(slots):
        parts, extra = from_message(messages[i][...], ray_count)
        grad = jnp.concatenate(parts, 1)
        grads.append(grad)
        extras.append(extra)
        grad_sum = jnp.sum(grad, 1, keepdims=True)
        spread = jnp.where(lane == samples, grad_sum, 0.0)
        for j in range(samples):
            rows = slice(ray_count * j, ray_count * (j + 1))
            value = jnp.sum(held[i][2][rows, :] * grad, 1, keepdims=True)
            spread = jnp.where(lane == j, value, spread)
        spreads.append(spread.T)
    extra = side_by_side(extras)
    trans = extra[0:1] + extra[1:2] + extra[2:3]
    after = extra[3:4] + extra[4:5] + extra[5:6]
    for i, k in enumerate(slots):
        cut = slice(ray_count * i, ray_count * (i + 1))
        if last:
            depth_ref[:, own_group(k, group_count, ray_count)] = -after[:, cut]
        else:
            depth_ref[i : i + 1] = -after[:, cut]
    spread = side_by_side(spreads)
    sample_grad = 0.5 * (spread[:samples] + spread[samples : samples + 1])
    local_weight, trans_after, slope = [
        side_by_side([refs_of[3][q] for refs_of in held]) for q in range(3)
    ]
    weighted = local_weight * sample_grad
    later = [jnp.zeros_like(after)]
    for j in range(samples - 1, 0, -1):
        later.append(later[-1] + weighted[j : j + 1])
    later = jnp.concatenate(later[::-1], 0)
    optical_grad = trans * (trans_after * sample_grad - later) - after
    columns = turned(jnp.concatenate([optical_grad * slope, trans], 0), after.shape[1])
    zero = jnp.zeros((), bf16)
    for i, k in enumerate(slots):
        one_ref, two_ref, _, _, one_turned, two_turned, slope_ref = held[i]
        own = columns[ray_count * i : ray_count * (i + 1)]
        grad_ahead = grads[i] * own[:, samples : samples + 1]
        pieces = []
        for j in range(samples):
            rows = slice(ray_count * j, ray_count * (j + 1))
            colour_grad = (grad_ahead * slope_ref[rows, :]).astype(bf16)
            density_part = jnp.where(lane == j, own, 0.0).astype(bf16)
            pieces.append(jnp.concatenate([colour_grad, density_part], 1))
        head_grad = jnp.concatenate(pieces, 0)
        second = product(head_grad, head_turned[...]).astype(bf16)
        sums[2] = sums[2] + product(two_turned[...], head_grad)
        second = jnp.where(two_ref[...] > 0, second, zero)
        first = product(second, mid_turned[...]).astype(bf16)
        sums[1] = sums[1] + product(one_turned[...], second)
        first = jnp.where(one_ref[...] > 0, first, zero)
        sums[0] = sums[0] + product(enc_turned[k], first)
    if not last:
        for value, ref in zip(sums, outs):
            ref[...] = value
        return
    values = [value[:-16] for value in sums]
    first_sum, second_sum, head_sum = [value[-16:-15] for value in sums]
    density_sum = jnp.sum(values[2][:, feat:].T, 0, keepdims=True)
    vec = jnp.concatenate([first_sum, second_sum, density_sum, head_sum[:, :feat]], 1)
    total = vec.shape[1]

    def write(s, ref):
        spot = 0
        for (rows, width), value in zip(shapes, values):
            for cut in blocks(width):
                ref[spot : spot + rows, :] = value[rows * s : rows * (s + 1), cut]
                spot += rows
        row = pltpu.roll(vec, total - vec_share * s, 1) if s else vec
        ref[spot : spot + 16, :] = row_block(row[:, : wide_rows(vec_share) * LANES], 16)

    if shards != 2:
        for s in range(shards):
            write(s, outs[0].at[s])
        return
    mine = lax.axis_index("rays")
    for s in range(2):

        @pl.when(mine == s)
        def _():
            write(s, outs[0])
            write(1 - s, outs[1])


def adam_body(*refs, shards):
    grad_refs, (depth_ref, *refs) = (refs[:shards], refs[shards:])
    state_refs, out_refs, depth_out = (refs[:4], refs[4:8], refs[8])
    depth_out[...] = depth_ref[...]

    def update(stacked, gradient):
        first_moment = beta_one * stacked[1] + (1.0 - beta_one) * gradient
        second = beta_two * stacked[2] + (1.0 - beta_two) * gradient * gradient
        step = first_moment / (jnp.sqrt(second * (1.0 / second_fix)) + epsilon)
        return (stacked[0] - (learn_rate / first_fix) * step, first_moment, second)

    def gathered(spot, rows):
        total = grad_refs[0][spot : spot + rows, :]
        for ref in grad_refs[1:]:
            total = total + ref[spot : spot + rows, :]
        return total

    spot = 0
    for ref, out in zip(state_refs[:3], out_refs[:3]):
        rows, width = ref.shape[2:]
        for cut in blocks(width):
            new = update([ref[i, 0, :, cut] for i in range(3)], gathered(spot, rows))
            spot += rows
            for i in range(3):
                out[i, 0, :, cut] = new[i]
    ref, out = (state_refs[3], out_refs[3])
    share = ref.shape[2]
    gradient = block_row(gathered(spot, 16), wide_rows(share))[:, :share]
    new = update([ref[i] for i in range(3)], gradient)
    for i in range(3):
        out[i] = new[i]


def shaped(shape, dtype):
    return jax.ShapeDtypeStruct(shape, dtype)


def swap(value, distance, size):
    return lax.ppermute(value, "region", [(i, i ^ distance) for i in range(size)])


def per_device(
    ray_codes,
    target,
    direction,
    entries,
    exits,
    depth_bins,
    in_layer,
    mid_layer,
    feat_layer,
    vectors,
):
    regions = lax.axis_size("region")
    shards = lax.axis_size("rays")
    samples, ray_count = depth_bins.shape[1:]
    quad = min(QUAD, regions)
    planes = regions // quad
    rays = ray_count // quad
    layers = (in_layer, mid_layer, feat_layer)
    states = (*layers, vectors)
    shapes = tuple(layer.shape[2:] for layer in layers)
    vec_share = vectors.shape[2]
    hidden = shapes[0][1]
    feat = shapes[2][1]
    code_width = ray_codes.shape[2]
    pack_rows = sum(rows * (width // LANES) for rows, width in shapes) + 16
    rows = samples * rays
    sizes = dict(shapes=shapes, vec_share=vec_share)
    pair = shards == 2
    flops = 2 * rows * (code_width * hidden + hidden * hidden + hidden * (feat + LANES))

    arguments = (*states, ray_codes, depth_bins, entries, exits, direction[None], target)
    pack, *geometric, own_target = call(
        functools.partial(fetch_body, slots=quad),
        (pltpu.VMEM((pack_rows, LANES), bf16),)
        + tuple(pltpu.VMEM(a.shape, a.dtype) for a in arguments[4:9])
        + (pltpu.VMEM((rays, feat), bf16),),
        [in_hbm(a) for a in arguments],
        16,
        scratch=[pltpu.VMEM(a.shape[1:], f32) for a in states]
        + [pltpu.SemaphoreType.DMA((10,))],
        specs=[pl.BlockSpec(memory_space=pltpu.HBM)] * 10,
    )
    if pair:
        packs = (pack, lax.ppermute(pack, "rays", [(0, 1), (1, 0)]))
    else:
        packs = (lax.all_gather(pack, "rays", axis=0),)
    encoded, geometry = call(
        functools.partial(encode_body, unit_length=depth_scale / (regions * BINS), slots=quad),
        (
            pltpu.VMEM((quad, rows, code_width), bf16),
            pltpu.VMEM((quad, samples + 8, rays), f32),
        ),
        [in_vmem(v) for v in geometric],
        16,
        scratch=[
            pltpu.VMEM((samples + 8, ray_count), f32),
            pltpu.VMEM((ray_count, LANES), f32),
        ],
        flops=10 * quad * rows * code_width,
        moved=quad * rows * code_width * 4,
    )

    message = pltpu.VMEM((rays * (feat // LANES) + 8, LANES), bf16)

    def kept_shapes(count):
        return (
            pltpu.VMEM((count, rows, hidden), bf16),
            pltpu.VMEM((count, rows, hidden), bf16),
            pltpu.VMEM((count, rows, feat), f32),
            pltpu.VMEM((count, 3, samples, rays), f32),
        )

    def moved(count):
        return count * rows * (feat + hidden) * 4

    weight_shapes = (
        pltpu.VMEM((shapes[0][0] * shards, hidden), bf16),
        pltpu.VMEM((hidden, hidden), bf16),
        pltpu.VMEM((hidden, feat + LANES), bf16),
        pltpu.VMEM((1, vec_share * shards), f32),
    )

    def forward(slots, inputs, first):
        if first:
            body = functools.partial(forward_first_body, pair=pair, slots=slots, **sizes)
        else:
            body = functools.partial(forward_rest_body, slots=slots)
        out = call(
            body,
            (weight_shapes if first else ())
            + kept_shapes(len(slots))
            + (message,) * len(slots),
            [in_vmem(v) for v in (*inputs, encoded, geometry)],
            16,
            scratch=[pltpu.VMEM((2, pack_rows, LANES), bf16)] if first and pair else (),
            flops=0 if slots == (0,) else 100 * flops,
            moved=0 if slots == (0,) else 100 * moved(1),
        )
        found, out = (out[:4], out[4:]) if first else (None, out)
        return (out[:4], list(out[4:]), found)

    groups = [(quad - 1,), tuple(range(1, quad - 1)), (0,)]
    kept, sent, weights = ([], {}, None)
    for slots in groups:
        inputs = weights if kept else packs
        arrays, messages, found = forward(slots, inputs, not kept)
        weights = weights or found
        kept.append(arrays)
        for k, value in zip(slots, messages):
            sent[k] = swap(value, k, regions) if k else value
    quad_messages = [in_vmem(sent[k]) for k in range(quad)]
    def ready_shapes(count):
        return (
            pltpu.VMEM((count, hidden + 16, rows), bf16),
            pltpu.VMEM((count, hidden + 16, rows), bf16),
            pltpu.VMEM((count, rows, feat), f32),
        )

    hbm, vmem = (pl.BlockSpec(memory_space=m) for m in (pltpu.HBM, pltpu.VMEM))
    local = [encoded, weights[1], weights[2], *kept[0]]
    results = call(
        ready_shared_body,
        tuple(pltpu.VMEM(s.shape, f32) for s in states)
        + (
            pltpu.VMEM((quad, code_width + 16, rows), bf16),
            pltpu.VMEM((hidden, hidden), bf16),
            pltpu.VMEM((feat + LANES, hidden), bf16),
        )
        + ready_shapes(len(groups[0])),
        [in_hbm(s) for s in states] + [in_vmem(v) for v in local],
        16,
        scratch=[pltpu.SemaphoreType.DMA((4,))],
        specs=[hbm] * 4 + [vmem] * len(local),
        flops=flops,
        moved=2 * moved(1),
    )
    states_near, enc_turned, turned_weights = (results[:4], results[4], results[5:7])
    ready = [results[7:]]
    results = call(
        ready_body,
        sum((ready_shapes(len(slots)) for slots in groups[1:]), ()),
        [in_vmem(v) for v in sum(map(list, kept[1:]), [])],
        16,
        flops=(quad - 1) * flops,
        moved=2 * moved(quad - 1),
    )
    ready += [results[3 * n : 3 * n + 3] for n in range(len(groups) - 1)]
    ahead = {1: [in_vmem(turned_weights[0])]}
    levels = [quad_messages]
    for level in range(planes.bit_length() - 1):
        composite = call(
            functools.partial(combine_body, rays=rays, level=level, quad=quad),
            message,
            levels[-1] + ahead.get(level, []),
            16,
            scratch=[pltpu.VMEM((len(levels[-1]), *message.shape), bf16)],
        )
        levels.append([in_vmem(composite), in_vmem(swap(composite, quad << level, regions))])
    counts = tuple(len(level) for level in levels)
    replies = call(
        functools.partial(owner_body, counts=counts, quad=quad),
        (message,) * quad,
        sum(levels, []) + [in_vmem(v) for v in (own_target, results[0])],
        16,
        scratch=[pltpu.VMEM((count, *message.shape), bf16) for count in counts]
        + [pltpu.VMEM((quad, 8, LANES), f32)],
    )
    answers = [replies[0]] + [swap(replies[k], k, regions) for k in range(1, quad)]
    gradient_shapes = (
        pltpu.VMEM((code_width + 16, hidden), f32),
        pltpu.VMEM((hidden + 16, hidden), f32),
        pltpu.VMEM((hidden + 16, feat + LANES), f32),
    )
    earlier, depths, before = ((), [], ())
    place = {k: (n, slots.index(k)) for n, slots in enumerate(groups) for k in slots}
    steps = [(0,), (2, 1), (3,)]
    for slots in steps:
        last = slots == steps[-1]
        if last:
            share = pltpu.VMEM((pack_rows, LANES), f32)
            out_shape = (pltpu.VMEM((1, ray_count), f32), share, share)
            if not pair:
                out_shape = (out_shape[0], shaped((shards, pack_rows, LANES), f32))
        else:
            out_shape = gradient_shapes + (pltpu.VMEM((len(slots), rays), f32),)
        used = sorted({place[k][0] for k in slots})
        inputs = [answers[k] for k in slots]
        inputs += sum(([*kept[n], *ready[n]] for n in used), [])
        inputs += [enc_turned, *turned_weights, *earlier] + (depths if last else [])
        out = call(
            functools.partial(
                backward_body,
                slots=slots,
                places=tuple((used.index(place[k][0]), place[k][1]) for k in slots),
                sources=len(used),
                before=before,
                last=last,
                group_count=quad,
                shards=shards,
                **sizes,
            ),
            out_shape,
            [in_vmem(v) for v in inputs],
            24,
            flops=0 if slots == (0,) else 100 * flops,
            moved=0 if slots == (0,) else 100 * moved(1),
        )
        earlier, before = (out[:3], before + (slots,))
        if not last:
            depths.append(out[3])
    depth_grad, *grads = out
    if pair:
        parts = (grads[0], lax.ppermute(grads[1], "rays", [(0, 1), (1, 0)]))
    else:
        exchanged = lax.all_to_all(grads[0], "rays", 0, 0)
        parts = tuple(exchanged[s] for s in range(shards))
    return call(
        functools.partial(adam_body, shards=shards),
        tuple(shaped(s.shape, f32) for s in states) + (shaped(depth_grad.shape, f32),),
        [in_vmem(v) for v in (*parts, depth_grad, *states_near)],
        16,
    )


def solution(mesh):
    placed = (
        P(None, "rays", None),
        P("rays", None),
        P("rays"),
        P("region", "rays"),
        P("region", "rays"),
        P("region", None, "rays"),
        P(None, "region", "rays", None),
        P(None, "region", "rays", None),
        P(None, "region", "rays", None),
        P(None, "region", "rays"),
    )
    return jax.shard_map(
        per_device,
        mesh=mesh,
        in_specs=placed,
        out_specs=(
            P(None, "region", "rays", None),
            P(None, "region", "rays", None),
            P(None, "region", "rays", None),
            P(None, "region", "rays"),
            P("region", "rays"),
        ),
        check_vma=False,
    )
```
